32 devices in a mesh: rows: 4 (over y, x), seq: 8 (over z, core).
Axes of the slice: x: 2, y: 2, z: 4, core: 2. Of those that a mesh axis runs over, the one named last changes fastest.
Arguments:
- tokens: bfloat16 [4, 1024, 768], P('rows', 'seq'), may hold values from -6 to 6
- doc_starts: int32 [4, 5], P('rows'), may hold values from 0 to 1023, as said below
- norm1_gain: bfloat16 [768], replicated, may hold values from 0.25 to 1.75
- norm1_bias: bfloat16 [768], replicated, may hold values from -1.75 to 1.75
- in_weight: bfloat16 [768, 2304], replicated, may hold values from -0.21875 to 0.21875
- in_bias: bfloat16 [2304], replicated, may hold values from -1.75 to 1.75
- short_weight: bfloat16 [3, 2304], replicated, may hold values from -3.5 to 3.5
- short_bias: bfloat16 [2304], replicated, may hold values from -1.75 to 1.75
- filter_first: bfloat16 [33, 64], replicated, may hold values from -1 to 1
- filter_first_bias: bfloat16 [64], replicated, may hold values from -6 to 6
- filter_second: bfloat16 [64, 64], replicated, may hold values from -0.75 to 0.75
- filter_second_bias: bfloat16 [64], replicated, may hold values from -6 to 6
- filter_third: bfloat16 [64, 64], replicated, may hold values from -0.75 to 0.75
- filter_third_bias: bfloat16 [64], replicated, may hold values from -6 to 6
- filter_last: bfloat16 [64, 768], replicated, may hold values from -0.046875 to 0.046875
- sine_freq: bfloat16 [64], replicated, may hold values from 4 to 16
- filter_bias: bfloat16 [768], replicated, may hold values from -6 to 6
- out_weight: bfloat16 [768, 768], replicated, may hold values from -0.21875 to 0.21875
- out_bias: bfloat16 [768], replicated, may hold values from -1.75 to 1.75
- norm2_gain: bfloat16 [768], replicated, may hold values from 0.25 to 1.75
- norm2_bias: bfloat16 [768], replicated, may hold values from -1.75 to 1.75
- up_weight: bfloat16 [768, 3072], replicated, may hold values from -0.21875 to 0.21875
- up_bias: bfloat16 [3072], replicated, may hold values from -1.75 to 1.75
- down_weight: bfloat16 [3072, 768], replicated, may hold values from -0.109375 to 0.109375
- down_bias: bfloat16 [768], replicated, may hold values from -1.75 to 1.75
- cotangent: bfloat16 [4, 1024, 768], P('rows', 'seq'), may hold values from -6 to 6
Outputs:
- output: bfloat16 [4, 1024, 768], P('rows', 'seq')
- grad_tokens: float32 [4, 1024, 768], P('rows', 'seq')
- grad_norm1_gain: float32 [768], replicated
- grad_norm1_bias: float32 [768], replicated
- grad_in_weight: float32 [768, 2304], P('seq')
- grad_in_bias: float32 [2304], replicated
- grad_short_weight: float32 [3, 2304], replicated
- grad_short_bias: float32 [2304], replicated
- grad_filter_first: float32 [33, 64], replicated
- grad_filter_first_bias: float32 [64], replicated
- grad_filter_second: float32 [64, 64], replicated
- grad_filter_second_bias: float32 [64], replicated
- grad_filter_third: float32 [64, 64], replicated
- grad_filter_third_bias: float32 [64], replicated
- grad_filter_last: float32 [64, 768], replicated
- grad_sine_freq: float32 [64], replicated
- grad_filter_bias: float32 [768], replicated
- grad_out_weight: float32 [768, 768], P('seq')
- grad_out_bias: float32 [768], replicated
- grad_norm2_gain: float32 [768], replicated
- grad_norm2_bias: float32 [768], replicated
- grad_up_weight: float32 [768, 3072], P('seq')
- grad_up_bias: float32 [3072], replicated
- grad_down_weight: float32 [3072, 768], P('seq')
- grad_down_bias: float32 [768], replicated
The draws below stay inside these ranges and needn't reach their ends.
Inputs may be any that keep to these rules, and one draw needn't show every extreme that they name: `doc_starts`: each row's starts rise strictly, the first is 0 and the last is 1023; a document runs from its start to the next start or the end of the row.
All inputs are finite; a program needn't handle non-finite values.
Results may differ from the reference program's by a relative error of at most 0.0098.
The reference program's roundings to bfloat16 on the way count: a program that leaves them out, or rounds other values in their place, can miss the bound.
Values may be sent and summed in bfloat16 or wider, within the bound.
No kernel may reach another device: no remote copies, remote signals or barrier semaphores. Data moves between devices by JAX's collectives and lax.ppermute only.
A program may use at most 320 MiB of HBM per device.

```python
import math
import jax
import jax.numpy as jnp
from jax import lax

D = 768
FF = 3072
FWIDTH = 64
FEAT = 33
SHORT = 3
NDOCS = 5
TOKENS_DEV = 128
SEQLEN = 1024
ROWS = 4


def draw_doc_starts(key, part):
    keys = jax.random.split(jax.random.fold_in(key, 11), 3)
    length = SEQLEN
    first = jax.random.randint(keys[0], (ROWS,), 1, TOKENS_DEV - 1)
    second = jax.random.randint(keys[1], (ROWS,), first + 1, TOKENS_DEV)
    third = jax.random.randint(keys[2], (ROWS,), length - TOKENS_DEV + 1, length - 1)
    fourth = jnp.zeros((ROWS,), jnp.int32) + (length - 1)
    zero = jnp.zeros((ROWS,), jnp.int32)
    return jnp.stack([zero, first, second, third, fourth], axis=1).astype(jnp.int32)


def steps_of(own_key, shape, cuts, low, largest):
    def one(position, blocks):
        heights = jax.random.uniform(jax.random.fold_in(jax.random.fold_in(own_key, 6), position), (blocks,), jnp.float32, low / len(cuts), largest / len(cuts))
        return jnp.repeat(jnp.exp(heights), shape[position] // blocks).reshape((-1,) + (1,) * (len(shape) - position - 1))

    level = one(*cuts[0])
    for cut in cuts[1:]:
        level = level * one(*cut)
    return level


def scatter_about(key, dims, width, most, pieces=(), held_as=jnp.bfloat16):
    level = steps_of(key, dims, pieces, -0.22, 0.18) if pieces else 1.0
    drawn = jax.random.normal(key, dims, jnp.float32) * width * level
    return jnp.minimum(jnp.maximum(drawn, -most), most).astype(held_as)


def setup_inputs(seed: int = 0) -> dict:
    streams_of = jax.random.split(jax.random.key(seed), 27)
    tokens = scatter_about(streams_of[0], (ROWS, SEQLEN, D), 1.0, 6.0, ((0, 4), (1, 8)))
    doc_starts = draw_doc_starts(jax.random.fold_in(streams_of[26], 71), 0)
    norm1_gain = jnp.clip(1.0 + 0.15 * jax.random.normal(streams_of[2], (D,), jnp.float32), 0.25, 1.75).astype(jnp.bfloat16)
    norm1_bias = scatter_about(streams_of[3], (D,), 0.3, 1.75)
    in_weight = scatter_about(streams_of[4], (D, 3 * D), D ** -0.5, 0.21875)
    in_bias = scatter_about(streams_of[5], (3 * D,), 0.3, 1.75)
    short_weight = scatter_about(streams_of[6], (SHORT, 3 * D), SHORT ** -0.5, 3.5)
    short_bias = scatter_about(streams_of[7], (3 * D,), 0.3, 1.75)
    filter_first = scatter_about(streams_of[8], (FEAT, FWIDTH), FEAT ** -0.5, 1.0)
    filter_first_bias = scatter_about(streams_of[9], (FWIDTH,), 1.0, 6.0)
    filter_second = scatter_about(streams_of[10], (FWIDTH, FWIDTH), FWIDTH ** -0.5, 0.75)
    filter_second_bias = scatter_about(streams_of[11], (FWIDTH,), 1.0, 6.0)
    filter_third = scatter_about(streams_of[12], (FWIDTH, FWIDTH), FWIDTH ** -0.5, 0.75)
    filter_third_bias = scatter_about(streams_of[13], (FWIDTH,), 1.0, 6.0)
    filter_last = scatter_about(streams_of[14], (FWIDTH, D), (FWIDTH * SEQLEN // 4) ** -0.5, 0.046875)
    sine_freq = jnp.clip(jnp.exp(jax.random.uniform(streams_of[15], (FWIDTH,), jnp.float32, math.log(4.0), math.log(16.0))), 4.0, 16.0).astype(jnp.bfloat16)
    filter_bias = scatter_about(streams_of[16], (D,), 1.0, 6.0)
    out_weight = scatter_about(streams_of[17], (D, D), D ** -0.5, 0.21875)
    out_bias = scatter_about(streams_of[18], (D,), 0.3, 1.75)
    norm2_gain = jnp.clip(1.0 + 0.15 * jax.random.normal(streams_of[19], (D,), jnp.float32), 0.25, 1.75).astype(jnp.bfloat16)
    norm2_bias = scatter_about(streams_of[20], (D,), 0.3, 1.75)
    up_weight = scatter_about(streams_of[21], (D, FF), D ** -0.5, 0.21875)
    up_bias = scatter_about(streams_of[22], (FF,), 0.3, 1.75)
    down_weight = scatter_about(streams_of[23], (FF, D), FF ** -0.5, 0.109375)
    down_bias = scatter_about(streams_of[24], (D,), 0.3, 1.75)
    cotangent = scatter_about(streams_of[25], (ROWS, SEQLEN, D), 1.0, 6.0, ((0, 4), (1, 8)))
    return {"tokens": tokens, "doc_starts": doc_starts, "norm1_gain": norm1_gain, "norm1_bias": norm1_bias, "in_weight": in_weight, "in_bias": in_bias, "short_weight": short_weight, "short_bias": short_bias, "filter_first": filter_first, "filter_first_bias": filter_first_bias, "filter_second": filter_second, "filter_second_bias": filter_second_bias, "filter_third": filter_third, "filter_third_bias": filter_third_bias, "filter_last": filter_last, "sine_freq": sine_freq, "filter_bias": filter_bias, "out_weight": out_weight, "out_bias": out_bias, "norm2_gain": norm2_gain, "norm2_bias": norm2_bias, "up_weight": up_weight, "up_bias": up_bias, "down_weight": down_weight, "down_bias": down_bias, "cotangent": cotangent}


EPSILON = 1e-05
HIGHEST = lax.Precision.HIGHEST
MIN_DECAY = math.log(100.0) / 1.5
MAX_DECAY = math.log(100.0) / 0.3

@jax.custom_vjp
def low(v):
    return lax.optimization_barrier(v.astype(jnp.bfloat16)).astype(jnp.float32)

@jax.custom_vjp
def low_back(v):
    return v

def low_keep(v):
    return (low(v), None)

def low_pass(kept, grad):
    return (grad,)

def back_keep(v):
    return (v, None)

def back_low(kept, grad):
    return (low(grad),)
low.defvjp(low_keep, low_pass)
low_back.defvjp(back_keep, back_low)

def layer_norm(values, gain, shift):
    average = lax.optimization_barrier(jnp.mean(values, axis=-1, keepdims=True))
    centred = values - average
    spread = lax.optimization_barrier(jnp.mean(centred * centred, axis=-1, keepdims=True))
    return centred * lax.rsqrt(spread + EPSILON) * gain + shift

def filter_taps(first, first_bias, second, second_bias, third, third_bias, last, sine_freq, length):
    lags = jnp.arange(length)
    bands = (first.shape[0] - 1) // 2
    moment = lags.astype(jnp.float32) / (length - 1)
    band_freq = jnp.linspace(0.0001, bands - 1, bands, dtype=jnp.float32)
    phase = 2.0 * math.pi / length * lags.astype(jnp.float32)
    angles = phase[:, None] * band_freq[None, :]
    features = jnp.concatenate([moment[:, None], jnp.cos(angles), -jnp.sin(angles)], axis=1)
    hidden = jnp.sin(sine_freq * (jnp.dot(features, first, precision=HIGHEST) + first_bias))
    hidden = jnp.sin(sine_freq * (jnp.dot(hidden, second, precision=HIGHEST) + second_bias))
    hidden = jnp.sin(sine_freq * (jnp.dot(hidden, third, precision=HIGHEST) + third_bias))
    rates = jnp.linspace(MIN_DECAY, MAX_DECAY, last.shape[1], dtype=jnp.float32)
    window = jnp.exp(-moment[:, None] * rates[None, :])
    return jnp.dot(hidden, last, precision=HIGHEST) * window

def doc_ids_of(starts, positions):
    return lax.optimization_barrier(jnp.sum((positions[:, None] >= starts[None, :]).astype(jnp.int32), axis=1)) - 1

def short_conv_rows(proj, ids, weight, bias):
    length = proj.shape[1]
    total = bias + jnp.zeros_like(proj)
    for offset in range(weight.shape[0]):
        moved = jnp.pad(proj, ((0, 0), (offset, 0), (0, 0)))[:, :length]
        moved_ids = jnp.pad(ids, ((0, 0), (offset, 0)), constant_values=-1)[:, :length]
        same = (moved_ids == ids).astype(proj.dtype)[:, :, None]
        total = total + weight[offset] * moved * same
    return total

def causal_conv(taps, signal):
    length = signal.shape[0]
    spectrum = jnp.fft.rfft(taps, n=2 * length, axis=0) * jnp.fft.rfft(signal, n=2 * length, axis=0)
    return jnp.fft.irfft(spectrum, n=2 * length, axis=0)[:length]

def long_conv_row(taps, signal, ids):
    total = jnp.zeros_like(signal)
    for document in range(NDOCS):
        member = (ids == document).astype(signal.dtype)[:, None]
        total = total + member * causal_conv(taps, signal * member)
    return total

def matmul(left, right):
    return jnp.dot(left, right, precision=HIGHEST)

def reference(tokens, doc_starts, norm1_gain, norm1_bias, in_weight, in_bias, short_weight, short_bias, filter_first, filter_first_bias, filter_second, filter_second_bias, filter_third, filter_third_bias, filter_last, sine_freq, filter_bias, out_weight, out_bias, norm2_gain, norm2_bias, up_weight, up_bias, down_weight, down_bias, cotangent):
    positions = jnp.arange(SEQLEN).astype(jnp.int32)
    ids = jax.vmap(doc_ids_of, in_axes=(0, None))(doc_starts, positions)
    params = tuple((item.astype(jnp.float32) for item in (norm1_gain, norm1_bias, in_weight, in_bias, short_weight, short_bias, filter_first, filter_first_bias, filter_second, filter_second_bias, filter_third, filter_third_bias, filter_last, sine_freq, filter_bias, out_weight, out_bias, norm2_gain, norm2_bias, up_weight, up_bias, down_weight, down_bias)))

    def forward(inputs, gain1, shift1, w_in, b_in, s_weight, s_bias, f_first, f_first_bias, f_second, f_second_bias, f_third, f_third_bias, f_last, s_freq, f_bias, w_out, b_out, gain2, shift2, w_up, b_up, w_down, b_down):
        normed1 = low(layer_norm(inputs, gain1, shift1))
        proj = low_back(matmul(normed1, w_in) + b_in)
        mixed = short_conv_rows(proj, ids, s_weight, s_bias)
        gate_out = mixed[:, :, :D]
        gate_in = mixed[:, :, D:2 * D]
        values = mixed[:, :, 2 * D:]
        carried = low(values * gate_in)
        taps = filter_taps(f_first, f_first_bias, f_second, f_second_bias, f_third, f_third_bias, f_last, s_freq, SEQLEN)
        long_out = jax.vmap(long_conv_row, in_axes=(None, 0, 0))(taps, carried, ids) + f_bias * carried
        gated = low(long_out * gate_out)
        mixer = low_back(matmul(gated, w_out) + b_out)
        resid = inputs + mixer
        normed2 = low(layer_norm(resid, gain2, shift2))
        pre = low_back(matmul(normed2, w_up) + b_up)
        active = low(jax.nn.gelu(pre, approximate=True))
        return resid + matmul(active, w_down) + b_down
    result, pull = jax.vjp(forward, tokens.astype(jnp.float32), *params)
    grads = pull(cotangent.astype(jnp.float32))
    return (result.astype(jnp.bfloat16), grads[0], grads[1], grads[2], grads[3], grads[4], grads[5], grads[6], grads[7], grads[8], grads[9], grads[10], grads[11], grads[12], grads[13], grads[14], grads[15], grads[16], grads[17], grads[18], grads[19], grads[20], grads[21], grads[22], grads[23])
```

```python
from functools import partial
import math

import jax
import jax.numpy as jnp
import numpy as np
from jax import lax
from jax.experimental import pallas as pl
from jax.experimental.pallas import tpu as pltpu
from jax.sharding import PartitionSpec as P

EPSILON = 1e-05
HIGHEST = lax.Precision.HIGHEST
MIN_DECAY = math.log(100.0) / 1.5
MAX_DECAY = math.log(100.0) / 0.3
F32 = jnp.float32
BF16 = jnp.bfloat16
RIM = 16
VMEM_LIMIT = 58 * 1024 * 1024
GELU_C = math.sqrt(2.0 / math.pi)
GELU_A = 0.044715


def params():
    return pltpu.CompilerParams(vmem_limit_bytes=VMEM_LIMIT)


def smem():
    return pl.BlockSpec(memory_space=pltpu.SMEM)


def whole(shape):
    return pl.BlockSpec(shape, lambda *_: (0,) * len(shape))


def dot(left, right):
    return jnp.dot(left, right, preferred_element_type=F32)


def dot_t(left, right):
    return lax.dot_general(left, right, (((1,), (1,)), ((), ())), preferred_element_type=F32)


def high_low(values):
    high = values.astype(BF16)
    return high, (values - high.astype(F32)).astype(BF16)


def doc_at(meta, ndocs, position):
    total = jnp.int32(-1)
    for d in range(ndocs):
        total = total + (position >= meta[4 + d]).astype(jnp.int32)
    return total


def doc_start(meta, ndocs, position):
    found = jnp.int32(0)
    for d in range(ndocs):
        found = jnp.where(position >= meta[4 + d], meta[4 + d], found)
    return found


def doc_end(meta, ndocs, position, length):
    found = jnp.int32(length)
    for d in reversed(range(ndocs)):
        found = jnp.where(position < meta[4 + d], meta[4 + d], found)
    return found


def doc_column(meta, ndocs, first, rows):
    position = first + lax.broadcasted_iota(jnp.int32, (rows, 1), 0)
    total = jnp.full((rows, 1), -1, jnp.int32)
    for d in range(ndocs):
        total = total + (position >= meta[4 + d]).astype(jnp.int32)
    return position, total


def block_tables(block):
    period = 2 * block
    packed = np.arange(period)
    freq = np.where(packed <= block, packed, packed - block)
    places = np.arange(period)
    angle = 2.0 * np.pi / period * (freq[:, None] * places[None, :] % period)
    real = (packed <= block)[:, None]
    forward = np.where(real, np.cos(angle), -np.sin(angle))
    scaling = np.where((packed == 0) | (packed == block), 1.0, 2.0) / period
    inverse = (forward * scaling[:, None]).T[block:]
    left = forward[:, :block]

    def split(table):
        table = table.astype(np.float32)
        high = table.astype(BF16)
        return high, (table - high.astype(np.float32)).astype(BF16)

    lh, ll = split(left)
    ih, il = split(inverse)
    return dict(
        left2=np.concatenate([lh, ll], 1),
        left3=np.concatenate([lh, lh, ll], 1),
        inv3=np.concatenate([ih, ih, il], 1),
        invt2=np.concatenate([ih.T, il.T], 1),
        leftt3=np.concatenate([lh.T, lh.T, ll.T], 1),
    )


def spectrum2(table, signal):
    return dot(table, jnp.concatenate([signal, signal], axis=0))


def spectrum3(table, values):
    high, low = high_low(values)
    return dot(table, jnp.concatenate([high, low, high], axis=0))


def masked(signal, mask):
    return jnp.where(mask, signal.astype(F32), 0.0).astype(BF16)


def first_row(shape):
    return lax.broadcasted_iota(jnp.int32, shape, 0) == 0


def times(left, right):
    half = left.shape[0] // 2
    lre, lim = left[:half], left[half:]
    rre, rim = right[:half], right[half:]
    row = first_row(lre.shape)
    edge = jnp.where(row, 0.0, lim)
    return lre * rre - edge * rim, edge * rre + jnp.where(row, lim, lre) * rim


def times_back(left, grad):
    half = left.shape[0] // 2
    lre, lim = left[:half], left[half:]
    gre, gim = grad[:half], grad[half:]
    row = first_row(lre.shape)
    edge = jnp.where(row, 0.0, lim)
    return lre * gre + edge * gim, jnp.where(row, lim, lre) * gim - edge * gre


def add_spec(acc, pair):
    half = acc.shape[0] // 2
    acc[:half, :] += pair[0]
    acc[half:, :] += pair[1]


def set_spec(acc, pair):
    half = acc.shape[0] // 2
    acc[:half, :] = pair[0]
    acc[half:, :] = pair[1]


def normalise(values):
    average = jnp.mean(values, axis=-1, keepdims=True)
    centred = values - average
    spread = jnp.mean(centred * centred, axis=-1, keepdims=True)
    rstd = lax.rsqrt(spread + EPSILON)
    return centred * rstd, rstd


def front_kernel(ndocs, meta, tokens, rim, gain, bias, weight, wbias, taps, tbias,
                 proj_ref, normt_ref, mixed_ref, carried_ref):
    block, width = tokens.shape
    taps_n = taps.shape[0]
    ext = jnp.concatenate([rim[...], tokens[...]], axis=0).astype(F32)
    hat, _ = normalise(ext)
    normed = hat * gain[...].astype(F32) + bias[...].astype(F32)
    normt_ref[...] = normed[RIM:].T.astype(BF16)
    low = normed.astype(BF16)
    base = meta[0] * block
    position, ids = doc_column(meta, ndocs, base, block)
    masks = []
    for k in range(taps_n):
        _, back = doc_column(meta, ndocs, base - k, block)
        masks.append(((back == ids) & (position >= k)).astype(F32))
    for third in range(3):
        cols = slice(third * width, (third + 1) * width)
        proj_ref[:, cols] = dot(low, weight[:, cols]) + wbias[:, cols].astype(F32)
        total = tbias[:, cols].astype(F32)
        for k in range(taps_n):
            moved = proj_ref[pl.ds(RIM - k, block), cols]
            total = total + taps[k : k + 1, cols].astype(F32) * moved * masks[k]
        mixed_ref[:, cols] = total
    carried_ref[...] = (mixed_ref[:, 2 * width :] * mixed_ref[:, width : 2 * width]).astype(BF16)


def lag_kernel(taps, left3, out):
    blocks = taps.shape[0]
    sign = 1.0 - 2.0 * (lax.broadcasted_iota(jnp.int32, (out.shape[1], 1), 0) % 2).astype(F32)

    def step(j, carry):
        spec = spectrum3(left3[...], taps[j])
        out[j] = out[j] + sign * spec

        @pl.when(j + 1 < blocks)
        def _():
            out[j + 1] = spec

        return carry

    out[0] = jnp.zeros(out.shape[1:], F32)
    lax.fori_loop(0, blocks, step, 0)


def conv_kernel(ndocs, length, meta, signal, lags, left2, inv3, out, acc):
    block = signal.shape[1]
    me = meta[0]
    base = me * block
    start = doc_start(meta, ndocs, base)
    low_block = start // block
    _, ids = doc_column(meta, ndocs, base, block)
    first_doc = doc_at(meta, ndocs, base)
    last_doc = doc_at(meta, ndocs, base + block - 1)
    own = signal[me]
    spec = spectrum2(left2[...], masked(own, ids == first_doc))
    set_spec(acc, times(lags[0], spec))

    def cross(s, carry):
        position = s * block + lax.broadcasted_iota(jnp.int32, (block, 1), 0)
        spec = spectrum2(left2[...], masked(signal[s], position >= start))
        add_spec(acc, times(lags[me - s], spec))
        return carry

    lax.fori_loop(low_block, me, cross, 0)
    out[...] = jnp.where(ids == first_doc, spectrum3(inv3[...], acc[...]), 0.0)

    def inner(d, carry):
        spec = spectrum2(left2[...], masked(own, ids == d))
        set_spec(acc, times(lags[0], spec))
        out[...] += jnp.where(ids == d, spectrum3(inv3[...], acc[...]), 0.0)
        return carry

    lax.fori_loop(first_doc + 1, last_doc + 1, inner, 0)


def mlp_kernel(tokens, cot, conv, carried, gate_out, fbias, w_out, b_out, gain, shift,
               up, up_bias, down, down_bias,
               output, actt, gpre_ref, ubias_grad, n2t, gatedt, gmix, gresid, glong, glong16,
               ggate, smalls,
               resid, n2, hat2, rstd2, oacc, gacc):
    j = pl.program_id(0)

    @pl.when(j == 0)
    def _():
        long_out = conv[...] + fbias[...].astype(F32) * carried[...].astype(F32)
        gated = long_out * gate_out[...]
        gatedt[...] = gated.T.astype(BF16)
        r = tokens[...].astype(F32) + dot(gated.astype(BF16), w_out[...]) + b_out[...].astype(F32)
        resid[...] = r
        hat, rstd = normalise(r)
        hat2[...] = hat
        rstd2[...] = rstd
        normed = hat * gain[...].astype(F32) + shift[...].astype(F32)
        n2t[...] = normed.T.astype(BF16)
        n2[...] = normed.astype(BF16)
        oacc[...] = jnp.zeros_like(oacc)
        gacc[...] = jnp.zeros_like(gacc)

    pre = dot(n2[...], up[...]) + up_bias[...].astype(F32)
    sq = pre * pre
    th = jnp.tanh(GELU_C * (pre * (1.0 + GELU_A * sq)))
    act = 0.5 * pre * (1.0 + th)
    slope = 0.5 * (1.0 + th) + 0.5 * pre * (1.0 - th * th) * (
        GELU_C * (1.0 + 3.0 * GELU_A * sq)
    )
    actt[...] = act.T.astype(BF16)
    oacc[...] += dot(act.astype(BF16), down[...])
    gpre = (dot_t(cot[...], down[...]) * slope).astype(BF16)
    gpre_ref[...] = gpre
    ubias_grad[...] = jnp.sum(gpre.astype(F32), axis=0, keepdims=True)
    gacc[...] += dot_t(gpre, up[...])

    @pl.when(j == pl.num_programs(0) - 1)
    def _():
        output[...] = (resid[...] + oacc[...] + down_bias[...].astype(F32)).astype(BF16)
        top = cot[...].astype(F32)
        gn = gacc[...]
        hat = hat2[...]
        q = gn * gain[...].astype(F32)
        mean_q = jnp.mean(q, axis=-1, keepdims=True)
        mean_qh = jnp.mean(q * hat, axis=-1, keepdims=True)
        gr = top + (q - mean_q - hat * mean_qh) * rstd2[...]
        gresid[...] = gr
        gm = gr.astype(BF16)
        gmix[...] = gm
        gg = dot_t(gm, w_out[...])
        c = carried[...].astype(F32)
        long_out = conv[...] + fbias[...].astype(F32) * c
        gl = gg * gate_out[...]
        glong[...] = gl
        glong16[...] = gl.astype(BF16)
        ggate[...] = gg * long_out
        rows = [
            jnp.sum(top, axis=0, keepdims=True),
            jnp.sum(gn * hat, axis=0, keepdims=True),
            jnp.sum(gn, axis=0, keepdims=True),
            jnp.sum(gm.astype(F32), axis=0, keepdims=True),
            jnp.sum(gl * c, axis=0, keepdims=True),
        ]
        rows.append(jnp.zeros((8 - len(rows), gn.shape[1]), F32))
        smalls[...] = jnp.concatenate(rows, axis=0)


def conv_back_kernel(ndocs, length, meta, grads, own_grad, lags, invt2, leftt3, fbias,
                     gate_in, values, for_in, for_values, acc):
    block = grads.shape[1]
    me = meta[0]
    base = me * block
    _, ids = doc_column(meta, ndocs, base, block)
    first_doc = doc_at(meta, ndocs, base)
    last_doc = doc_at(meta, ndocs, base + block - 1)
    last_block = (doc_end(meta, ndocs, base + block - 1, length) - 1) // block
    own = grads[me]
    spec = spectrum2(invt2[...], masked(own, ids == last_doc))
    set_spec(acc, times_back(lags[0], spec))

    def cross(t, carry):
        _, far = doc_column(meta, ndocs, t * block, block)
        spec = spectrum2(invt2[...], masked(grads[t], far == last_doc))
        add_spec(acc, times_back(lags[t - me], spec))
        return carry

    lax.fori_loop(me + 1, last_block + 1, cross, 0)
    for_in[...] = jnp.where(ids == last_doc, spectrum3(leftt3[...], acc[...]), 0.0)

    def inner(d, carry):
        spec = spectrum2(invt2[...], masked(own, ids == d))
        set_spec(acc, times_back(lags[0], spec))
        for_in[...] += jnp.where(ids == d, spectrum3(leftt3[...], acc[...]), 0.0)
        return carry

    lax.fori_loop(first_doc, last_doc, inner, 0)
    total = for_in[...] + fbias[...].astype(F32) * own_grad[...]
    for_in[...] = total * values[...]
    for_values[...] = total * gate_in[...]


def taps_grad_kernel(ndocs, length, meta, signal, own_grad, left2, invt2, leftt3, out, win, gspec):
    blocks, block = signal.shape[0], signal.shape[1]
    me = meta[0]
    base = me * block
    start = doc_start(meta, ndocs, base)
    low_block = start // block
    _, ids = doc_column(meta, ndocs, base, block)
    first_doc = doc_at(meta, ndocs, base)
    last_doc = doc_at(meta, ndocs, base + block - 1)
    sign = 1.0 - 2.0 * (lax.broadcasted_iota(jnp.int32, (2 * block, 1), 0) % 2).astype(F32)
    own = signal[me]
    grad = own_grad[...]
    out[...] = jnp.zeros_like(out)
    win[me - low_block + 1] = jnp.zeros(win.shape[1:], F32)
    gspec[...] = spectrum2(invt2[...], masked(grad, ids == first_doc))
    spec = spectrum2(left2[...], masked(own, ids == first_doc))
    set_spec(win.at[0], times_back(spec, gspec[...]))

    def inner(d, carry):
        spec = spectrum2(left2[...], masked(own, ids == d))
        back = spectrum2(invt2[...], masked(grad, ids == d))
        add_spec(win.at[0], times_back(spec, back))
        return carry

    lax.fori_loop(first_doc + 1, last_doc + 1, inner, 0)

    def cross(s, carry):
        position = s * block + lax.broadcasted_iota(jnp.int32, (block, 1), 0)
        spec = spectrum2(left2[...], masked(signal[s], position >= start))
        set_spec(win.at[me - s], times_back(spec, gspec[...]))
        return carry

    lax.fori_loop(low_block, me, cross, 0)

    def emit(k, carry):
        out[k] = spectrum3(leftt3[...], win[k + 1] + sign * win[k])
        return carry

    lax.fori_loop(0, me - low_block + 1, emit, 0)


def short_back_kernel(ndocs, meta, ggate, for_in, for_values, rim, proj, taps,
                      gproj_ref, smalls):
    block, width = ggate.shape
    taps_n = taps.shape[0]
    base = meta[0] * block
    position, ids = doc_column(meta, ndocs, base, block)
    masks = []
    for k in range(taps_n):
        _, back = doc_column(meta, ndocs, base - k, block)
        masks.append(((back == ids) & (position >= k)).astype(F32))
    row = lax.broadcasted_iota(jnp.int32, (block, 1), 0)
    ahead = []
    for k in range(1, taps_n):
        _, later = doc_column(meta, ndocs, base + k, block)
        ahead.append(((later == ids) & (row < block - k)).astype(F32))
    bias_rows, weight_rows, short_rows = [], [], []
    for third, grad_ref in enumerate((ggate, for_in, for_values)):
        cols = slice(third * width, (third + 1) * width)
        grad = grad_ref[...]
        total = taps[0:1, cols].astype(F32) * grad
        weights = [jnp.sum(grad * proj[pl.ds(RIM, block), cols], axis=0, keepdims=True)]
        for k in range(1, taps_n):
            moved = pltpu.roll(grad, block - k, 0) * ahead[k - 1]
            total = total + taps[k : k + 1, cols].astype(F32) * moved
            weights.append(
                jnp.sum(grad * masks[k] * proj[pl.ds(RIM - k, block), cols], axis=0, keepdims=True)
            )
        tail = jnp.concatenate([jnp.zeros((block - 8, width), F32), rim[:, cols]], axis=0)
        low = (total + tail).astype(BF16)
        gproj_ref[:, cols] = low
        bias_rows.append(jnp.sum(low.astype(F32), axis=0, keepdims=True))
        short_rows.append(jnp.sum(grad, axis=0, keepdims=True))
        weight_rows.append(weights)
    rows = bias_rows + [weight_rows[t][k] for k in range(taps_n) for t in range(3)] + short_rows
    pad = smalls.shape[0] - len(rows)
    smalls[...] = jnp.concatenate(rows + [jnp.zeros((pad, width), F32)], axis=0)


def tail_kernel(gproj, weight, tokens, gain, gresid, out, smalls):
    gn = dot_t(gproj[...], weight[...])
    hat, rstd = normalise(tokens[...].astype(F32))
    q = gn * gain[...].astype(F32)
    mean_q = jnp.mean(q, axis=-1, keepdims=True)
    mean_qh = jnp.mean(q * hat, axis=-1, keepdims=True)
    out[...] = gresid[...] + (q - mean_q - hat * mean_qh) * rstd
    rows = [
        jnp.sum(gn * hat, axis=0, keepdims=True),
        jnp.sum(gn, axis=0, keepdims=True),
        jnp.zeros((6, gn.shape[1]), F32),
    ]
    smalls[...] = jnp.concatenate(rows, axis=0)


def filter_taps(first, first_bias, second, second_bias, third, third_bias, last, sine_freq, length):
    lags = jnp.arange(length)
    bands = (first.shape[0] - 1) // 2
    moment = lags.astype(F32) / (length - 1)
    band_freq = jnp.linspace(0.0001, bands - 1, bands, dtype=F32)
    phase = 2.0 * math.pi / length * lags.astype(F32)
    angles = phase[:, None] * band_freq[None, :]
    features = jnp.concatenate([moment[:, None], jnp.cos(angles), -jnp.sin(angles)], axis=1)
    hidden = jnp.sin(sine_freq * (jnp.dot(features, first, precision=HIGHEST) + first_bias))
    hidden = jnp.sin(sine_freq * (jnp.dot(hidden, second, precision=HIGHEST) + second_bias))
    hidden = jnp.sin(sine_freq * (jnp.dot(hidden, third, precision=HIGHEST) + third_bias))
    rates = jnp.linspace(MIN_DECAY, MAX_DECAY, last.shape[1], dtype=F32)
    window = jnp.exp(-moment[:, None] * rates[None, :])
    return jnp.dot(hidden, last, precision=HIGHEST) * window


def shift(block, axis, distance):
    devices = range(lax.axis_size(axis))
    return lax.ppermute(block, axis, [(i - distance, i) for i in devices if i - distance in devices])


def swap(block, axis, mask):
    return lax.ppermute(block, axis, [(i, i ^ mask) for i in range(lax.axis_size(axis))])


def butterfly(values):
    for axis in ("seq", "rows"):
        mask = 1
        while mask < lax.axis_size(axis):
            values = values + swap(values, axis, mask)
            mask *= 2
    return values


def strips(ref, chips, rows, core, first, take):
    return [
        ref[pl.ds(pl.multiple_of((2 * z + core) * rows + first, 16), take), :] for z in range(chips)
    ]


def early_grad_kernel(chips, meta, actt, act_sib, cot, cot_sib, n2t, n2_sib, gpre, gpre_sib,
                      gatedt, gated_sib, n1t, n1_sib, gmix, gmix_sib, gproj, gproj_sib, out):
    core, chip, row = meta[1], meta[2], meta[3]
    part = pl.program_id(0) ^ row
    rows = n2t.shape[0] // (2 * chips)
    width = cot.shape[1]

    def emit(left, left_sib, right, right_sib, first):
        lhs = jnp.concatenate([left, left_sib], axis=1)
        rhs = jnp.concatenate([right, right_sib], axis=0)
        made = dot(lhs, rhs).astype(BF16)
        for z in range(chips):
            out[0, z ^ chip, :, first : first + made.shape[1]] = made[z * rows : (z + 1) * rows]

    big = actt.shape[0] // (2 * chips)
    offset = pl.multiple_of(part * rows, 16)
    emit(
        jnp.concatenate(strips(actt, chips, big, core, offset, rows), axis=0),
        jnp.concatenate([act_sib[z, pl.ds(offset, rows), :] for z in range(chips)], axis=0),
        cot[...], cot_sib[...], 0,
    )
    cols = pl.ds(pl.multiple_of(part * width, 128), width)
    emit(
        jnp.concatenate(strips(n2t, chips, rows, core, 0, rows), axis=0),
        n2_sib[...].reshape(chips * rows, -1),
        gpre[:, cols], gpre_sib[:, cols], width,
    )
    half = pl.ds(pl.multiple_of((part % 2) * (width // 2), 128), width // 2)

    @pl.when(part < 2)
    def _():
        emit(
            jnp.concatenate(strips(gatedt, chips, rows, core, 0, rows), axis=0),
            gated_sib[...].reshape(chips * rows, -1),
            gmix[:, half], gmix_sib[:, half], 2 * width,
        )

    @pl.when(part >= 2)
    def _():
        emit(
            jnp.concatenate(strips(n1t, chips, rows, core, 0, rows), axis=0),
            n1_sib[...].reshape(chips * rows, -1),
            gproj[:, half], gproj_sib[:, half], 2 * width,
        )


def late_grad_kernel(chips, meta, n1t, n1_sib, gproj, gproj_sib, out):
    core, chip, row = meta[1], meta[2], meta[3]
    part = pl.program_id(0) ^ row
    rows = n1t.shape[0] // (2 * chips)
    take = out.shape[3]
    cols = pl.ds(pl.multiple_of(part * take, 128), take)
    left = jnp.concatenate(strips(n1t, chips, rows, core, 0, rows), axis=0)
    lhs = jnp.concatenate([left, n1_sib[...].reshape(chips * rows, -1)], axis=1)
    rhs = jnp.concatenate([gproj[:, cols], gproj_sib[:, cols]], axis=0)
    made = dot(lhs, rhs).astype(BF16)
    for z in range(chips):
        out[0, z ^ chip, :, :] = made[z * rows : (z + 1) * rows]


def sum_over_mesh(parts):
    chips = parts.shape[1]
    total = parts[0].astype(F32)
    for j in range(1, parts.shape[0]):
        total = total + swap(parts[j], "rows", j).astype(F32)
    low = total.astype(BF16)
    own = total[0]
    for j in range(1, chips):
        own = own + swap(low[j], "seq", 2 * j).astype(F32)
    own = own.astype(BF16)
    return [own] + [swap(own, "rows", j) for j in range(1, parts.shape[0])]


def place_early_kernel(meta, *refs):
    pieces, (down, up, out_w, in_w) = refs[:-4], refs[-4:]
    row = meta[3]
    rows = pieces[0].shape[0]
    width = out_w.shape[1]
    for j, piece in enumerate(pieces):
        part = row ^ j
        down[pl.ds(pl.multiple_of(part * rows, 8), rows), :] = piece[:, :width].astype(F32)
        up[:, pl.ds(pl.multiple_of(part * width, 128), width)] = piece[:, width : 2 * width].astype(F32)
        half = pl.ds(pl.multiple_of((part % 2) * (width // 2), 128), width // 2)

        @pl.when(part < 2)
        def _():
            out_w[:, half] = piece[:, 2 * width :].astype(F32)

        @pl.when(part >= 2)
        def _():
            in_w[:, half] = piece[:, 2 * width :].astype(F32)


def place_late_kernel(meta, early, *refs):
    pieces, in_w = refs[:-1], refs[-1]
    row = meta[3]
    width = early.shape[1]
    take = pieces[0].shape[1]
    in_w[:, :width] = early[...]
    for j, piece in enumerate(pieces):
        part = row ^ j
        in_w[:, pl.ds(pl.multiple_of(width + part * take, 128), take)] = piece[...].astype(F32)


def local(
    tokens, doc_starts, norm1_gain, norm1_bias, in_weight, in_bias, short_weight, short_bias,
    filter_first, filter_first_bias, filter_second, filter_second_bias, filter_third,
    filter_third_bias, filter_last, sine_freq, filter_bias, out_weight, out_bias, norm2_gain,
    norm2_bias, up_weight, up_bias, down_weight, down_bias, cotangent,
):
    block, width = tokens.shape[1:]
    blocks = lax.axis_size("seq")
    chips = blocks // 2
    nrows = lax.axis_size("rows")
    length = block * blocks
    hidden = up_weight.shape[1]
    index = lax.axis_index("seq")
    row = lax.axis_index("rows")
    starts = doc_starts[0]
    ndocs = starts.shape[0]
    taps_n = short_weight.shape[0]
    meta = jnp.concatenate(
        [jnp.stack([index, index % 2, index // 2, row]).astype(jnp.int32), starts]
    )
    tables = {k: jnp.asarray(v) for k, v in block_tables(block).items()}
    chunk = width if blocks <= 8 else 128
    steps = width // chunk
    tok, cot = tokens[0], cotangent[0]
    line = lambda v: v.reshape(1, -1)

    rim = shift(tok[block - RIM :], "seq", 1)
    proj, n1t, mixed, carried = pl.pallas_call(
        partial(front_kernel, ndocs),
        out_shape=(
            jax.ShapeDtypeStruct((block + RIM, 3 * width), F32),
            jax.ShapeDtypeStruct((width, block), BF16),
            jax.ShapeDtypeStruct((block, 3 * width), F32),
            jax.ShapeDtypeStruct((block, width), BF16),
        ),
        in_specs=[smem()] + [pl.BlockSpec(memory_space=pltpu.VMEM)] * 8,
        compiler_params=params(),
        name="front",
    )(meta, tok, rim, line(norm1_gain), line(norm1_bias), in_weight, line(in_bias), short_weight,
      line(short_bias))

    filter_params = tuple(
        v.astype(F32)
        for v in (filter_first, filter_first_bias, filter_second, filter_second_bias, filter_third,
                  filter_third_bias, filter_last, sine_freq)
    )
    taps, taps_pull = jax.vjp(partial(filter_taps, length=length), *filter_params)
    by_chunk = lambda lead: pl.BlockSpec(lead + (chunk,), lambda i: (0,) * len(lead) + (i,))
    lags = pl.pallas_call(
        lag_kernel,
        grid=(steps,),
        out_shape=jax.ShapeDtypeStruct((blocks, 2 * block, width), F32),
        in_specs=[by_chunk((blocks, block)), whole(tables["left3"].shape)],
        out_specs=by_chunk((blocks, 2 * block)),
        compiler_params=params(),
        name="lags",
    )(taps.reshape(blocks, block, width), tables["left3"])

    signal = lax.all_gather(carried, "seq", axis=0, tiled=False)
    conv = pl.pallas_call(
        partial(conv_kernel, ndocs, length),
        grid=(steps,),
        out_shape=jax.ShapeDtypeStruct((block, width), F32),
        in_specs=[smem(), by_chunk((blocks, block)), by_chunk((blocks, 2 * block)),
                  whole(tables["left2"].shape), whole(tables["inv3"].shape)],
        out_specs=by_chunk((block,)),
        scratch_shapes=[pltpu.VMEM((2 * block, chunk), F32)],
        compiler_params=params(),
        name="conv",
    )(meta, signal, lags, tables["left2"], tables["inv3"])

    ff = width
    fsteps = hidden // ff
    row_spec = whole((1, width))
    mat = whole((block, width))
    (output, actt, gpre, up_bias_grad, n2t, gatedt, gmix, gresid, glong, glong16, ggate,
     smalls_mlp) = pl.pallas_call(
        mlp_kernel,
        grid=(fsteps,),
        out_shape=(
            jax.ShapeDtypeStruct((block, width), BF16),
            jax.ShapeDtypeStruct((hidden, block), BF16),
            jax.ShapeDtypeStruct((block, hidden), BF16),
            jax.ShapeDtypeStruct((1, hidden), F32),
            jax.ShapeDtypeStruct((width, block), BF16),
            jax.ShapeDtypeStruct((width, block), BF16),
            jax.ShapeDtypeStruct((block, width), BF16),
            jax.ShapeDtypeStruct((block, width), F32),
            jax.ShapeDtypeStruct((block, width), F32),
            jax.ShapeDtypeStruct((block, width), BF16),
            jax.ShapeDtypeStruct((block, width), F32),
            jax.ShapeDtypeStruct((8, width), F32),
        ),
        in_specs=[
            mat, mat, mat, mat, mat, row_spec, whole((width, width)), row_spec, row_spec, row_spec,
            pl.BlockSpec((width, ff), lambda i: (0, i)), pl.BlockSpec((1, ff), lambda i: (0, i)),
            pl.BlockSpec((ff, width), lambda i: (i, 0)), row_spec,
        ],
        out_specs=(
            mat, pl.BlockSpec((ff, block), lambda i: (i, 0)), pl.BlockSpec((block, ff), lambda i: (0, i)),
            pl.BlockSpec((1, ff), lambda i: (0, i)), whole((width, block)), whole((width, block)),
            mat, mat, mat, mat, mat, whole((8, width)),
        ),
        scratch_shapes=[
            pltpu.VMEM((block, width), F32), pltpu.VMEM((block, width), BF16),
            pltpu.VMEM((block, width), F32), pltpu.VMEM((block, 1), F32),
            pltpu.VMEM((block, width), F32), pltpu.VMEM((block, width), F32),
        ],
        compiler_params=params(),
        name="mlp",
    )(tok, cot, conv, carried, mixed, line(filter_bias), out_weight, line(out_bias),
      line(norm2_gain), line(norm2_bias), up_weight, line(up_bias), down_weight, line(down_bias))

    grads = lax.all_gather(glong16, "seq", axis=0, tiled=False)
    third = lambda n: pl.BlockSpec((block, chunk), lambda i: (0, n * steps + i))
    for_in, for_values = pl.pallas_call(
        partial(conv_back_kernel, ndocs, length),
        grid=(steps,),
        out_shape=(jax.ShapeDtypeStruct((block, width), F32),) * 2,
        in_specs=[smem(), by_chunk((blocks, block)), by_chunk((block,)), by_chunk((blocks, 2 * block)),
                  whole(tables["invt2"].shape), whole(tables["leftt3"].shape), by_chunk((1,)),
                  third(1), third(2)],
        out_specs=(by_chunk((block,)),) * 2,
        scratch_shapes=[pltpu.VMEM((2 * block, chunk), F32)],
        compiler_params=params(),
        name="conv_back",
    )(meta, grads, glong, lags, tables["invt2"], tables["leftt3"], line(filter_bias), mixed, mixed)

    base = index * block
    head = jnp.concatenate([ggate[: taps_n - 1], for_in[: taps_n - 1], for_values[: taps_n - 1]], axis=1)
    places = base - (taps_n - 1) + jnp.arange(2 * (taps_n - 1))
    ids = jnp.sum((places[:, None] >= starts[None, :]).astype(jnp.int32), axis=1) - 1
    rim_out = []
    for p in range(taps_n - 1):
        total = jnp.zeros((3 * width,), F32)
        for k in range(1, taps_n):
            t = p - (taps_n - 1) + k
            if 0 <= t < taps_n - 1:
                same = ((ids[p] == ids[t + taps_n - 1]) & (base > 0)).astype(F32)
                total = total + short_weight[k].astype(F32) * head[t] * same
        rim_out.append(total)
    rim_out = jnp.concatenate([jnp.zeros((8 - (taps_n - 1), 3 * width), F32), jnp.stack(rim_out)], axis=0)
    rim_back = shift(rim_out, "seq", -1)

    vm = pl.BlockSpec(memory_space=pltpu.VMEM)
    gproj, smalls_short = pl.pallas_call(
        partial(short_back_kernel, ndocs),
        out_shape=(
            jax.ShapeDtypeStruct((block, 3 * width), BF16),
            jax.ShapeDtypeStruct((24, width), F32),
        ),
        in_specs=[smem()] + [vm] * 6,
        compiler_params=params(),
        name="short_back",
    )(meta, ggate, for_in, for_values, rim_back, proj, short_weight)

    grad_tokens, smalls_norm = pl.pallas_call(
        tail_kernel,
        out_shape=(
            jax.ShapeDtypeStruct((block, width), F32),
            jax.ShapeDtypeStruct((8, width), F32),
        ),
        in_specs=[vm] * 5,
        compiler_params=params(),
        name="tail",
    )(gproj, in_weight, tok, line(norm1_gain), gresid)

    taps_grad = pl.pallas_call(
        partial(taps_grad_kernel, ndocs, length),
        grid=(steps,),
        out_shape=jax.ShapeDtypeStruct((blocks, block, width), F32),
        in_specs=[smem(), by_chunk((blocks, block)), by_chunk((block,)), whole(tables["left2"].shape),
                  whole(tables["invt2"].shape), whole(tables["leftt3"].shape)],
        out_specs=by_chunk((blocks, block)),
        scratch_shapes=[pltpu.VMEM((blocks + 1, 2 * block, chunk), F32), pltpu.VMEM((2 * block, chunk), F32)],
        compiler_params=params(),
        name="taps_grad",
    )(meta, signal, glong, tables["left2"], tables["invt2"], tables["leftt3"])
    filter_grads = taps_pull(taps_grad.reshape(length, width))

    share = width // blocks
    if share % 16 == 0 and nrows == 4 and width % (2 * 128) == 0 and taps_n == 3:
        other = 1 - index % 2

        def for_sibling(features):
            parted = features.reshape(chips, 2, features.shape[0] // blocks, block)
            return lax.dynamic_index_in_dim(parted, other, 1, keepdims=False)

        cot_sib = swap(cot, "seq", 1)
        n1_sib = swap(for_sibling(n1t), "seq", 1)
        gproj_sib = swap(gproj, "seq", 1)
        early_cols = 2 * width + width // 2
        early = pl.pallas_call(
            partial(early_grad_kernel, chips),
            grid=(nrows,),
            out_shape=jax.ShapeDtypeStruct((nrows, chips, share, early_cols), BF16),
            in_specs=[smem()] + [
                whole(s) for s in (
                    (hidden, block), (chips, hidden // blocks, block), (block, width), (block, width),
                    (width, block), (chips, share, block), (block, hidden), (block, hidden),
                    (width, block), (chips, share, block), (width, block), (chips, share, block),
                    (block, width), (block, width), (block, width), (block, width),
                )
            ],
            out_specs=pl.BlockSpec((1, chips, share, early_cols), lambda i: (i, 0, 0, 0)),
            compiler_params=params(),
            name="early_grad",
        )(meta, actt, swap(for_sibling(actt), "seq", 1), cot, cot_sib, n2t,
          swap(for_sibling(n2t), "seq", 1), gpre, swap(gpre, "seq", 1), gatedt,
          swap(for_sibling(gatedt), "seq", 1), n1t, n1_sib, gmix, swap(gmix, "seq", 1),
          gproj, gproj_sib)
        pieces = sum_over_mesh(early)
        grad_down, grad_up, grad_out, grad_in_early = pl.pallas_call(
            place_early_kernel,
            out_shape=(
                jax.ShapeDtypeStruct((hidden // blocks, width), F32),
                jax.ShapeDtypeStruct((share, hidden), F32),
                jax.ShapeDtypeStruct((share, width), F32),
                jax.ShapeDtypeStruct((share, width), F32),
            ),
            in_specs=[smem()] + [vm] * 4,
            compiler_params=params(),
            name="place_early",
        )(meta, *pieces)
        late_cols = width // 2
        late = pl.pallas_call(
            partial(late_grad_kernel, chips),
            grid=(nrows,),
            out_shape=jax.ShapeDtypeStruct((nrows, chips, share, late_cols), BF16),
            in_specs=[smem(), whole((width, block)), whole((chips, share, block)),
                      whole((block, 2 * width)), whole((block, 2 * width))],
            out_specs=pl.BlockSpec((1, chips, share, late_cols), lambda i: (i, 0, 0, 0)),
            compiler_params=params(),
            name="late_grad",
        )(meta, n1t, n1_sib, gproj[:, width:], gproj_sib[:, width:])
        grad_in = pl.pallas_call(
            place_late_kernel,
            out_shape=jax.ShapeDtypeStruct((share, 3 * width), F32),
            in_specs=[smem()] + [vm] * 5,
            compiler_params=params(),
            name="place_late",
        )(meta, grad_in_early, *sum_over_mesh(late))
    else:
        def spread(left, right):
            part = lax.psum_scatter(dot(left, right), "seq", scatter_dimension=0, tiled=True)
            return lax.psum(part, "rows")

        grad_in = spread(n1t, gproj)
        grad_out = spread(gatedt, gmix)
        grad_up = spread(n2t, gpre)
        grad_down = spread(actt, cot)

    flat_filter = jnp.concatenate([filter_grads[i].reshape(-1) for i in (0, 1, 2, 3, 4, 5, 7)])
    used = flat_filter.shape[0]
    fill = -used % width
    smalls = jnp.concatenate(
        [
            up_bias_grad.reshape(-1, width),
            smalls_mlp,
            smalls_short,
            smalls_norm,
            filter_grads[6],
            jnp.pad(flat_filter, (0, fill)).reshape(-1, width),
        ],
        axis=0,
    )
    smalls = butterfly(smalls)
    at = hidden // width
    grad_up_bias = smalls[:at].reshape(-1)
    grad_down_bias, grad_gain2, grad_shift2, grad_out_bias, grad_filter_bias = (
        smalls[at + i] for i in range(5)
    )
    at += 8
    grad_in_bias = smalls[at : at + 3].reshape(-1)
    grad_short_weight = smalls[at + 3 : at + 3 + 3 * taps_n].reshape(taps_n, 3 * width)
    grad_short_bias = smalls[at + 3 + 3 * taps_n : at + 6 + 3 * taps_n].reshape(-1)
    at += 24
    grad_gain1, grad_shift1 = smalls[at], smalls[at + 1]
    at += 8
    grad_last = smalls[at : at + filter_last.shape[0]]
    at += filter_last.shape[0]
    flat = smalls[at:].reshape(-1)
    pieces, place = {}, 0
    for i in (0, 1, 2, 3, 4, 5, 7):
        size = math.prod(filter_grads[i].shape)
        pieces[i] = flat[place : place + size].reshape(filter_grads[i].shape)
        place += size
    return (
        output[None], grad_tokens[None], grad_gain1, grad_shift1, grad_in, grad_in_bias,
        grad_short_weight, grad_short_bias, pieces[0], pieces[1], pieces[2], pieces[3], pieces[4],
        pieces[5], grad_last, pieces[7], grad_filter_bias, grad_out, grad_out_bias, grad_gain2,
        grad_shift2, grad_up, grad_up_bias, grad_down, grad_down_bias,
    )


def solution(mesh):
    sharded = P("rows", "seq", None)
    placed = (sharded, P("rows", None)) + (P(),) * 23 + (sharded,)
    outs = [P()] * 25
    outs[0] = outs[1] = sharded
    for i in (4, 17, 21, 23):
        outs[i] = P("seq", None)
    return jax.shard_map(local, mesh=mesh, in_specs=placed, out_specs=tuple(outs), check_vma=False)
```

```python
from functools import partial
import math

import jax
import jax.numpy as jnp
import numpy as np
from jax import lax
from jax.experimental import pallas as pl
from jax.experimental.pallas import tpu as pltpu
from jax.sharding import PartitionSpec as P

EPSILON = 1e-05
HIGHEST = lax.Precision.HIGHEST
MIN_DECAY = math.log(100.0) / 1.5
MAX_DECAY = math.log(100.0) / 0.3
F32 = jnp.float32
BF16 = jnp.bfloat16
RIM = 16
VMEM_LIMIT = 26 * 1024 * 1024
GELU_C = math.sqrt(2.0 / math.pi)
GELU_A = 0.044715


def params():
    return pltpu.CompilerParams(vmem_limit_bytes=VMEM_LIMIT)


def cost(micros):
    return pl.CostEstimate(flops=0, bytes_accessed=int(micros * 3.0e6), transcendentals=0)


def single(kernel, name, micros, outs, scalars, arrays, after=(), scratch=()):
    count, skip = 1 + len(arrays), len(after)

    def body(*refs):
        kernel(*refs[:count], *refs[count + skip :])

    made = pl.pallas_call(
        body,
        grid=(1,),
        out_shape=tuple(outs),
        in_specs=[smem()] + [whole(v.shape) for v in arrays]
        + [pl.BlockSpec(memory_space=pl.ANY)] * skip,
        out_specs=tuple(whole(v.shape) for v in outs),
        scratch_shapes=list(scratch),
        compiler_params=params(),
        cost_estimate=cost(micros),
        name=name,
    )(scalars, *arrays, *after)
    return made


def smem():
    return pl.BlockSpec(memory_space=pltpu.SMEM)


def whole(shape):
    return pl.BlockSpec(shape, lambda *_: (0,) * len(shape))


def dot(left, right):
    return jnp.dot(left, right, preferred_element_type=F32)


def dot_t(left, right):
    return lax.dot_general(left, right, (((1,), (1,)), ((), ())), preferred_element_type=F32)


def high_low(values):
    high = values.astype(BF16)
    return high, (values - high.astype(F32)).astype(BF16)


def doc_at(meta, ndocs, position):
    total = jnp.int32(-1)
    for d in range(ndocs):
        total = total + (position >= meta[4 + d]).astype(jnp.int32)
    return total


def doc_start(meta, ndocs, position):
    found = jnp.int32(0)
    for d in range(ndocs):
        found = jnp.where(position >= meta[4 + d], meta[4 + d], found)
    return found


def doc_end(meta, ndocs, position, length):
    found = jnp.int32(length)
    for d in reversed(range(ndocs)):
        found = jnp.where(position < meta[4 + d], meta[4 + d], found)
    return found


def doc_column(meta, ndocs, first, rows):
    position = first + lax.broadcasted_iota(jnp.int32, (rows, 1), 0)
    total = jnp.full((rows, 1), -1, jnp.int32)
    for d in range(ndocs):
        total = total + (position >= meta[4 + d]).astype(jnp.int32)
    return position, total


def block_tables(block):
    period = 2 * block
    packed = np.arange(period)
    freq = np.where(packed <= block, packed, packed - block)
    places = np.arange(period)
    angle = 2.0 * np.pi / period * (freq[:, None] * places[None, :] % period)
    real = (packed <= block)[:, None]
    forward = np.where(real, np.cos(angle), -np.sin(angle))
    scaling = np.where((packed == 0) | (packed == block), 1.0, 2.0) / period
    inverse = (forward * scaling[:, None]).T[block:]
    left = forward[:, :block]

    def split(table):
        table = table.astype(np.float32)
        high = table.astype(BF16)
        return high, (table - high.astype(np.float32)).astype(BF16)

    lh, ll = split(left)
    ih, il = split(inverse)
    return dict(
        left2=np.concatenate([lh, ll], 1),
        left3=np.concatenate([lh, lh, ll], 1),
        inv3=np.concatenate([ih, ih, il], 1),
        invt2=np.concatenate([ih.T, il.T], 1),
        leftt3=np.concatenate([lh.T, lh.T, ll.T], 1),
    )


def spectrum2(table, signal):
    return dot(table, jnp.concatenate([signal, signal], axis=0))


def spectrum3(table, values):
    high, low = high_low(values)
    return dot(table, jnp.concatenate([high, low, high], axis=0))


def masked(signal, mask):
    return jnp.where(mask, signal.astype(F32), 0.0).astype(BF16)


def first_row(shape):
    return lax.broadcasted_iota(jnp.int32, shape, 0) == 0


def times(left, right):
    half = left.shape[0] // 2
    lre, lim = left[:half], left[half:]
    rre, rim = right[:half], right[half:]
    row = first_row(lre.shape)
    edge = jnp.where(row, 0.0, lim)
    return lre * rre - edge * rim, edge * rre + jnp.where(row, lim, lre) * rim


def times_back(left, grad):
    half = left.shape[0] // 2
    lre, lim = left[:half], left[half:]
    gre, gim = grad[:half], grad[half:]
    row = first_row(lre.shape)
    edge = jnp.where(row, 0.0, lim)
    return lre * gre + edge * gim, jnp.where(row, lim, lre) * gim - edge * gre


def add_spec(acc, pair):
    half = acc.shape[0] // 2
    acc[:half, :] += pair[0]
    acc[half:, :] += pair[1]


def set_spec(acc, pair):
    half = acc.shape[0] // 2
    acc[:half, :] = pair[0]
    acc[half:, :] = pair[1]


def normalise(values):
    average = jnp.mean(values, axis=-1, keepdims=True)
    centred = values - average
    spread = jnp.mean(centred * centred, axis=-1, keepdims=True)
    rstd = lax.rsqrt(spread + EPSILON)
    return centred * rstd, rstd


def row_of(ref):
    return ref[...].astype(F32).reshape(1, -1)


def part_of(ref, first, size):
    return ref[pl.ds(first, size)].astype(F32).reshape(1, -1)


def write_strips(out, first, source, count, rows, core):
    for p in range(2):
        for z in range(count):
            out[pl.ds(first + (p * count + z) * rows, rows), :] = source[
                pl.ds(pl.multiple_of((2 * z + (core ^ p)) * rows, 16), rows), :
            ]


def write_tiles(out, first, source, start, count):
    tokens = source.shape[0]
    for t in range(count):
        out[pl.ds(first + t * tokens, tokens), :] = source[
            :, pl.ds(pl.multiple_of(start + t * 128, 128), 128)
        ]


def front_kernel(ndocs, packed, meta, tokens, rim, cot, gain, bias, weight, wbias, taps, tbias,
                 proj_ref, normt_ref, mixed_ref, carried_ref, turned):
    block, width = tokens.shape
    taps_n = taps.shape[0]
    ext = jnp.concatenate([rim[...], tokens[...]], axis=0).astype(F32)
    hat, _ = normalise(ext)
    normed = hat * row_of(gain) + row_of(bias)
    turned[...] = normed[RIM:].T.astype(BF16)
    if packed:
        chips = packed
        write_strips(normt_ref, 0, turned, chips, width // (2 * chips), meta[1])
        write_tiles(normt_ref, width, cot, 0, width // 128)
    else:
        normt_ref[...] = turned[...]
    low = normed.astype(BF16)
    base = meta[0] * block
    position, ids = doc_column(meta, ndocs, base, block)
    masks = []
    for k in range(taps_n):
        _, back = doc_column(meta, ndocs, base - k, block)
        masks.append(((back == ids) & (position >= k)).astype(F32))
    for third in range(3):
        cols = slice(third * width, (third + 1) * width)
        proj_ref[:, cols] = dot(low, weight[:, cols]) + part_of(wbias, third * width, width)
        total = part_of(tbias, third * width, width)
        for k in range(taps_n):
            moved = proj_ref[pl.ds(RIM - k, block), cols]
            total = total + taps[k : k + 1, cols].astype(F32) * moved * masks[k]
        mixed_ref[:, cols] = total
    carried_ref[...] = (mixed_ref[:, 2 * width :] * mixed_ref[:, width : 2 * width]).astype(BF16)


def lag_kernel(taps, left3, out):
    blocks = taps.shape[0]
    sign = 1.0 - 2.0 * (lax.broadcasted_iota(jnp.int32, (out.shape[1], 1), 0) % 2).astype(F32)

    def step(j, carry):
        spec = spectrum3(left3[...], taps[j])
        out[j] = out[j] + sign * spec

        @pl.when(j + 1 < blocks)
        def _():
            out[j + 1] = spec

        return carry

    out[0] = jnp.zeros(out.shape[1:], F32)
    lax.fori_loop(0, blocks, step, 0)


def fill(meta, parts, held, ahead):
    own, sibling = parts
    chips = own.shape[0]
    for k in range(chips):
        z = meta[2] + k if ahead else meta[2] - k

        @pl.when((z >= 0) & (z < chips))
        def _():
            held[2 * z + meta[1]] = own[k]
            held[2 * z + 1 - meta[1]] = sibling[k]


def conv_kernel(ndocs, nparts, meta, *refs):
    parts, (lags, left2, inv3, out, acc), rest = refs[:nparts], refs[nparts : nparts + 5], refs[nparts + 5 :]
    signal = parts[0]
    if nparts > 1:
        (signal,) = rest
        fill(meta, parts, signal, False)
    block = signal.shape[1]
    me = meta[0]
    base = me * block
    start = doc_start(meta, ndocs, base)
    low_block = start // block
    _, ids = doc_column(meta, ndocs, base, block)
    first_doc = doc_at(meta, ndocs, base)
    last_doc = doc_at(meta, ndocs, base + block - 1)
    own = signal[me]
    spec = spectrum2(left2[...], masked(own, ids == first_doc))
    set_spec(acc, times(lags[0], spec))

    def cross(s, carry):
        position = s * block + lax.broadcasted_iota(jnp.int32, (block, 1), 0)
        spec = spectrum2(left2[...], masked(signal[s], position >= start))
        add_spec(acc, times(lags[me - s], spec))
        return carry

    lax.fori_loop(low_block, me, cross, 0)
    out[...] = jnp.where(ids == first_doc, spectrum3(inv3[...], acc[...]), 0.0)

    def inner(d, carry):
        spec = spectrum2(left2[...], masked(own, ids == d))
        set_spec(acc, times(lags[0], spec))
        out[...] += jnp.where(ids == d, spectrum3(inv3[...], acc[...]), 0.0)
        return carry

    lax.fori_loop(first_doc + 1, last_doc + 1, inner, 0)


def mlp_kernel(packed, meta, tokens, cot, conv, carried, gate_out, fbias, w_out, b_out, gain, shift,
               up, up_bias, down, down_bias, *refs):
    (output, gresid, glong, glong16, ggate, smalls), refs = refs[:6], refs[6:]
    (e1, e1_send, e2, e2_send) = refs[:4]
    if packed:
        refs = refs[4:]
    else:
        actt, gpre_out, n2t_out, gatedt_out, gmix_out = refs[:5]
        refs = refs[5:]
    resid, n2, hat2, rstd2, oacc, gacc, ubias, ubias_grad, turned, rows_held = refs
    j = pl.program_id(0)
    block, width = tokens.shape
    ff = up.shape[1]
    core, x, y = meta[1], meta[3] % 2, meta[3] // 2
    chips = packed
    if packed:
        share, big = width // (2 * chips), ff // 2
        half = big // 2
        slot = chips * (half + share)

    @pl.when(j == 0)
    def _():
        ubias[...] = row_of(up_bias)
        long_out = conv[...] + row_of(fbias) * carried[...].astype(F32)
        gated = long_out * gate_out[...]
        gated_t = gated.T.astype(BF16)
        r = tokens[...].astype(F32) + dot(gated.astype(BF16), w_out[...]) + row_of(b_out)
        resid[...] = r
        hat, rstd = normalise(r)
        hat2[...] = hat
        rstd2[...] = rstd
        normed = hat * row_of(gain) + row_of(shift)
        n2[...] = normed.astype(BF16)
        oacc[...] = jnp.zeros_like(oacc)
        gacc[...] = jnp.zeros_like(gacc)
        if packed:
            turned[...] = gated_t
            for dest in (e1, e1_send):
                for p in range(2):
                    for z in range(chips):
                        dest[pl.ds(p * slot + chips * half + z * share, share), :] = turned[
                            pl.ds(pl.multiple_of((2 * z + (core ^ p)) * share, 16), share), :
                        ]
            turned[...] = normed.T.astype(BF16)
            for dest in (e2, e2_send):
                write_strips(dest, 0, turned, chips, share, core)
        else:
            gatedt_out[...] = gated_t
            n2t_out[...] = normed.T.astype(BF16)

    bias = ubias[:, pl.ds(pl.multiple_of(j * ff, 128), ff)]
    pre = dot(n2[...], up[...]) + bias
    sq = pre * pre
    th = jnp.tanh(GELU_C * (pre * (1.0 + GELU_A * sq)))
    act = 0.5 * pre * (1.0 + th)
    slope = 0.5 * (1.0 + th) + 0.5 * pre * (1.0 - th * th) * (
        GELU_C * (1.0 + 3.0 * GELU_A * sq)
    )
    if packed:
        turned[...] = act.T.astype(BF16)
        for p in range(2):
            for dest, side in ((e1, x), (e1_send, 1 - x)):
                dest[pl.ds(pl.multiple_of(p * slot + j * half, 16), half), :] = turned[
                    pl.ds(pl.multiple_of((core ^ p) * big + side * half, 16), half), :
                ]
    else:
        actt[...] = act.T.astype(BF16)
    oacc[...] += dot(act.astype(BF16), down[...])
    gpre = (dot_t(cot[...], down[...]) * slope).astype(BF16)
    if packed:
        rows_held[...] = gpre
        per = chips // 2
        for t in range(ff // 128):
            place = pl.ds(pl.multiple_of(width + ((j % per) * (ff // 128) + t) * block, 16), block)
            tile = gpre[:, t * 128 : (t + 1) * 128]

            @pl.when(j // per == y)
            def _():
                e2[place, :] = tile

            @pl.when(j // per != y)
            def _():
                e2_send[place, :] = tile
    else:
        gpre_out[...] = gpre
    ubias_grad[:, pl.ds(pl.multiple_of(j * ff, 128), ff)] = jnp.sum(
        gpre.astype(F32), axis=0, keepdims=True
    )
    gacc[...] += dot_t(gpre, up[...])

    @pl.when(j == pl.num_programs(0) - 1)
    def _():
        output[...] = (resid[...] + oacc[...] + row_of(down_bias)).astype(BF16)
        top = cot[...].astype(F32)
        gn = gacc[...]
        hat = hat2[...]
        q = gn * row_of(gain)
        mean_q = jnp.mean(q, axis=-1, keepdims=True)
        mean_qh = jnp.mean(q * hat, axis=-1, keepdims=True)
        gr = top + (q - mean_q - hat * mean_qh) * rstd2[...]
        gresid[...] = gr
        gm = gr.astype(BF16)
        if packed:
            rows_held[...] = gm
            for dest, side in ((e1, x), (e1_send, 1 - x)):
                write_tiles(dest, 2 * slot, rows_held, side * (width // 2), width // 256)
        else:
            gmix_out[...] = gm
        gg = dot_t(gm, w_out[...])
        c = carried[...].astype(F32)
        long_out = conv[...] + row_of(fbias) * c
        gl = gg * gate_out[...]
        glong[...] = gl
        glong16[...] = gl.astype(BF16)
        ggate[...] = gg * long_out
        rows = [
            jnp.sum(top, axis=0, keepdims=True),
            jnp.sum(gn * hat, axis=0, keepdims=True),
            jnp.sum(gn, axis=0, keepdims=True),
            jnp.sum(gm.astype(F32), axis=0, keepdims=True),
            jnp.sum(gl * c, axis=0, keepdims=True),
        ]
        lanes = smalls.shape[1]
        for i, made in enumerate(rows):
            smalls[i : i + 1, :width] = made
            smalls[i : i + 1, width:] = jnp.zeros((1, lanes - width), F32)
        for i in range(ubias_grad.shape[1] // lanes):
            smalls[len(rows) + i : len(rows) + i + 1, :] = ubias_grad[:, i * lanes : (i + 1) * lanes]


def conv_back_kernel(ndocs, length, nparts, meta, *refs):
    parts, refs = refs[:nparts], refs[nparts:]
    (own_grad, lags, invt2, leftt3, fbias, gate_in, values, ggate, short_gate, short_in,
     short_values, for_in, for_values, rim, acc) = refs[:15]
    grads = parts[0]
    if nparts > 1:
        grads = refs[15]
        fill(meta, parts, grads, True)
    block = grads.shape[1]
    me = meta[0]
    base = me * block
    _, ids = doc_column(meta, ndocs, base, block)
    first_doc = doc_at(meta, ndocs, base)
    last_doc = doc_at(meta, ndocs, base + block - 1)
    last_block = (doc_end(meta, ndocs, base + block - 1, length) - 1) // block
    own = grads[me]
    spec = spectrum2(invt2[...], masked(own, ids == last_doc))
    set_spec(acc, times_back(lags[0], spec))

    def cross(t, carry):
        _, far = doc_column(meta, ndocs, t * block, block)
        spec = spectrum2(invt2[...], masked(grads[t], far == last_doc))
        add_spec(acc, times_back(lags[t - me], spec))
        return carry

    lax.fori_loop(me + 1, last_block + 1, cross, 0)
    for_in[...] = jnp.where(ids == last_doc, spectrum3(leftt3[...], acc[...]), 0.0)

    def inner(d, carry):
        spec = spectrum2(invt2[...], masked(own, ids == d))
        set_spec(acc, times_back(lags[0], spec))
        for_in[...] += jnp.where(ids == d, spectrum3(leftt3[...], acc[...]), 0.0)
        return carry

    lax.fori_loop(first_doc, last_doc, inner, 0)
    total = for_in[...] + row_of(fbias) * own_grad[...]
    for_in[...] = total * values[...]
    for_values[...] = total * gate_in[...]
    reach = short_gate.shape[0] - 1
    for third, (grad, taps) in enumerate(
        ((ggate, short_gate), (for_in, short_in), (for_values, short_values))
    ):
        rows = [jnp.zeros((8 - reach, grad.shape[1]), F32)]
        for p in range(reach):
            made = jnp.zeros((1, grad.shape[1]), F32)
            for k in range(1, reach + 1):
                t = p - reach + k
                if 0 <= t < reach:
                    same = doc_at(meta, ndocs, base - reach + p) == doc_at(meta, ndocs, base + t)
                    keep = (same & (base > 0)).astype(F32)
                    made = made + taps[k : k + 1, :].astype(F32) * grad[t : t + 1, :] * keep
            rows.append(made)
        rim[third] = jnp.concatenate(rows, axis=0)


def taps_grad_kernel(ndocs, nparts, meta, *refs):
    parts, refs = refs[:nparts], refs[nparts:]
    own_grad, left2, invt2, leftt3, out, win, gspec = refs[:7]
    signal = parts[0]
    if nparts > 1:
        signal = refs[7]
        fill(meta, parts, signal, False)
    blocks, block = signal.shape[0], signal.shape[1]
    me = meta[0]
    base = me * block
    start = doc_start(meta, ndocs, base)
    low_block = start // block
    _, ids = doc_column(meta, ndocs, base, block)
    first_doc = doc_at(meta, ndocs, base)
    last_doc = doc_at(meta, ndocs, base + block - 1)
    sign = 1.0 - 2.0 * (lax.broadcasted_iota(jnp.int32, (2 * block, 1), 0) % 2).astype(F32)
    own = signal[me]
    grad = own_grad[...]
    out[...] = jnp.zeros_like(out)
    win[me - low_block + 1] = jnp.zeros(win.shape[1:], F32)
    gspec[...] = spectrum2(invt2[...], masked(grad, ids == first_doc))
    spec = spectrum2(left2[...], masked(own, ids == first_doc))
    set_spec(win.at[0], times_back(spec, gspec[...]))

    def inner(d, carry):
        spec = spectrum2(left2[...], masked(own, ids == d))
        back = spectrum2(invt2[...], masked(grad, ids == d))
        add_spec(win.at[0], times_back(spec, back))
        return carry

    lax.fori_loop(first_doc + 1, last_doc + 1, inner, 0)

    def cross(s, carry):
        position = s * block + lax.broadcasted_iota(jnp.int32, (block, 1), 0)
        spec = spectrum2(left2[...], masked(signal[s], position >= start))
        set_spec(win.at[me - s], times_back(spec, gspec[...]))
        return carry

    lax.fori_loop(low_block, me, cross, 0)

    def emit(k, carry):
        out[k] = spectrum3(leftt3[...], win[k + 1] + sign * win[k])
        return carry

    lax.fori_loop(0, me - low_block + 1, emit, 0)


def short_back_kernel(ndocs, packed, meta, ggate, for_in, for_values, rim, proj, taps,
                      gproj_ref, smalls, *sends):
    block, width = ggate.shape
    taps_n = taps.shape[0]
    base = meta[0] * block
    position, ids = doc_column(meta, ndocs, base, block)
    masks = []
    for k in range(taps_n):
        _, back = doc_column(meta, ndocs, base - k, block)
        masks.append(((back == ids) & (position >= k)).astype(F32))
    row = lax.broadcasted_iota(jnp.int32, (block, 1), 0)
    ahead = []
    for k in range(1, taps_n):
        _, later = doc_column(meta, ndocs, base + k, block)
        ahead.append(((later == ids) & (row < block - k)).astype(F32))
    bias_rows, weight_rows, short_rows = [], [], []
    for third, grad_ref in enumerate((ggate, for_in, for_values)):
        cols = slice(third * width, (third + 1) * width)
        grad = grad_ref[...]
        total = taps[0:1, cols].astype(F32) * grad
        weights = [jnp.sum(grad * proj[pl.ds(RIM, block), cols], axis=0, keepdims=True)]
        for k in range(1, taps_n):
            moved = pltpu.roll(grad, block - k, 0) * ahead[k - 1]
            total = total + taps[k : k + 1, cols].astype(F32) * moved
            weights.append(
                jnp.sum(grad * masks[k] * proj[pl.ds(RIM - k, block), cols], axis=0, keepdims=True)
            )
        tail = jnp.concatenate([jnp.zeros((block - 8, width), F32), rim[third]], axis=0)
        low = (total + tail).astype(BF16)
        gproj_ref[:, cols] = low
        bias_rows.append(jnp.sum(low.astype(F32), axis=0, keepdims=True))
        short_rows.append(jnp.sum(grad, axis=0, keepdims=True))
        weight_rows.append(weights)
    rows = bias_rows + [weight_rows[t][k] for k in range(taps_n) for t in range(3)] + short_rows
    pad = smalls.shape[0] - len(rows)
    smalls[...] = jnp.concatenate(rows + [jnp.zeros((pad, width), F32)], axis=0)
    if packed:
        x = meta[3] % 2
        half = 3 * width // 2
        for dest, side in zip(sends, (x, 1 - x)):
            write_tiles(dest, 0, gproj_ref, side * half, half // 128)


def tail_kernel(meta, gproj, weight, tokens, gain, gresid, others, out, smalls):
    gn = dot_t(gproj[...], weight[...])
    hat, rstd = normalise(tokens[...].astype(F32))
    q = gn * row_of(gain)
    mean_q = jnp.mean(q, axis=-1, keepdims=True)
    mean_qh = jnp.mean(q * hat, axis=-1, keepdims=True)
    out[...] = gresid[...] + (q - mean_q - hat * mean_qh) * rstd
    smalls[...] = others[...]
    count = smalls.shape[0]
    smalls[count - 2 : count - 1, :] = jnp.sum(gn * hat, axis=0, keepdims=True)
    smalls[count - 1 :, :] = jnp.sum(gn, axis=0, keepdims=True)


def filter_taps(first, first_bias, second, second_bias, third, third_bias, last, sine_freq, length):
    lags = jnp.arange(length)
    bands = (first.shape[0] - 1) // 2
    moment = lags.astype(F32) / (length - 1)
    band_freq = jnp.linspace(0.0001, bands - 1, bands, dtype=F32)
    phase = 2.0 * math.pi / length * lags.astype(F32)
    angles = phase[:, None] * band_freq[None, :]
    features = jnp.concatenate([moment[:, None], jnp.cos(angles), -jnp.sin(angles)], axis=1)
    hidden = jnp.sin(sine_freq * (jnp.dot(features, first, precision=HIGHEST) + first_bias))
    hidden = jnp.sin(sine_freq * (jnp.dot(hidden, second, precision=HIGHEST) + second_bias))
    hidden = jnp.sin(sine_freq * (jnp.dot(hidden, third, precision=HIGHEST) + third_bias))
    rates = jnp.linspace(MIN_DECAY, MAX_DECAY, last.shape[1], dtype=F32)
    window = jnp.exp(-moment[:, None] * rates[None, :])
    return jnp.dot(hidden, last, precision=HIGHEST) * window


def sine_pair(values):
    turns = jnp.floor(values * (2.0 / math.pi) + 0.5)
    rest = values - turns * 1.5703125
    rest = rest - turns * 4.837512969970703125e-4
    rest = rest - turns * 7.549789948768648e-8
    sq = rest * rest
    s = ((-1.9515295891e-4 * sq + 8.3321608736e-3) * sq - 1.6666654611e-1) * sq * rest + rest
    c = ((2.443315711809948e-5 * sq - 1.388731625493765e-3) * sq + 4.166664568298827e-2) * sq * sq
    c = c - 0.5 * sq + 1.0
    quarter = turns.astype(jnp.int32)
    odd = (quarter & 1) == 1
    half = (quarter & 2) == 2
    first = jnp.where(odd, c, s)
    second = jnp.where(odd, s, c)
    return jnp.where(half, -first, first), jnp.where(half ^ odd, -second, second)


def exact_dot(weights, values):
    high = values.astype(BF16)
    rest = values - high.astype(F32)
    middle = rest.astype(BF16)
    low = (rest - middle.astype(F32)).astype(BF16)
    return dot(weights, high) + (dot(weights, middle) + dot(weights, low))


def feature_table(length, bands):
    lags = np.arange(length).astype(np.float32)
    moment = lags / np.float32(length - 1)
    freq = np.linspace(0.0001, bands - 1, bands).astype(np.float32)
    phase = np.float32(2.0 * math.pi / length) * lags
    angles = (phase[:, None] * freq[None, :]).astype(np.float64)
    table = np.concatenate(
        [moment[:, None].astype(np.float64), np.cos(angles), -np.sin(angles)], axis=1
    )
    return np.pad(table.astype(np.float32), ((0, 0), (0, -table.shape[1] % 8))).T


def decay_window(width, length):
    moment = lax.broadcasted_iota(jnp.int32, (length, 1), 0).astype(F32) / (length - 1)
    step = (MAX_DECAY - MIN_DECAY) / (width - 1)
    rates = MIN_DECAY + step * lax.broadcasted_iota(jnp.int32, (1, width), 1).astype(F32)
    return jnp.exp(-moment * rates)


def turned_column(ref):
    return jnp.broadcast_to(row_of(ref), (8, ref.shape[0])).T[:, :1]


def filter_kernel(meta, table, first, b1, second, b2, third, b3, last, freq, left3,
                  lags, window, act, slope, pre, a3):
    blocks, period, width = lags.shape
    block = period // 2
    length = blocks * block
    fwidth = freq.shape[0]
    scale = turned_column(freq)
    hidden = table[...]
    pad = table.shape[0] - first.shape[0]
    firsts = jnp.concatenate([first[...].astype(F32), jnp.zeros((pad, fwidth), F32)], axis=0)
    for i, (weight, bias) in enumerate(
        ((firsts, b1), (second[...].astype(F32), b2), (third[...].astype(F32), b3))
    ):
        u = exact_dot(weight.T.astype(BF16), hidden) + turned_column(bias)
        hidden, cosine = sine_pair(scale * u)
        rows = slice(i * fwidth, (i + 1) * fwidth)
        act[rows, :] = hidden
        slope[rows, :] = cosine
        pre[rows, :] = u
    a3[...] = hidden.T
    window[...] = decay_window(width, length)
    sign = 1.0 - 2.0 * (lax.broadcasted_iota(jnp.int32, (period, 1), 0) % 2).astype(F32)
    before = None
    for j in range(blocks):
        part = a3[j * block : (j + 1) * block, :]
        high = part.astype(BF16)
        rest = part - high.astype(F32)
        middle = rest.astype(BF16)
        low = (rest - middle.astype(F32)).astype(BF16)
        lhs = jnp.concatenate([high, middle, low], axis=1)
        rhs = jnp.concatenate([last[...]] * 3, axis=0)
        taps = dot(lhs, rhs) * window[j * block : (j + 1) * block, :]
        spec = spectrum3(left3[...], taps)
        lags[j] = sign * spec if before is None else before + sign * spec
        before = spec


def filter_back_kernel(meta, grads, window, act, slope, pre, table, first, second, third, last,
                       freq, others, mine, send, packed):
    blocks, block, width = grads.shape
    length = blocks * block
    fwidth = freq.shape[0]
    scale = turned_column(freq)
    core = meta[1]
    weighted = grads[...].reshape(length, width) * window[...]
    wh, wl = high_low(weighted)
    ah, al = high_low(act[2 * fwidth :, :])
    packed[...] = jnp.zeros_like(packed)
    packed[:fwidth, :width] = dot(ah, wh) + (dot(ah, wl) + dot(al, wh))
    packed[fwidth : fwidth + others.shape[0], :] = others[...]
    back = dot_t(last[...], wh) + dot_t(last[...], wl)
    ones = jnp.ones((8, length), BF16)

    def wide_t(left, right):
        lh, ll = high_low(left)
        rh, rl = high_low(right)
        return dot_t(lh, rh) + (dot_t(lh, rl) + dot_t(ll, rh))

    def sums(values):
        high, low = high_low(values)
        return (dot_t(ones, high) + dot_t(ones, low))[:1]

    freq_total = jnp.zeros((1, fwidth), F32)
    place = width
    for i, weight in ((2, third), (1, second), (0, first)):
        rows = slice(i * fwidth, (i + 1) * fwidth)
        step = back * slope[rows, :]
        freq_total = freq_total + sums(step * pre[rows, :])
        step = step * scale
        below = act[(i - 1) * fwidth : i * fwidth, :] if i else table[...]
        made = wide_t(below, step)
        packed[: made.shape[0], place : place + fwidth] = made
        packed[fwidth + others.shape[0] + i : fwidth + others.shape[0] + i + 1, :fwidth] = sums(step)
        place += fwidth
        if i:
            high, low = high_low(step)
            back = dot(weight[...], high) + dot(weight[...], low)
    at = fwidth + others.shape[0] + 3
    packed[at : at + 1, :fwidth] = freq_total
    half = packed.shape[0] // 2
    for side in range(2):

        def store(dest):
            dest[...] = packed[side * half : (side + 1) * half, :]

        pick(core == side, mine, send, store)


def shift(block, axis, distance):
    devices = range(lax.axis_size(axis))
    return lax.ppermute(block, axis, [(i - distance, i) for i in devices if i - distance in devices])


def swap(block, axis, mask):
    return lax.ppermute(block, axis, [(i, i ^ mask) for i in range(lax.axis_size(axis))])


def butterfly(values):
    for axis in ("seq", "rows"):
        mask = 1
        while mask < lax.axis_size(axis):
            values = values + swap(values, axis, mask)
            mask *= 2
    return values


def collect_kernel(meta, *refs):
    out = refs[-1]
    for k, ref in enumerate(refs[:-1]):
        out[k] = ref[...]


def along_row(meta, block, blocks, ahead, after):
    if blocks > 8:
        return (lax.all_gather(block, "seq", axis=0, tiled=False),)
    step = -2 if ahead else 2
    near = [block] + [shift(block, "seq", step * k) for k in range(1, blocks // 2)]
    (own,) = single(
        collect_kernel, "collect", 0.5, [jax.ShapeDtypeStruct((len(near),) + block.shape, block.dtype)],
        meta, near, after,
    )
    return own, swap(own, "seq", 1)


def joined_left(sources, first, slot, rows):
    return jnp.concatenate(
        [ref[pl.ds(first + (i % 2) * slot, rows), :] for i, ref in enumerate(sources)], axis=1
    )


def joined_right(sources, first, block, count):
    return jnp.concatenate(
        [
            jnp.concatenate([ref[pl.ds(first + t * block, block), :] for t in range(count)], axis=1)
            for ref in sources
        ],
        axis=0,
    )


def pick(flag, keep, send, store):
    @pl.when(flag)
    def _():
        store(keep)

    @pl.when(jnp.logical_not(flag))
    def _():
        store(send)


def down_out_kernel(chips, meta, *refs):
    acts, early, (keep, send) = refs[:4], refs[4:8], refs[8:]
    block = acts[0].shape[1]
    share = keep.shape[1]
    width = early[0].shape[0] // 2
    half = 2 * share
    slot = chips * (half + share)
    y, chip = meta[3] // 2, meta[2]
    made = dot(
        joined_left(acts, 0, slot, chips * half), joined_right(early, width, block, width // 128)
    ).astype(BF16)
    out = dot(
        joined_left(acts, chips * half, slot, chips * share),
        joined_right(acts, 2 * slot, block, width // 256),
    ).astype(BF16)
    part = share // 2
    for side in range(2):

        def store(dest):
            for z in range(chips):
                at = z ^ chip
                first = z * half + side * share
                dest[at, :, :width] = made[first : first + share]
                rows = out[z * share + side * part : z * share + (side + 1) * part]
                dest[at, :part, width : width + 128] = rows[:, :128]
                dest[at, part:, width : width + 128] = rows[:, 128:256]
                dest[at, :part, width + 128 :] = rows[:, 256:]
                dest[at, part:, width + 128 :] = jnp.zeros((part, 128), BF16)

        pick(y == side, keep, send, store)


def up_kernel(chips, meta, *refs):
    acts, (keep, send) = refs[:4], refs[4:]
    block = acts[0].shape[1]
    share, width = keep.shape[1:]
    x, chip = meta[3] % 2, meta[2]
    left = joined_left(acts, 0, width // 2, width // 2)
    for side in range(2):
        right = joined_right(acts, width + side * width, block, width // 128)
        made = dot(left, right).astype(BF16)

        def store(dest):
            for z in range(chips):
                dest[z ^ chip] = made[z * share : (z + 1) * share]

        pick(x == side, keep, send, store)


def in_kernel(chips, meta, *refs):
    acts, early, (keep, send) = refs[:4], refs[4:8], refs[8:]
    block = acts[0].shape[1]
    part, cols = keep.shape[1:]
    width = early[0].shape[0] // 2
    y, chip = meta[3] // 2, meta[2]
    made = dot(
        joined_left(early, 0, width // 2, width // 2), joined_right(acts, 0, block, cols // 128)
    ).astype(BF16)
    for side in range(2):

        def store(dest):
            for z in range(chips):
                first = (2 * z + side) * part
                dest[z ^ chip] = made[first : first + part]

        pick(y == side, keep, send, store)


def merge_kernel(meta, keep, got, own, *sends):
    own[...] = keep[0].astype(F32) + got[0].astype(F32)
    for j, dest in enumerate(sends):
        dest[...] = (keep[j + 1].astype(F32) + got[j + 1].astype(F32)).astype(BF16)


def spread_out(meta, keep, send, mask):
    chips, rows, cols = keep.shape
    outs = [jax.ShapeDtypeStruct((rows, cols), F32)]
    outs += [jax.ShapeDtypeStruct((rows, cols), BF16)] * (chips - 1)
    own, *sends = single(merge_kernel, "merge", 1.0, outs, meta, [keep, swap(send, "rows", mask)])
    for j, block in enumerate(sends):
        own = own + swap(block, "seq", 2 * (j + 1)).astype(F32)
    own = own.astype(BF16)
    return [own] + [swap(own, "rows", j) for j in (1, 2, 3)]


def unpack_kernel(taps_n, fwidth, feats, meta, first_half, second_half, late, *outs):
    (gain1, shift1, in_bias, short_weight, short_bias, f1, f1b, f2, f2b, f3, f3b, flast, freq,
     fbias, obias, gain2, shift2, ubias, dbias) = outs
    width = gain1.shape[0]
    half = first_half.shape[0]

    def rows(first, count):
        if first >= half:
            return second_half[first - half : first - half + count, :]
        return first_half[first : first + count, :]

    def flat(ref, piece, start=0):
        ref[pl.ds(start, piece.shape[1])] = piece.reshape(-1)

    for g in range(0, fwidth, 8):
        eight = rows(g, 8)
        flast[g : g + 8, :] = eight[:, :width]
        f3[g : g + 8, :] = eight[:, width : width + fwidth]
        f2[g : g + 8, :] = eight[:, width + fwidth : width + 2 * fwidth]
        take = min(8, feats - g)
        if take > 0:
            f1[g : g + take, :] = eight[:take, width + 2 * fwidth : width + 3 * fwidth]
    for i, ref in enumerate((dbias, gain2, shift2, obias, fbias)):
        flat(ref, rows(fwidth + i, 1)[:, :width])
    ubias[...] = jnp.concatenate([rows(fwidth + 5 + i, 1) for i in range(3)], axis=1).reshape(-1)
    for i, ref in enumerate((f1b, f2b, f3b, freq)):
        flat(ref, rows(fwidth + 8 + i, 1)[:, :fwidth])
    wide = lambda first: jnp.concatenate([late[first + i : first + i + 1, :] for i in range(3)], axis=1)
    in_bias[...] = wide(0).reshape(-1)
    for k in range(taps_n):
        short_weight[k : k + 1, :] = wide(3 + 3 * k)
    short_bias[...] = wide(3 + 3 * taps_n).reshape(-1)
    count = late.shape[0]
    flat(gain1, late[count - 2 : count - 1, :])
    flat(shift1, late[count - 1 : count, :])


def place_down_out_kernel(meta, *refs):
    pieces, (down, out) = refs[:4], refs[4:]
    row = meta[3]
    share = pieces[0].shape[0]
    width = out.shape[1]
    part = share // 2
    for j, piece in enumerate(pieces):
        x, y = (row ^ j) % 2, (row ^ j) // 2
        down[pl.ds(pl.multiple_of((2 * x + y) * share, 8), share), :] = piece[:, :width].astype(F32)
        tiles = (
            piece[:part, width : width + 128],
            piece[part:, width : width + 128],
            piece[:part, width + 128 :],
        )
        for t, tile in enumerate(tiles):
            cols = pl.ds(pl.multiple_of(x * (width // 2) + t * 128, 128), 128)
            out[pl.ds(pl.multiple_of(y * part, 8), part), cols] = tile.astype(F32)


def place_up_kernel(meta, *refs):
    pieces, up = refs[:4], refs[4]
    width = pieces[0].shape[1]
    for j, piece in enumerate(pieces):
        x, y = (meta[3] ^ j) % 2, (meta[3] ^ j) // 2
        up[:, pl.ds(pl.multiple_of((2 * y + x) * width, 128), width)] = piece[...].astype(F32)


def place_in_kernel(meta, *refs):
    pieces, full = refs[:4], refs[4]
    part, cols = pieces[0].shape
    for j, piece in enumerate(pieces):
        x, y = (meta[3] ^ j) % 2, (meta[3] ^ j) // 2
        full[pl.ds(pl.multiple_of(y * part, 8), part), pl.ds(pl.multiple_of(x * cols, 128), cols)] = (
            piece[...].astype(F32)
        )


def local(
    tokens, doc_starts, norm1_gain, norm1_bias, in_weight, in_bias, short_weight, short_bias,
    filter_first, filter_first_bias, filter_second, filter_second_bias, filter_third,
    filter_third_bias, filter_last, sine_freq, filter_bias, out_weight, out_bias, norm2_gain,
    norm2_bias, up_weight, up_bias, down_weight, down_bias, cotangent,
):
    block, width = tokens.shape[1:]
    blocks = lax.axis_size("seq")
    chips = blocks // 2
    nrows = lax.axis_size("rows")
    length = block * blocks
    hidden = up_weight.shape[1]
    index = lax.axis_index("seq")
    row = lax.axis_index("rows")
    starts = doc_starts[0]
    ndocs = starts.shape[0]
    taps_n = short_weight.shape[0]
    ff = width
    fsteps = hidden // ff
    share = width // blocks
    fits = blocks == 8 and nrows == 4 and fsteps == chips and share % 32 == 0 and block == 128
    packed = chips if fits and width == 768 else 0
    meta = jnp.concatenate(
        [jnp.stack([index, index % 2, index // 2, row]).astype(jnp.int32), starts]
    )
    tables = {k: jnp.asarray(v) for k, v in block_tables(block).items()}
    chunk = width if blocks <= 8 else 128
    steps = width // chunk
    tok, cot = tokens[0], cotangent[0]
    mat = whole((block, width))
    vec = whole((width,))
    sds = jax.ShapeDtypeStruct

    rim = shift(tok[block - RIM :], "seq", 1)
    proj, early, mixed, carried = single(
        partial(front_kernel, ndocs, packed), "front", 3.0,
        [sds((block + RIM, 3 * width), F32), sds((2 * width if packed else width, block), BF16),
         sds((block, 3 * width), F32), sds((block, width), BF16)],
        meta,
        [tok, rim, cot, norm1_gain, norm1_bias, in_weight, in_bias, short_weight, short_bias],
        scratch=[pltpu.VMEM((width, block), BF16)],
    )

    by_chunk = lambda lead: pl.BlockSpec(lead + (chunk,), lambda i: (0,) * len(lead) + (i,))
    fwidth, feats = sine_freq.shape[0], filter_first.shape[0]
    if packed:
        table = jnp.asarray(feature_table(length, (feats - 1) // 2))
        lags, window, *net = single(
            filter_kernel, "filter", 8.0,
            [sds((blocks, 2 * block, width), F32), sds((length, width), F32)]
            + [sds((3 * fwidth, length), F32)] * 3,
            meta,
            [table, filter_first, filter_first_bias, filter_second, filter_second_bias, filter_third,
             filter_third_bias, filter_last, sine_freq, tables["left3"]],
            after=[carried], scratch=[pltpu.VMEM((length, fwidth), F32)],
        )
    else:
        filter_params = tuple(
            v.astype(F32)
            for v in (filter_first, filter_first_bias, filter_second, filter_second_bias, filter_third,
                      filter_third_bias, filter_last, sine_freq)
        )
        taps, taps_pull = jax.vjp(partial(filter_taps, length=length), *filter_params)
        lags = pl.pallas_call(
            lag_kernel,
            grid=(steps,),
            out_shape=sds((blocks, 2 * block, width), F32),
            in_specs=[by_chunk((blocks, block)), whole(tables["left3"].shape)],
            out_specs=by_chunk((blocks, 2 * block)),
            compiler_params=params(),
            name="lags",
        )(taps.reshape(blocks, block, width), tables["left3"])

    signal = along_row(meta, carried, blocks, False, [lags])
    nparts = len(signal)
    part_specs = [by_chunk((v.shape[0], block)) for v in signal]
    held = [pltpu.VMEM((blocks, block, chunk), BF16)] if nparts > 1 else []
    spec_scratch = pltpu.VMEM((2 * block, chunk), F32)
    conv = pl.pallas_call(
        partial(conv_kernel, ndocs, nparts),
        grid=(steps,),
        out_shape=sds((block, width), F32),
        in_specs=[smem()] + part_specs + [by_chunk((blocks, 2 * block)),
                  whole(tables["left2"].shape), whole(tables["inv3"].shape)],
        out_specs=by_chunk((block,)),
        scratch_shapes=[spec_scratch] + held,
        compiler_params=params(),
        cost_estimate=cost(3.0),
        name="conv",
    )(meta, *signal, lags, tables["left2"], tables["inv3"])

    if packed:
        e1_rows = 2 * chips * 3 * share + width // 2
        e2_rows = width + hidden // 2
        extra = (sds((e1_rows, block), BF16),) * 2 + (sds((e2_rows, block), BF16),) * 2
        extra_specs = (whole((e1_rows, block)),) * 2 + (whole((e2_rows, block)),) * 2
    else:
        extra = (sds((hidden, block), BF16), sds((block, hidden), BF16), sds((width, block), BF16),
                 sds((width, block), BF16), sds((block, width), BF16))
        extra_specs = (pl.BlockSpec((ff, block), lambda i: (i, 0)),
                       pl.BlockSpec((block, ff), lambda i: (0, i)),
                       whole((width, block)), whole((width, block)), mat)
    lanes = hidden // 3
    output, gresid, glong, glong16, ggate, smalls_mlp, *acts = pl.pallas_call(
        partial(mlp_kernel, packed),
        grid=(fsteps,),
        out_shape=(
            sds((block, width), BF16), sds((block, width), F32),
            sds((block, width), F32), sds((block, width), BF16), sds((block, width), F32),
            sds((8, lanes), F32),
        ) + extra,
        in_specs=[
            smem(), mat, mat, mat, mat, mat, vec, whole((width, width)), vec, vec, vec,
            pl.BlockSpec((width, ff), lambda i: (0, i)), whole((hidden,)),
            pl.BlockSpec((ff, width), lambda i: (i, 0)), vec,
        ],
        out_specs=(mat, mat, mat, mat, mat, whole((8, lanes))) + extra_specs,
        scratch_shapes=[
            pltpu.VMEM((block, width), F32), pltpu.VMEM((block, width), BF16),
            pltpu.VMEM((block, width), F32), pltpu.VMEM((block, 1), F32),
            pltpu.VMEM((block, width), F32), pltpu.VMEM((block, width), F32),
            pltpu.VMEM((1, hidden), F32), pltpu.VMEM((1, hidden), F32),
            pltpu.VMEM((width, block), BF16), pltpu.VMEM((block, width), BF16),
        ],
        compiler_params=params(),
        cost_estimate=cost(10.0),
        name="mlp",
    )(meta, tok, cot, conv, carried, mixed, filter_bias, out_weight, out_bias, norm2_gain,
      norm2_bias, up_weight, up_bias, down_weight, down_bias)

    taps_grad = pl.pallas_call(
        partial(taps_grad_kernel, ndocs, nparts),
        grid=(steps,),
        out_shape=sds((blocks, block, width), F32),
        in_specs=[smem()] + part_specs + [
            by_chunk((block,)), whole(tables["left2"].shape), whole(tables["invt2"].shape),
            whole(tables["leftt3"].shape)],
        out_specs=by_chunk((blocks, block)),
        scratch_shapes=[pltpu.VMEM((blocks + 1, 2 * block, chunk), F32), spec_scratch] + held,
        compiler_params=params(),
        cost_estimate=cost(4.0),
        name="taps_grad",
    )(meta, *signal, glong, tables["left2"], tables["invt2"], tables["leftt3"])
    if packed:
        half_rows = (fwidth + 16) // 2
        mine, send = single(
            filter_back_kernel, "filter_back", 5.0, [sds((half_rows, lanes), F32)] * 2, meta,
            [taps_grad, window, *net, table, filter_first, filter_second, filter_third, filter_last,
             sine_freq, smalls_mlp],
            scratch=[pltpu.VMEM((2 * half_rows, lanes), F32)],
        )
        wait_for = [mine]
    else:
        filter_grads = taps_pull(taps_grad.reshape(length, width))
        wait_for = []

    grads = along_row(meta, glong16, blocks, True, wait_for)
    third = lambda n: pl.BlockSpec((block, chunk), lambda i: (0, n * steps + i))
    tap_third = lambda n: pl.BlockSpec((taps_n, chunk), lambda i: (0, n * steps + i))
    for_in, for_values, rim_out = pl.pallas_call(
        partial(conv_back_kernel, ndocs, length, nparts),
        grid=(steps,),
        out_shape=(sds((block, width), F32), sds((block, width), F32), sds((3, 8, width), F32)),
        in_specs=[smem()] + part_specs + [
            by_chunk((block,)), by_chunk((blocks, 2 * block)), whole(tables["invt2"].shape),
            whole(tables["leftt3"].shape), vec if steps == 1 else by_chunk((1,)), third(1), third(2),
            by_chunk((block,)), tap_third(0), tap_third(1), tap_third(2)],
        out_specs=(by_chunk((block,)), by_chunk((block,)), by_chunk((3, 8))),
        scratch_shapes=[spec_scratch] + held,
        compiler_params=params(),
        cost_estimate=cost(4.0),
        name="conv_back",
    )(meta, *grads, glong, lags, tables["invt2"], tables["leftt3"],
      filter_bias if steps == 1 else filter_bias.reshape(1, -1),
      mixed, mixed, ggate, short_weight, short_weight, short_weight)
    rim_back = shift(rim_out, "seq", -1)

    parts1 = parts2 = ()
    if packed:
        def gathered(mine, send, mask):
            got = swap(send, "rows", mask)
            return mine, swap(mine, "seq", 1), got, swap(got, "seq", 1)

        def partials(kernel, name, piece, arrays, after=()):
            return single(
                partial(kernel, chips), name, 3.0, [sds((chips,) + piece, BF16)] * 2, meta, arrays, after
            )

        e1, e1_send, e2, e2_send = acts
        early_all = gathered(early, early, 1)
        e1_all = gathered(e1, e1_send, 1)
        e2_all = gathered(e2, e2_send, 2)
        parts2 = partials(up_kernel, "up_grad", (share, width), e2_all, [rim_out])
        parts1 = partials(
            down_out_kernel, "down_out", (share, width + 256), (*e1_all, *early_all), [rim_out]
        )

    gproj, smalls_short, *late = single(
        partial(short_back_kernel, ndocs, packed), "short_back", 3.0,
        [sds((block, 3 * width), BF16), sds((24, width), F32)]
        + ([sds((3 * width // 2, block), BF16)] * 2 if packed else []),
        meta, [ggate, for_in, for_values, rim_back, proj, short_weight],
        after=[v[0] for v in (parts1, parts2) if v],
    )
    grad_tokens, smalls_late = single(
        tail_kernel, "tail", 2.5, [sds((block, width), F32), sds((24, width), F32)],
        meta, [gproj, in_weight, tok, norm1_gain, gresid, smalls_short],
    )

    if packed:
        def placed(kernel, name, shapes, pieces):
            return single(kernel, name, 1.5, [sds(v, F32) for v in shapes], meta, pieces)

        pieces1 = spread_out(meta, *parts1, 2)
        pieces2 = spread_out(meta, *parts2, 1)
        late_all = gathered(*late, 1)
        parts3 = partials(in_kernel, "in_grad", (share // 2, 3 * width // 2), (*late_all, *early_all))
        pieces3 = spread_out(meta, *parts3, 2)
        grad_down, grad_out = placed(
            place_down_out_kernel, "place_down_out", ((hidden // blocks, width), (share, width)), pieces1
        )
        (grad_up,) = placed(place_up_kernel, "place_up", ((share, hidden),), pieces2)
        (grad_in,) = placed(place_in_kernel, "place_in", ((share, 3 * width),), pieces3)

        small = mine + swap(send, "seq", 1)
        for axis, mask in (("rows", 1), ("rows", 2), ("seq", 2), ("seq", 4)):
            small = small + swap(small, axis, mask)
        other = swap(small, "seq", 1)
        first_half = jnp.where(index % 2 == 0, small, other)
        second_half = jnp.where(index % 2 == 0, other, small)
        shapes = [
            (width,), (width,), (3 * width,), (taps_n, 3 * width), (3 * width,), (feats, fwidth),
            (fwidth,), (fwidth, fwidth), (fwidth,), (fwidth, fwidth), (fwidth,), (fwidth, width),
            (fwidth,), (width,), (width,), (width,), (width,), (hidden,), (width,),
        ]
        smalls = single(
            partial(unpack_kernel, taps_n, fwidth, feats), "unpack", 1.5, [sds(v, F32) for v in shapes],
            meta, [first_half, second_half, butterfly(smalls_late)],
        )
    else:
        def summed(left, right):
            part = lax.psum_scatter(dot(left, right), "seq", scatter_dimension=0, tiled=True)
            return lax.psum(part, "rows")

        actt, gpre, n2t, gatedt, gmix = acts
        grad_in = summed(early, gproj)
        grad_out = summed(gatedt, gmix)
        grad_up = summed(n2t, gpre)
        grad_down = summed(actt, cot)
        small, late_sum, *fg = lax.psum((smalls_mlp, smalls_late, *filter_grads), ("rows", "seq"))
        wide = lambda first: late_sum[first : first + 3].reshape(-1)
        smalls = [
            late_sum[22], late_sum[23], wide(0), late_sum[3 : 3 + 3 * taps_n].reshape(taps_n, -1),
            wide(3 + 3 * taps_n), *fg, small[4, :width], small[3, :width], small[1, :width],
            small[2, :width], small[5:8].reshape(-1), small[0, :width],
        ]
    (grad_gain1, grad_shift1, grad_in_bias, grad_short_weight, grad_short_bias, f1, f1b, f2, f2b, f3,
     f3b, flast, freq, grad_filter_bias, grad_out_bias, grad_gain2, grad_shift2, grad_up_bias,
     grad_down_bias) = smalls
    return (
        output[None], grad_tokens[None], grad_gain1, grad_shift1, grad_in, grad_in_bias,
        grad_short_weight, grad_short_bias, f1, f1b, f2, f2b, f3, f3b, flast, freq,
        grad_filter_bias, grad_out, grad_out_bias, grad_gain2, grad_shift2, grad_up, grad_up_bias,
        grad_down, grad_down_bias,
    )


def solution(mesh):
    sharded = P("rows", "seq", None)
    placed = (sharded, P("rows", None)) + (P(),) * 23 + (sharded,)
    outs = [P()] * 25
    outs[0] = outs[1] = sharded
    for i in (4, 17, 21, 23):
        outs[i] = P("seq", None)
    return jax.shard_map(local, mesh=mesh, in_specs=placed, out_specs=tuple(outs), check_vma=False)
```

```python
from functools import partial
import math

import jax
import jax.numpy as jnp
import numpy as np
from jax import lax
from jax.experimental import pallas as pl
from jax.experimental.pallas import tpu as pltpu
from jax.sharding import PartitionSpec as P

EPSILON = 1e-05
HIGHEST = lax.Precision.HIGHEST
MIN_DECAY = math.log(100.0) / 1.5
MAX_DECAY = math.log(100.0) / 0.3
F32 = jnp.float32
BF16 = jnp.bfloat16
RIM = 16
LATE_ROWS = tuple(range(15)) + (22, 23)
VMEM_LIMIT = 26 * 1024 * 1024
GELU_C = math.sqrt(2.0 / math.pi)
GELU_A = 0.044715


def params(limit=VMEM_LIMIT):
    return pltpu.CompilerParams(vmem_limit_bytes=limit)


def cost(micros):
    return pl.CostEstimate(flops=int(micros * 1.1e9), bytes_accessed=0, transcendentals=0)


def single(kernel, name, micros, outs, scalars, arrays, after=(), scratch=(), fetch=(), limit=VMEM_LIMIT):
    count, skip, nouts = len(arrays), len(after), len(outs)

    def body(meta, *refs):
        ins, made = list(refs[:count]), refs[count + skip : count + skip + nouts]
        rest = list(refs[count + skip + nouts :])
        if fetch:
            sems, rest = rest[-1], rest[:-1]
            held, rest = rest[: len(fetch)], rest[len(fetch) :]
            copies = [
                pltpu.make_async_copy(ins[p], dest, sems.at[i])
                for i, (p, dest) in enumerate(zip(fetch, held))
            ]
            for copy in copies:
                copy.start()
            for copy in copies:
                copy.wait()
            for p, dest in zip(fetch, held):
                ins[p] = dest
        kernel(meta, *ins, *made, *rest)

    own = [pltpu.VMEM(arrays[p].shape, arrays[p].dtype) for p in fetch]
    sems = [pltpu.SemaphoreType.DMA((len(fetch),))] if fetch else []
    return pl.pallas_call(
        body,
        grid=(1,),
        out_shape=tuple(outs),
        in_specs=[smem()]
        + [
            pl.BlockSpec(memory_space=pltpu.HBM) if p in fetch else whole(v.shape)
            for p, v in enumerate(arrays)
        ]
        + [pl.BlockSpec(memory_space=pl.ANY)] * skip,
        out_specs=tuple(whole(v.shape) for v in outs),
        scratch_shapes=own + list(scratch) + sems,
        compiler_params=params(limit),
        cost_estimate=cost(micros),
        name=name,
    )(scalars, *arrays, *after)


def smem():
    return pl.BlockSpec(memory_space=pltpu.SMEM)


def whole(shape):
    return pl.BlockSpec(shape, lambda *_: (0,) * len(shape))


def dot(left, right):
    return jnp.dot(left, right, preferred_element_type=F32)


def dot_t(left, right):
    return lax.dot_general(left, right, (((1,), (1,)), ((), ())), preferred_element_type=F32)


def high_low(values):
    high = values.astype(BF16)
    return high, (values - high.astype(F32)).astype(BF16)


def doc_at(meta, ndocs, position):
    total = jnp.int32(-1)
    for d in range(ndocs):
        total = total + (position >= meta[4 + d]).astype(jnp.int32)
    return total


def doc_start(meta, ndocs, position):
    found = jnp.int32(0)
    for d in range(ndocs):
        found = jnp.where(position >= meta[4 + d], meta[4 + d], found)
    return found


def doc_end(meta, ndocs, position, length):
    found = jnp.int32(length)
    for d in reversed(range(ndocs)):
        found = jnp.where(position < meta[4 + d], meta[4 + d], found)
    return found


def doc_column(meta, ndocs, first, rows):
    position = first + lax.broadcasted_iota(jnp.int32, (rows, 1), 0)
    total = jnp.full((rows, 1), -1, jnp.int32)
    for d in range(ndocs):
        total = total + (position >= meta[4 + d]).astype(jnp.int32)
    return position, total


def block_tables(block):
    period = 2 * block
    packed = np.arange(period)
    freq = np.where(packed <= block, packed, packed - block)
    places = np.arange(period)
    angle = 2.0 * np.pi / period * (freq[:, None] * places[None, :] % period)
    real = (packed <= block)[:, None]
    forward = np.where(real, np.cos(angle), -np.sin(angle))
    scaling = np.where((packed == 0) | (packed == block), 1.0, 2.0) / period
    inverse = (forward * scaling[:, None]).T[block:]
    left = forward[:, :block]

    def split(table):
        table = table.astype(np.float32)
        high = table.astype(BF16)
        return high, (table - high.astype(np.float32)).astype(BF16)

    lh, ll = split(left)
    ih, il = split(inverse)
    return dict(
        left2=np.concatenate([lh, ll], 1),
        left3=np.concatenate([lh, lh, ll], 1),
        inv3=np.concatenate([ih, ih, il], 1),
        invt2=np.concatenate([ih.T, il.T], 1),
        leftt3=np.concatenate([lh.T, lh.T, ll.T], 1),
    )


def spectrum2(table, signal):
    return dot(table, jnp.concatenate([signal, signal], axis=0))


def spectrum3(table, values):
    high, low = high_low(values)
    return dot(table, jnp.concatenate([high, low, high], axis=0))


def masked(signal, mask):
    return jnp.where(mask, signal.astype(F32), 0.0).astype(BF16)


def first_row(shape):
    return lax.broadcasted_iota(jnp.int32, shape, 0) == 0


def times(left, right):
    half = left.shape[0] // 2
    lre, lim = left[:half], left[half:]
    rre, rim = right[:half], right[half:]
    row = first_row(lre.shape)
    edge = jnp.where(row, 0.0, lim)
    return lre * rre - edge * rim, edge * rre + jnp.where(row, lim, lre) * rim


def times_back(left, grad):
    half = left.shape[0] // 2
    lre, lim = left[:half], left[half:]
    gre, gim = grad[:half], grad[half:]
    row = first_row(lre.shape)
    edge = jnp.where(row, 0.0, lim)
    return lre * gre + edge * gim, jnp.where(row, lim, lre) * gim - edge * gre


def add_spec(acc, pair):
    half = acc.shape[0] // 2
    acc[:half, :] += pair[0]
    acc[half:, :] += pair[1]


def set_spec(acc, pair):
    half = acc.shape[0] // 2
    acc[:half, :] = pair[0]
    acc[half:, :] = pair[1]


def normalise(values):
    average = jnp.mean(values, axis=-1, keepdims=True)
    centred = values - average
    spread = jnp.mean(centred * centred, axis=-1, keepdims=True)
    rstd = lax.rsqrt(spread + EPSILON)
    return centred * rstd, rstd


def row_of(ref):
    return ref[...].astype(F32).reshape(1, -1)


def part_of(ref, first, size):
    return ref[pl.ds(first, size)].astype(F32).reshape(1, -1)


def write_side(out, first, source, count, rows, parity):
    for z in range(count):
        out[pl.ds(first + z * rows, rows), :] = source[
            pl.ds(pl.multiple_of((2 * z + parity) * rows, 16), rows), :
        ]


def write_strips(out, first, source, count, rows, core):
    for p in range(2):
        for z in range(count):
            out[pl.ds(first + (p * count + z) * rows, rows), :] = source[
                pl.ds(pl.multiple_of((2 * z + (core ^ p)) * rows, 16), rows), :
            ]


def write_tiles(out, first, source, start, count):
    tokens = source.shape[0]
    for t in range(count):
        out[pl.ds(first + t * tokens, tokens), :] = source[
            :, pl.ds(pl.multiple_of(start + t * 128, 128), 128)
        ]


def front_kernel(ndocs, packed, meta, tokens, rim, cot, gain, bias, weight, wbias, taps, tbias,
                 proj_ref, normt_ref, mixed_ref, carried_ref, turned):
    block, width = tokens.shape
    taps_n = taps.shape[0]
    ext = jnp.concatenate([rim[...], tokens[...]], axis=0).astype(F32)
    hat, _ = normalise(ext)
    normed = hat * row_of(gain) + row_of(bias)
    turned[...] = normed[RIM:].T.astype(BF16)
    if packed:
        chips = packed
        write_strips(normt_ref, 0, turned, chips, width // (2 * chips), meta[1])
        write_tiles(normt_ref, width, cot, 0, width // 128)
    else:
        normt_ref[...] = turned[...]
    low = normed.astype(BF16)
    base = meta[0] * block
    position, ids = doc_column(meta, ndocs, base, block)
    masks = []
    for k in range(taps_n):
        _, back = doc_column(meta, ndocs, base - k, block)
        masks.append(((back == ids) & (position >= k)).astype(F32))
    for third in range(3):
        cols = slice(third * width, (third + 1) * width)
        proj_ref[:, cols] = dot(low, weight[:, cols]) + part_of(wbias, third * width, width)
        total = part_of(tbias, third * width, width)
        for k in range(taps_n):
            moved = proj_ref[pl.ds(RIM - k, block), cols]
            total = total + taps[k : k + 1, cols].astype(F32) * moved * masks[k]
        mixed_ref[:, cols] = total
    carried_ref[...] = (mixed_ref[:, 2 * width :] * mixed_ref[:, width : 2 * width]).astype(BF16)


def lag_kernel(taps, left3, out):
    blocks = taps.shape[0]
    sign = 1.0 - 2.0 * (lax.broadcasted_iota(jnp.int32, (out.shape[1], 1), 0) % 2).astype(F32)

    def step(j, carry):
        spec = spectrum3(left3[...], taps[j])
        out[j] = out[j] + sign * spec

        @pl.when(j + 1 < blocks)
        def _():
            out[j + 1] = spec

        return carry

    out[0] = jnp.zeros(out.shape[1:], F32)
    lax.fori_loop(0, blocks, step, 0)


def fill(meta, parts, first, held):
    near, sibling = parts[:-1], parts[-1]
    block, width = held.shape[1:]
    for k, ref in enumerate(near):
        z = meta[2] ^ k
        held[2 * z + meta[1]] = ref[...]
        for t in range(width // 128):
            rows = pl.ds(first + (k * (width // 128) + t) * block, block)
            held[2 * z + 1 - meta[1], :, t * 128 : (t + 1) * 128] = sibling[rows, :]


def conv_kernel(ndocs, nparts, first, meta, *refs):
    parts, (lags, left2, inv3, out, acc), rest = refs[:nparts], refs[nparts : nparts + 5], refs[nparts + 5 :]
    signal = parts[0]
    if nparts > 1:
        (signal,) = rest
        fill(meta, parts, first, signal)
    block = signal.shape[1]
    me = meta[0]
    base = me * block
    start = doc_start(meta, ndocs, base)
    low_block = start // block
    _, ids = doc_column(meta, ndocs, base, block)
    first_doc = doc_at(meta, ndocs, base)
    last_doc = doc_at(meta, ndocs, base + block - 1)
    own = signal[me]
    spec = spectrum2(left2[...], masked(own, ids == first_doc))
    set_spec(acc, times(lags[0], spec))

    def cross(s, carry):
        position = s * block + lax.broadcasted_iota(jnp.int32, (block, 1), 0)
        spec = spectrum2(left2[...], masked(signal[s], position >= start))
        add_spec(acc, times(lags[me - s], spec))
        return carry

    lax.fori_loop(low_block, me, cross, 0)
    out[...] = jnp.where(ids == first_doc, spectrum3(inv3[...], acc[...]), 0.0)

    def inner(d, carry):
        spec = spectrum2(left2[...], masked(own, ids == d))
        set_spec(acc, times(lags[0], spec))
        out[...] += jnp.where(ids == d, spectrum3(inv3[...], acc[...]), 0.0)
        return carry

    lax.fori_loop(first_doc + 1, last_doc + 1, inner, 0)


def mlp_kernel(packed, meta, tokens, cot, conv, carried, gate_out, fbias, w_out, b_out, gain, shift,
               up, up_bias, down, down_bias, *refs):
    (output, gresid, glong, glong16, ggate, smalls), refs = refs[:6], refs[6:]
    (own, shared, e1_send, e2_send) = refs[:4]
    if packed:
        refs = refs[4:]
    else:
        actt, gpre_out, n2t_out, gatedt_out, gmix_out = refs[:5]
        refs = refs[5:]
    resid, n2, hat2, rstd2, oacc, gacc, ubias, ubias_grad, turned, rows_held = refs
    j = pl.program_id(0)
    block, width = tokens.shape
    ff = up.shape[1]
    core, x, y = meta[1], meta[3] % 2, meta[3] // 2
    chips = packed
    if packed:
        share, big = width // (2 * chips), ff // 2
        half = big // 2
        slot = chips * (half + share)

    @pl.when(j == 0)
    def _():
        ubias[...] = row_of(up_bias)
        long_out = conv[...] + row_of(fbias) * carried[...].astype(F32)
        gated = long_out * gate_out[...]
        gated_t = gated.T.astype(BF16)
        r = tokens[...].astype(F32) + dot(gated.astype(BF16), w_out[...]) + row_of(b_out)
        resid[...] = r
        hat, rstd = normalise(r)
        hat2[...] = hat
        rstd2[...] = rstd
        normed = hat * row_of(gain) + row_of(shift)
        n2[...] = normed.astype(BF16)
        oacc[...] = jnp.zeros_like(oacc)
        gacc[...] = jnp.zeros_like(gacc)
        if packed:
            turned[...] = gated_t
            later = chips * half
            for dest, p, first in ((own, 0, later), (shared, 1, later), (e1_send, 0, later),
                                   (e1_send, 1, slot + later)):
                write_side(dest, first, turned, chips, share, core ^ p)
            turned[...] = normed.T.astype(BF16)
            after1 = slot + width // 2
            for dest, p, first in ((own, 0, slot), (shared, 1, after1), (e2_send, 0, 0),
                                   (e2_send, 1, chips * share)):
                write_side(dest, first, turned, chips, share, core ^ p)
        else:
            gatedt_out[...] = gated_t
            n2t_out[...] = normed.T.astype(BF16)

    bias = ubias[:, pl.ds(pl.multiple_of(j * ff, 128), ff)]
    pre = dot(n2[...], up[...]) + bias
    sq = pre * pre
    th = jnp.tanh(GELU_C * (pre * (1.0 + GELU_A * sq)))
    act = 0.5 * pre * (1.0 + th)
    slope = 0.5 * (1.0 + th) + 0.5 * pre * (1.0 - th * th) * (
        GELU_C * (1.0 + 3.0 * GELU_A * sq)
    )
    if packed:
        turned[...] = act.T.astype(BF16)
        for dest, p, side, first in ((own, 0, x, 0), (shared, 1, x, 0), (e1_send, 0, 1 - x, 0),
                                     (e1_send, 1, 1 - x, slot)):
            dest[pl.ds(pl.multiple_of(first + j * half, 16), half), :] = turned[
                pl.ds(pl.multiple_of((core ^ p) * big + side * half, 16), half), :
            ]
    else:
        actt[...] = act.T.astype(BF16)
    oacc[...] += dot(act.astype(BF16), down[...])
    gpre = (dot_t(cot[...], down[...]) * slope).astype(BF16)
    if packed:
        rows_held[...] = gpre
        per = chips // 2
        for t in range(ff // 128):
            at = ((j % per) * (ff // 128) + t) * block
            tile = gpre[:, t * 128 : (t + 1) * 128]

            @pl.when(j // per == y)
            def _():
                first = slot + width // 2 + chips * share
                shared[pl.ds(pl.multiple_of(first + at, 16), block), :] = tile

            @pl.when(j // per != y)
            def _():
                e2_send[pl.ds(pl.multiple_of(width + at, 16), block), :] = tile
    else:
        gpre_out[...] = gpre
    ubias_grad[:, pl.ds(pl.multiple_of(j * ff, 128), ff)] = jnp.sum(
        gpre.astype(F32), axis=0, keepdims=True
    )
    gacc[...] += dot_t(gpre, up[...])

    @pl.when(j == pl.num_programs(0) - 1)
    def _():
        output[...] = (resid[...] + oacc[...] + row_of(down_bias)).astype(BF16)
        top = cot[...].astype(F32)
        gn = gacc[...]
        hat = hat2[...]
        q = gn * row_of(gain)
        mean_q = jnp.mean(q, axis=-1, keepdims=True)
        mean_qh = jnp.mean(q * hat, axis=-1, keepdims=True)
        gr = top + (q - mean_q - hat * mean_qh) * rstd2[...]
        gresid[...] = gr
        gm = gr.astype(BF16)
        if packed:
            rows_held[...] = gm
            write_tiles(shared, slot, rows_held, x * (width // 2), width // 256)
            write_tiles(e1_send, 2 * slot, rows_held, (1 - x) * (width // 2), width // 256)
        else:
            gmix_out[...] = gm
        gg = dot_t(gm, w_out[...])
        c = carried[...].astype(F32)
        long_out = conv[...] + row_of(fbias) * c
        gl = gg * gate_out[...]
        glong[...] = gl
        glong16[...] = gl.astype(BF16)
        ggate[...] = gg * long_out
        rows = [
            jnp.sum(top, axis=0, keepdims=True),
            jnp.sum(gn * hat, axis=0, keepdims=True),
            jnp.sum(gn, axis=0, keepdims=True),
            jnp.sum(gm.astype(F32), axis=0, keepdims=True),
            jnp.sum(gl * c, axis=0, keepdims=True),
        ]
        lanes = smalls.shape[1]
        for i, made in enumerate(rows):
            smalls[i : i + 1, :width] = made
            smalls[i : i + 1, width:] = jnp.zeros((1, lanes - width), F32)
        for i in range(ubias_grad.shape[1] // lanes):
            smalls[len(rows) + i : len(rows) + i + 1, :] = ubias_grad[:, i * lanes : (i + 1) * lanes]


def conv_back_kernel(ndocs, length, nparts, first, meta, *refs):
    parts, refs = refs[:nparts], refs[nparts:]
    (own_grad, lags, invt2, leftt3, fbias, gate_in, values, ggate, short_gate, short_in,
     short_values, for_in, for_values, rim, acc) = refs[:15]
    grads = parts[0]
    if nparts > 1:
        grads = refs[15]
        fill(meta, parts, first, grads)
    block = grads.shape[1]
    me = meta[0]
    base = me * block
    _, ids = doc_column(meta, ndocs, base, block)
    first_doc = doc_at(meta, ndocs, base)
    last_doc = doc_at(meta, ndocs, base + block - 1)
    last_block = (doc_end(meta, ndocs, base + block - 1, length) - 1) // block
    own = grads[me]
    spec = spectrum2(invt2[...], masked(own, ids == last_doc))
    set_spec(acc, times_back(lags[0], spec))

    def cross(t, carry):
        _, far = doc_column(meta, ndocs, t * block, block)
        spec = spectrum2(invt2[...], masked(grads[t], far == last_doc))
        add_spec(acc, times_back(lags[t - me], spec))
        return carry

    lax.fori_loop(me + 1, last_block + 1, cross, 0)
    for_in[...] = jnp.where(ids == last_doc, spectrum3(leftt3[...], acc[...]), 0.0)

    def inner(d, carry):
        spec = spectrum2(invt2[...], masked(own, ids == d))
        set_spec(acc, times_back(lags[0], spec))
        for_in[...] += jnp.where(ids == d, spectrum3(leftt3[...], acc[...]), 0.0)
        return carry

    lax.fori_loop(first_doc, last_doc, inner, 0)
    total = for_in[...] + row_of(fbias) * own_grad[...]
    for_in[...] = total * values[...]
    for_values[...] = total * gate_in[...]
    reach = short_gate.shape[0] - 1
    for third, (grad, taps) in enumerate(
        ((ggate, short_gate), (for_in, short_in), (for_values, short_values))
    ):
        rows = [jnp.zeros((8 - reach, grad.shape[1]), F32)]
        for p in range(reach):
            made = jnp.zeros((1, grad.shape[1]), F32)
            for k in range(1, reach + 1):
                t = p - reach + k
                if 0 <= t < reach:
                    same = doc_at(meta, ndocs, base - reach + p) == doc_at(meta, ndocs, base + t)
                    keep = (same & (base > 0)).astype(F32)
                    made = made + taps[k : k + 1, :].astype(F32) * grad[t : t + 1, :] * keep
            rows.append(made)
        rim[third] = jnp.concatenate(rows, axis=0)


def taps_grad_kernel(ndocs, nparts, first, meta, *refs):
    parts, refs = refs[:nparts], refs[nparts:]
    own_grad, left2, invt2, leftt3, out, win, gspec = refs[:7]
    signal = parts[0]
    if nparts > 1:
        signal = refs[7]
        fill(meta, parts, first, signal)
    blocks, block = signal.shape[0], signal.shape[1]
    me = meta[0]
    base = me * block
    start = doc_start(meta, ndocs, base)
    low_block = start // block
    _, ids = doc_column(meta, ndocs, base, block)
    first_doc = doc_at(meta, ndocs, base)
    last_doc = doc_at(meta, ndocs, base + block - 1)
    sign = 1.0 - 2.0 * (lax.broadcasted_iota(jnp.int32, (2 * block, 1), 0) % 2).astype(F32)
    own = signal[me]
    grad = own_grad[...]
    out[...] = jnp.zeros_like(out)
    win[me - low_block + 1] = jnp.zeros(win.shape[1:], F32)
    gspec[...] = spectrum2(invt2[...], masked(grad, ids == first_doc))
    spec = spectrum2(left2[...], masked(own, ids == first_doc))
    set_spec(win.at[0], times_back(spec, gspec[...]))

    def inner(d, carry):
        spec = spectrum2(left2[...], masked(own, ids == d))
        back = spectrum2(invt2[...], masked(grad, ids == d))
        add_spec(win.at[0], times_back(spec, back))
        return carry

    lax.fori_loop(first_doc + 1, last_doc + 1, inner, 0)

    def cross(s, carry):
        position = s * block + lax.broadcasted_iota(jnp.int32, (block, 1), 0)
        spec = spectrum2(left2[...], masked(signal[s], position >= start))
        set_spec(win.at[me - s], times_back(spec, gspec[...]))
        return carry

    lax.fori_loop(low_block, me, cross, 0)

    def emit(k, carry):
        out[k] = spectrum3(leftt3[...], win[k + 1] + sign * win[k])
        return carry

    lax.fori_loop(0, me - low_block + 1, emit, 0)


def short_back_kernel(ndocs, packed, meta, ggate, for_in, for_values, rim, proj, taps,
                      gproj_ref, smalls, *sends):
    block, width = ggate.shape
    taps_n = taps.shape[0]
    base = meta[0] * block
    position, ids = doc_column(meta, ndocs, base, block)
    masks = []
    for k in range(taps_n):
        _, back = doc_column(meta, ndocs, base - k, block)
        masks.append(((back == ids) & (position >= k)).astype(F32))
    row = lax.broadcasted_iota(jnp.int32, (block, 1), 0)
    ahead = []
    for k in range(1, taps_n):
        _, later = doc_column(meta, ndocs, base + k, block)
        ahead.append(((later == ids) & (row < block - k)).astype(F32))
    bias_rows, weight_rows, short_rows = [], [], []
    for third, grad_ref in enumerate((ggate, for_in, for_values)):
        cols = slice(third * width, (third + 1) * width)
        grad = grad_ref[...]
        total = taps[0:1, cols].astype(F32) * grad
        weights = [jnp.sum(grad * proj[pl.ds(RIM, block), cols], axis=0, keepdims=True)]
        for k in range(1, taps_n):
            moved = pltpu.roll(grad, block - k, 0) * ahead[k - 1]
            total = total + taps[k : k + 1, cols].astype(F32) * moved
            weights.append(
                jnp.sum(grad * masks[k] * proj[pl.ds(RIM - k, block), cols], axis=0, keepdims=True)
            )
        tail = jnp.concatenate([jnp.zeros((block - 8, width), F32), rim[third]], axis=0)
        low = (total + tail).astype(BF16)
        gproj_ref[:, cols] = low
        bias_rows.append(jnp.sum(low.astype(F32), axis=0, keepdims=True))
        short_rows.append(jnp.sum(grad, axis=0, keepdims=True))
        weight_rows.append(weights)
    rows = bias_rows + [weight_rows[t][k] for k in range(taps_n) for t in range(3)] + short_rows
    pad = smalls.shape[0] - len(rows)
    smalls[...] = jnp.concatenate(rows + [jnp.zeros((pad, width), F32)], axis=0)
    if packed:
        x = meta[3] % 2
        half = 3 * width // 2
        for dest, side in zip(sends, (x, 1 - x)):
            write_tiles(dest, 0, gproj_ref, side * half, half // 128)


def tail_kernel(meta, gproj, weight, tokens, gain, gresid, others, out, smalls):
    gn = dot_t(gproj[...], weight[...])
    hat, rstd = normalise(tokens[...].astype(F32))
    q = gn * row_of(gain)
    mean_q = jnp.mean(q, axis=-1, keepdims=True)
    mean_qh = jnp.mean(q * hat, axis=-1, keepdims=True)
    out[...] = gresid[...] + (q - mean_q - hat * mean_qh) * rstd
    rows = [others[i : i + 1, :] for i in range(others.shape[0] - 2)]
    rows += [jnp.sum(gn * hat, axis=0, keepdims=True), jnp.sum(gn, axis=0, keepdims=True)]
    if smalls.shape[1] == others.shape[1]:
        smalls[...] = jnp.concatenate(rows, axis=0)
        return
    smalls[...] = jnp.zeros_like(smalls)
    half = others.shape[1] // 2
    for k, (r, h) in enumerate((r, h) for r in LATE_ROWS for h in range(2)):
        smalls[k // 3 : k // 3 + 1, k % 3 * half : (k % 3 + 1) * half] = rows[r][:, h * half : (h + 1) * half]


def filter_taps(first, first_bias, second, second_bias, third, third_bias, last, sine_freq, length):
    lags = jnp.arange(length)
    bands = (first.shape[0] - 1) // 2
    moment = lags.astype(F32) / (length - 1)
    band_freq = jnp.linspace(0.0001, bands - 1, bands, dtype=F32)
    phase = 2.0 * math.pi / length * lags.astype(F32)
    angles = phase[:, None] * band_freq[None, :]
    features = jnp.concatenate([moment[:, None], jnp.cos(angles), -jnp.sin(angles)], axis=1)
    hidden = jnp.sin(sine_freq * (jnp.dot(features, first, precision=HIGHEST) + first_bias))
    hidden = jnp.sin(sine_freq * (jnp.dot(hidden, second, precision=HIGHEST) + second_bias))
    hidden = jnp.sin(sine_freq * (jnp.dot(hidden, third, precision=HIGHEST) + third_bias))
    rates = jnp.linspace(MIN_DECAY, MAX_DECAY, last.shape[1], dtype=F32)
    window = jnp.exp(-moment[:, None] * rates[None, :])
    return jnp.dot(hidden, last, precision=HIGHEST) * window


def sine_pair(values):
    turns = jnp.floor(values * (2.0 / math.pi) + 0.5)
    rest = values - turns * 1.5703125
    rest = rest - turns * 4.837512969970703125e-4
    rest = rest - turns * 7.549789948768648e-8
    sq = rest * rest
    s = ((-1.9515295891e-4 * sq + 8.3321608736e-3) * sq - 1.6666654611e-1) * sq * rest + rest
    c = ((2.443315711809948e-5 * sq - 1.388731625493765e-3) * sq + 4.166664568298827e-2) * sq * sq
    c = c - 0.5 * sq + 1.0
    quarter = turns.astype(jnp.int32)
    odd = (quarter & 1) == 1
    half = (quarter & 2) == 2
    first = jnp.where(odd, c, s)
    second = jnp.where(odd, s, c)
    return jnp.where(half, -first, first), jnp.where(half ^ odd, -second, second)


def exact_dot(weights, values):
    high = values.astype(BF16)
    rest = values - high.astype(F32)
    middle = rest.astype(BF16)
    low = (rest - middle.astype(F32)).astype(BF16)
    return dot(weights, high) + (dot(weights, middle) + dot(weights, low))


def feature_table(length, bands):
    lags = np.arange(length).astype(np.float32)
    moment = lags / np.float32(length - 1)
    freq = np.linspace(0.0001, bands - 1, bands).astype(np.float32)
    phase = np.float32(2.0 * math.pi / length) * lags
    angles = (phase[:, None] * freq[None, :]).astype(np.float64)
    table = np.concatenate(
        [moment[:, None].astype(np.float64), np.cos(angles), -np.sin(angles)], axis=1
    )
    return np.pad(table.astype(np.float32), ((0, 0), (0, -table.shape[1] % 8))).T


def decay_window(width, length):
    moment = lax.broadcasted_iota(jnp.int32, (length, 1), 0).astype(F32) / (length - 1)
    step = (MAX_DECAY - MIN_DECAY) / (width - 1)
    rates = MIN_DECAY + step * lax.broadcasted_iota(jnp.int32, (1, width), 1).astype(F32)
    return jnp.exp(-moment * rates)


def turned_column(ref):
    return jnp.broadcast_to(row_of(ref), (8, ref.shape[0])).T[:, :1]


def filter_kernel(meta, table, first, b1, second, b2, third, b3, last, freq, left3,
                  lags, window, act, slope, pre, a3):
    blocks, period, width = lags.shape
    block = period // 2
    length = blocks * block
    fwidth = freq.shape[0]
    scale = turned_column(freq)
    hidden = table[...]
    pad = table.shape[0] - first.shape[0]
    firsts = jnp.concatenate([first[...].astype(F32), jnp.zeros((pad, fwidth), F32)], axis=0)
    for i, (weight, bias) in enumerate(
        ((firsts, b1), (second[...].astype(F32), b2), (third[...].astype(F32), b3))
    ):
        u = exact_dot(weight.T.astype(BF16), hidden) + turned_column(bias)
        hidden, cosine = sine_pair(scale * u)
        rows = slice(i * fwidth, (i + 1) * fwidth)
        act[rows, :] = hidden
        slope[rows, :] = cosine
        pre[rows, :] = u
    a3[...] = hidden.T
    window[...] = decay_window(width, length)
    sign = 1.0 - 2.0 * (lax.broadcasted_iota(jnp.int32, (period, 1), 0) % 2).astype(F32)
    before = None
    for j in range(blocks):
        part = a3[j * block : (j + 1) * block, :]
        high = part.astype(BF16)
        rest = part - high.astype(F32)
        middle = rest.astype(BF16)
        low = (rest - middle.astype(F32)).astype(BF16)
        lhs = jnp.concatenate([high, middle, low], axis=1)
        rhs = jnp.concatenate([last[...]] * 3, axis=0)
        taps = dot(lhs, rhs) * window[j * block : (j + 1) * block, :]
        spec = spectrum3(left3[...], taps)
        lags[j] = sign * spec if before is None else before + sign * spec
        before = spec


def filter_back_kernel(meta, grads, window, act, slope, pre, table, first, second, third, last,
                       freq, others, mine, send, packed):
    blocks, block, width = grads.shape
    length = blocks * block
    fwidth = freq.shape[0]
    scale = turned_column(freq)
    core = meta[1]
    weighted = grads[...].reshape(length, width) * window[...]
    wh, wl = high_low(weighted)
    ah, al = high_low(act[2 * fwidth :, :])
    packed[...] = jnp.zeros_like(packed)
    half = fwidth // 2
    made = dot(ah, wh) + (dot(ah, wl) + dot(al, wh))
    packed[:half, :width] = made[:half]
    packed[:half, width : 2 * width] = made[half:]
    packed[half : half + others.shape[0], 256 : 256 + others.shape[1]] = others[...]
    back = dot_t(last[...], wh) + dot_t(last[...], wl)
    ones = jnp.ones((8, length), BF16)

    def wide_t(left, right):
        lh, ll = high_low(left)
        rh, rl = high_low(right)
        return dot_t(lh, rh) + (dot_t(lh, rl) + dot_t(ll, rh))

    def sums(values):
        high, low = high_low(values)
        return (dot_t(ones, high) + dot_t(ones, low))[:1]

    freq_total = jnp.zeros((1, fwidth), F32)
    place = 2 * width
    for i, weight in ((2, third), (1, second), (0, first)):
        rows = slice(i * fwidth, (i + 1) * fwidth)
        step = back * slope[rows, :]
        freq_total = freq_total + sums(step * pre[rows, :])
        step = step * scale
        below = act[(i - 1) * fwidth : i * fwidth, :] if i else table[...]
        made = wide_t(below, step)
        if i:
            packed[:half, place : place + fwidth] = made[:half]
            packed[:half, place + fwidth : place + 2 * fwidth] = made[half:]
            place += 2 * fwidth
        else:
            for part in range(0, made.shape[0], 16):
                lanes = slice(part // 16 * fwidth, part // 16 * fwidth + fwidth)
                piece = made[part : part + 16]
                packed[half : half + piece.shape[0], lanes] = piece
        packed[half + 8 + i : half + 9 + i, 2 * fwidth : 3 * fwidth] = sums(step)
        if i:
            high, low = high_low(step)
            back = dot(weight[...], high) + dot(weight[...], low)
    packed[half + 11 : half + 12, 2 * fwidth : 3 * fwidth] = freq_total
    half = packed.shape[0] // 2
    for side in range(2):

        def store(dest):
            dest[...] = packed[side * half : (side + 1) * half, :]

        pick(core == side, mine, send, store)


def shift(block, axis, distance):
    devices = range(lax.axis_size(axis))
    return lax.ppermute(block, axis, [(i - distance, i) for i in devices if i - distance in devices])


def swap(block, axis, mask):
    return lax.ppermute(block, axis, [(i, i ^ mask) for i in range(lax.axis_size(axis))])


def collect_kernel(spans, meta, *refs):
    out, place = refs[-1], 0
    for ref, span in zip(refs[:-1], spans):
        if span is None:
            write_tiles(out, place, ref, 0, ref.shape[1] // 128)
            place += ref.shape[0] * (ref.shape[1] // 128)
        else:
            out[pl.ds(place, span[1] - span[0]), :] = ref[pl.ds(span[0], span[1] - span[0]), :]
            place += span[1] - span[0]


def collected(meta, pieces, after=()):
    rows = sum(v.shape[0] * v.shape[1] // 128 if span is None else span[1] - span[0] for v, span in pieces)
    (out,) = single(
        partial(collect_kernel, [span for _, span in pieces]), "collect", 0.6,
        [jax.ShapeDtypeStruct((rows, 128), BF16)], meta, [v for v, _ in pieces], after,
    )
    return out


def near_blocks(block, blocks):
    got = {k: swap(block, "seq", 2 * k) for k in (2, 3, 1)}
    return [block] + [got[k] for k in range(1, blocks // 2)]


def joined_left(sources, rows):
    return jnp.concatenate([ref[pl.ds(first, rows), :] for ref, first in sources], axis=1)


def joined_right(sources, block, start, count):
    return jnp.concatenate(
        [
            jnp.concatenate(
                [ref[pl.ds(first + t * block, block), :] for t in range(start, start + count)], axis=1
            )
            for ref, first in sources
        ],
        axis=0,
    )


def pick(flag, keep, send, store):
    @pl.when(flag)
    def _():
        store(keep)

    @pl.when(jnp.logical_not(flag))
    def _():
        store(send)


def early_sources(early, early_got, early_sib, width, columns):
    half = width // 2
    if columns:
        return ((early, width), (early_sib, half), (early_got, width), (early_sib, 2 * width))
    return ((early, 0), (early_sib, 0), (early_got, 0), (early_sib, half + width))


def down_out_kernel(chips, meta, own, shared, shared_sib, got, got_sib, early, early_got, early_sib,
                    keep, send):
    block = own.shape[1]
    share = keep.shape[1]
    width = early.shape[0] // 2
    half = 2 * share
    slot = chips * (half + share)
    y, chip = meta[3] // 2, meta[2]
    sources = (own, shared_sib, got, got_sib)
    made = dot(
        joined_left([(v, 0) for v in sources], chips * half),
        joined_right(early_sources(early, early_got, early_sib, width, True), block, 0, width // 128),
    ).astype(BF16)
    right = ((shared, slot), (shared_sib, slot), (got, 2 * slot), (got_sib, slot))
    out = dot(
        joined_left([(v, chips * half) for v in sources], chips * share),
        joined_right(right, block, 0, width // 256),
    ).astype(BF16)
    part = share // 2
    for side in range(2):

        def store(dest):
            for z in range(chips):
                at = z ^ chip
                first = z * half + side * share
                dest[at, :, :width] = made[first : first + share]
                rows = out[z * share + side * part : z * share + (side + 1) * part]
                dest[at, :part, width : width + 128] = rows[:, :128]
                dest[at, part:, width : width + 128] = rows[:, 128:256]
                dest[at, :part, width + 128 :] = rows[:, 256:]
                dest[at, part:, width + 128 :] = jnp.zeros((part, 128), BF16)

        pick(y == side, keep, send, store)


def up_kernel(chips, meta, own, shared, shared_sib, got, got_sib, keep, send):
    block = own.shape[1]
    share, width = keep.shape[1:]
    x, chip = meta[3] % 2, meta[2]
    rows = chips * share
    slot = 3 * rows
    first = slot + width // 2
    left = joined_left(((own, slot), (shared_sib, first), (got, 0), (got_sib, first)), rows)
    right = ((shared, first + rows), (shared_sib, first + rows), (got, 2 * rows), (got_sib, first + rows))
    for side in range(2):
        made = dot(left, joined_right(right, block, side * (width // 128), width // 128)).astype(BF16)

        def store(dest):
            for z in range(chips):
                dest[z ^ chip] = made[z * share : (z + 1) * share]

        pick(x == side, keep, send, store)


def in_kernel(chips, meta, mine, got, sib, early, early_got, early_sib, keep, send):
    block = mine.shape[1]
    part, cols = keep.shape[1:]
    width = early.shape[0] // 2
    y, chip = meta[3] // 2, meta[2]
    right = ((mine, 0), (sib, 0), (got, 0), (sib, mine.shape[0]))
    made = dot(
        joined_left(early_sources(early, early_got, early_sib, width, False), width // 2),
        joined_right(right, block, 0, cols // 128),
    ).astype(BF16)
    for side in range(2):

        def store(dest):
            for z in range(chips):
                first = (2 * z + side) * part
                dest[z ^ chip] = made[first : first + part]

        pick(y == side, keep, send, store)


def merge_kernel(pairs, meta, *refs):
    ins, refs = refs[: 2 * pairs], refs[2 * pairs :]
    rows = ins[0].shape[1]
    chips = ins[0].shape[0]
    extra, (own, *sends) = refs[:-chips], refs[-chips:]
    first = 0
    for p in range(pairs):
        keep, got = ins[2 * p : 2 * p + 2]
        cols = slice(first, first + keep.shape[2])
        first += keep.shape[2]
        own[:rows, cols] = keep[0].astype(F32) + got[0].astype(F32)
        for j, dest in enumerate(sends):
            dest[:rows, cols] = (keep[j + 1].astype(F32) + got[j + 1].astype(F32)).astype(BF16)
    if extra:
        value = (extra[0][...] + extra[1][...]).astype(BF16)
        own[rows:, :] = value.astype(F32)
        for dest in sends:
            dest[rows:, :] = value


def total_kernel(extras, meta, own, one, two, three, *refs):
    rows = own.shape[0]
    out = refs[-1]
    out[:rows, :] = (
        (own[...] + one[...].astype(F32)) + (two[...].astype(F32) + three[...].astype(F32))
    ).astype(BF16)
    if extras:
        small = refs[0]
        out[rows : rows + small.shape[0], :] = small[...].astype(BF16)
        out[rows + small.shape[0] :, :] = jnp.zeros(
            (out.shape[0] - rows - small.shape[0], out.shape[1]), BF16
        )


def spread_out(meta, pairs, with_merge=(), with_total=()):
    chips, rows, _ = pairs[0].shape
    cols = sum(v.shape[2] for v in pairs[::2])
    rows += with_merge[0].shape[0] if with_merge else 0
    sds = jax.ShapeDtypeStruct
    own, *sends = single(
        partial(merge_kernel, len(pairs) // 2), "merge", 1.0,
        [sds((rows, cols), F32)] + [sds((rows, cols), BF16)] * (chips - 1), meta, (*pairs, *with_merge),
    )
    got = {j: swap(sends[j - 1], "seq", 2 * j) for j in (2, 3, 1)}
    (total,) = single(
        partial(total_kernel, len(with_total)), "total", 1.0,
        [sds((rows + (32 if with_total else 0), cols), BF16)], meta,
        [own, got[1], got[2], got[3], *with_total],
    )
    return [total] + [swap(total, "rows", j) for j in (1, 2, 3)]


def small_kernel(rows, meta, *refs):
    pieces, out = refs[:4], refs[4]
    take = pl.ds(rows, 32)
    a, b, c, d = (ref[take, :].astype(F32) for ref in pieces)
    total = (a + b) + (c + d)
    out[...] = total[: out.shape[0]]


def unpack_kernel(taps_n, fwidth, feats, first_late, meta, small, other, *refs):
    late_pieces, outs, packed, late = refs[:4], refs[4:-2], refs[-2], refs[-1]
    half = small.shape[0]
    even = meta[1] == 0
    packed[:half, :] = jnp.where(even, small[...], other[...])
    packed[half:, :] = jnp.where(even, other[...], small[...])
    (gain1, shift1, in_bias, short_weight, short_bias, f1, f1b, f2, f2b, f3, f3b, flast, freq,
     fbias, obias, gain2, shift2, ubias, dbias) = outs
    width = gain1.shape[0]
    take = pl.ds(first_late, late_pieces[0].shape[0] - first_late)
    a, b, c, d = (ref[take, :].astype(F32) for ref in late_pieces)
    late[...] = (a + b) + (c + d)
    part = fwidth // 2
    flast[:part, :] = packed[:part, :width]
    flast[part:, :] = packed[:part, width : 2 * width]
    place = 2 * width
    for ref in (f3, f2):
        ref[:part, :] = packed[:part, place : place + fwidth]
        ref[part:, :] = packed[:part, place + fwidth : place + 2 * fwidth]
        place += 2 * fwidth
    for first in range(0, feats, 16):
        count = min(16, feats - first)
        lanes = slice(first // 16 * fwidth, first // 16 * fwidth + fwidth)
        f1[first : first + count, :] = packed[part : part + count, lanes]
    for i, ref in enumerate((f1b, f2b, f3b, freq)):
        ref[...] = packed[part + 8 + i : part + 9 + i, 2 * fwidth : 3 * fwidth].reshape(-1)
    for i, ref in enumerate((dbias, gain2, shift2, obias, fbias)):
        ref[...] = packed[part + i : part + i + 1, 256 : 256 + width].reshape(-1)
    lanes = ubias.shape[0] // 3
    ubias[...] = jnp.concatenate(
        [packed[part + 5 + i : part + 6 + i, 256 : 256 + lanes] for i in range(3)], axis=1
    ).reshape(-1)
    side = late.shape[1] // 3

    def row(r):
        return [
            late[k // 3 : k // 3 + 1, k % 3 * side : (k % 3 + 1) * side] for k in (2 * r, 2 * r + 1)
        ]

    def wide(first):
        return jnp.concatenate(row(first) + row(first + 1) + row(first + 2), axis=1)

    in_bias[...] = wide(0).reshape(-1)
    for k in range(taps_n):
        short_weight[k : k + 1, :] = wide(3 + 3 * k)
    short_bias[...] = wide(3 + 3 * taps_n).reshape(-1)
    count = 6 + 3 * taps_n
    gain1[...] = jnp.concatenate(row(count), axis=1).reshape(-1)
    shift1[...] = jnp.concatenate(row(count + 1), axis=1).reshape(-1)


def place_early_kernel(meta, *refs):
    pieces, (down, out, up) = refs[:4], refs[4:]
    row = meta[3]
    share, width = out.shape
    part = share // 2
    for j, piece in enumerate(pieces):
        x, y = (row ^ j) % 2, (row ^ j) // 2
        down[pl.ds(pl.multiple_of((2 * x + y) * share, 8), share), :] = piece[:share, :width].astype(F32)
        tiles = (
            piece[:part, width : width + 128],
            piece[part:share, width : width + 128],
            piece[:part, width + 128 : width + 256],
        )
        for t, tile in enumerate(tiles):
            cols = pl.ds(pl.multiple_of(x * (width // 2) + t * 128, 128), 128)
            out[pl.ds(pl.multiple_of(y * part, 8), part), cols] = tile.astype(F32)
        cols = pl.ds(pl.multiple_of((2 * y + x) * width, 128), width)
        up[:, cols] = piece[:share, width + 256 :].astype(F32)


def place_in_kernel(meta, *refs):
    pieces, full = refs[:4], refs[4]
    part, cols = full.shape[0] // 2, pieces[0].shape[1]
    for j, piece in enumerate(pieces):
        x, y = (meta[3] ^ j) % 2, (meta[3] ^ j) // 2
        full[pl.ds(pl.multiple_of(y * part, 8), part), pl.ds(pl.multiple_of(x * cols, 128), cols)] = (
            piece[:part, :].astype(F32)
        )


def local(
    tokens, doc_starts, norm1_gain, norm1_bias, in_weight, in_bias, short_weight, short_bias,
    filter_first, filter_first_bias, filter_second, filter_second_bias, filter_third,
    filter_third_bias, filter_last, sine_freq, filter_bias, out_weight, out_bias, norm2_gain,
    norm2_bias, up_weight, up_bias, down_weight, down_bias, cotangent,
):
    block, width = tokens.shape[1:]
    blocks = lax.axis_size("seq")
    chips = blocks // 2
    nrows = lax.axis_size("rows")
    length = block * blocks
    hidden = up_weight.shape[1]
    index = lax.axis_index("seq")
    row = lax.axis_index("rows")
    starts = doc_starts[0]
    ndocs = starts.shape[0]
    taps_n = short_weight.shape[0]
    ff = width
    fsteps = hidden // ff
    share = width // blocks
    fits = blocks == 8 and nrows == 4 and fsteps == chips and share % 32 == 0 and block == 128
    packed = chips if fits and width == 768 else 0
    meta = jnp.concatenate(
        [jnp.stack([index, index % 2, index // 2, row]).astype(jnp.int32), starts]
    )
    tables = {k: jnp.asarray(v) for k, v in block_tables(block).items()}
    chunk = width if blocks <= 8 else 128
    steps = width // chunk
    tok, cot = tokens[0], cotangent[0]
    mat = whole((block, width))
    vec = whole((width,))
    sds = jax.ShapeDtypeStruct

    rim = shift(tok[block - RIM :], "seq", 1)
    proj, early, mixed, carried = single(
        partial(front_kernel, ndocs, packed), "front", 3.0,
        [sds((block + RIM, 3 * width), F32), sds((2 * width if packed else width, block), BF16),
         sds((block, 3 * width), F32), sds((block, width), BF16)],
        meta,
        [tok, rim, cot, norm1_gain, norm1_bias, in_weight, in_bias, short_weight, short_bias],
        scratch=[pltpu.VMEM((width, block), BF16)], limit=58 * 1024 * 1024,
    )

    early_got = swap(early, "rows", 1) if packed else None

    by_chunk = lambda lead: pl.BlockSpec(lead + (chunk,), lambda i: (0,) * len(lead) + (i,))
    fwidth, feats = sine_freq.shape[0], filter_first.shape[0]
    if packed:
        table = jnp.asarray(feature_table(length, (feats - 1) // 2))
        lags, window, *net = single(
            filter_kernel, "filter", 8.0,
            [sds((blocks, 2 * block, width), F32), sds((length, width), F32)]
            + [sds((3 * fwidth, length), F32)] * 3,
            meta,
            [table, filter_first, filter_first_bias, filter_second, filter_second_bias, filter_third,
             filter_third_bias, filter_last, sine_freq, tables["left3"]],
            after=[carried], scratch=[pltpu.VMEM((length, fwidth), F32)],
        )
    else:
        filter_params = tuple(
            v.astype(F32)
            for v in (filter_first, filter_first_bias, filter_second, filter_second_bias, filter_third,
                      filter_third_bias, filter_last, sine_freq)
        )
        taps, taps_pull = jax.vjp(partial(filter_taps, length=length), *filter_params)
        lags = pl.pallas_call(
            lag_kernel,
            grid=(steps,),
            out_shape=sds((blocks, 2 * block, width), F32),
            in_specs=[by_chunk((blocks, block)), whole(tables["left3"].shape)],
            out_specs=by_chunk((blocks, 2 * block)),
            compiler_params=params(),
            name="lags",
        )(taps.reshape(blocks, block, width), tables["left3"])

    if packed:
        near = near_blocks(carried, blocks)
        span = (width // 2, 2 * width)
        early_sib = swap(
            collected(
                meta, [(early, span), (early_got, span)] + [(v, None) for v in near], [lags]
            ), "seq", 1,
        )
        signal, signal_row = near + [early_sib], 3 * width
        nparts = len(signal)
        part_specs = [whole(v.shape) for v in signal]
        held = [pltpu.VMEM((blocks, block, chunk), BF16)]
    else:
        signal, signal_row = [lax.all_gather(carried, "seq", axis=0, tiled=False)], 0
        nparts, part_specs, held = 1, [by_chunk((blocks, block))], []
    spec_scratch = pltpu.VMEM((2 * block, chunk), F32)
    conv = pl.pallas_call(
        partial(conv_kernel, ndocs, nparts, signal_row),
        grid=(steps,),
        out_shape=sds((block, width), F32),
        in_specs=[smem()] + part_specs + [by_chunk((blocks, 2 * block)),
                  whole(tables["left2"].shape), whole(tables["inv3"].shape)],
        out_specs=by_chunk((block,)),
        scratch_shapes=[spec_scratch] + held,
        compiler_params=params(),
        cost_estimate=cost(3.0),
        name="conv",
    )(meta, *signal, lags, tables["left2"], tables["inv3"])

    if packed:
        left1, right1, left2, right2 = chips * 3 * share, width // 2, width // 2, hidden // 2
        row_counts = (
            left1 + left2, left1 + right1 + left2 + right2, 2 * left1 + right1, 2 * left2 + right2
        )
        extra = tuple(sds((n, block), BF16) for n in row_counts)
        extra_specs = tuple(whole((n, block)) for n in row_counts)
    else:
        extra = (sds((hidden, block), BF16), sds((block, hidden), BF16), sds((width, block), BF16),
                 sds((width, block), BF16), sds((block, width), BF16))
        extra_specs = (pl.BlockSpec((ff, block), lambda i: (i, 0)),
                       pl.BlockSpec((block, ff), lambda i: (0, i)),
                       whole((width, block)), whole((width, block)), mat)
    lanes = hidden // 3
    output, gresid, glong, glong16, ggate, smalls_mlp, *acts = pl.pallas_call(
        partial(mlp_kernel, packed),
        grid=(fsteps,),
        out_shape=(
            sds((block, width), BF16), sds((block, width), F32),
            sds((block, width), F32), sds((block, width), BF16), sds((block, width), F32),
            sds((8, lanes), F32),
        ) + extra,
        in_specs=[
            smem(), mat, mat, mat, mat, mat, vec, whole((width, width)), vec, vec, vec,
            pl.BlockSpec((width, ff), lambda i: (0, i)), whole((hidden,)),
            pl.BlockSpec((ff, width), lambda i: (i, 0)), vec,
        ],
        out_specs=(mat, mat, mat, mat, mat, whole((8, lanes))) + extra_specs,
        scratch_shapes=[
            pltpu.VMEM((block, width), F32), pltpu.VMEM((block, width), BF16),
            pltpu.VMEM((block, width), F32), pltpu.VMEM((block, 1), F32),
            pltpu.VMEM((block, width), F32), pltpu.VMEM((block, width), F32),
            pltpu.VMEM((1, hidden), F32), pltpu.VMEM((1, hidden), F32),
            pltpu.VMEM((width, block), BF16), pltpu.VMEM((block, width), BF16),
        ],
        compiler_params=params(),
        cost_estimate=cost(10.0),
        name="mlp",
    )(meta, tok, cot, conv, carried, mixed, filter_bias, out_weight, out_bias, norm2_gain,
      norm2_bias, up_weight, up_bias, down_weight, down_bias)

    taps_grad = pl.pallas_call(
        partial(taps_grad_kernel, ndocs, nparts, signal_row),
        grid=(steps,),
        out_shape=sds((blocks, block, width), F32),
        in_specs=[smem()] + part_specs + [
            by_chunk((block,)), whole(tables["left2"].shape), whole(tables["invt2"].shape),
            whole(tables["leftt3"].shape)],
        out_specs=by_chunk((blocks, block)),
        scratch_shapes=[pltpu.VMEM((blocks + 1, 2 * block, chunk), F32), spec_scratch] + held,
        compiler_params=params(),
        cost_estimate=cost(4.0),
        name="taps_grad",
    )(meta, *signal, glong, tables["left2"], tables["invt2"], tables["leftt3"])
    if packed:
        own, shared, e1_send, e2_send = acts
        got1, got2 = swap(e1_send, "rows", 1), swap(e2_send, "rows", 2)
        near = near_blocks(glong16, blocks)
        shared_sib = swap(shared, "seq", 1)
        bundle = collected(
            meta, [(got1, (left1, 2 * left1 + right1)), (got2, (left2, 2 * left2 + right2))]
            + [(v, None) for v in near],
        )
        got_sib = swap(bundle, "seq", 1)
        grads, grads_row = near + [got_sib], shared.shape[0]
        grad_specs = [whole(v.shape) for v in grads]
        half_rows, small_cols = (fwidth // 2 + 16) // 2, 2 * width + 4 * fwidth
        mine, send = single(
            filter_back_kernel, "filter_back", 5.0, [sds((half_rows, small_cols), F32)] * 2, meta,
            [taps_grad, window, *net, table, filter_first, filter_second, filter_third, filter_last,
             sine_freq, smalls_mlp],
            after=[bundle], scratch=[pltpu.VMEM((2 * half_rows, small_cols), F32)],
        )
    else:
        grads, grads_row = [lax.all_gather(glong16, "seq", axis=0, tiled=False)], 0
        grad_specs = part_specs
        filter_grads = taps_pull(taps_grad.reshape(length, width))

    third = lambda n: pl.BlockSpec((block, chunk), lambda i: (0, n * steps + i))
    tap_third = lambda n: pl.BlockSpec((taps_n, chunk), lambda i: (0, n * steps + i))
    for_in, for_values, rim_out = pl.pallas_call(
        partial(conv_back_kernel, ndocs, length, nparts, grads_row),
        grid=(steps,),
        out_shape=(sds((block, width), F32), sds((block, width), F32), sds((3, 8, width), F32)),
        in_specs=[smem()] + grad_specs + [
            by_chunk((block,)), by_chunk((blocks, 2 * block)), whole(tables["invt2"].shape),
            whole(tables["leftt3"].shape), vec if steps == 1 else by_chunk((1,)), third(1), third(2),
            by_chunk((block,)), tap_third(0), tap_third(1), tap_third(2)],
        out_specs=(by_chunk((block,)), by_chunk((block,)), by_chunk((3, 8))),
        scratch_shapes=[spec_scratch] + held,
        compiler_params=params(),
        cost_estimate=cost(4.0),
        name="conv_back",
    )(meta, *grads, glong, lags, tables["invt2"], tables["leftt3"],
      filter_bias if steps == 1 else filter_bias.reshape(1, -1),
      mixed, mixed, ggate, short_weight, short_weight, short_weight)
    rim_back = shift(rim_out, "seq", -1)
    tied = ()
    if packed:
        def partials(kernel, name, piece, arrays, after=()):
            return single(
                partial(kernel, chips), name, 3.0, [sds((chips,) + piece, BF16)] * 2, meta, arrays, after
            )

        parts2 = partials(up_kernel, "up_grad", (share, width), (own, shared, shared_sib, got2, got_sib), [rim_out])
        parts1 = partials(
            down_out_kernel, "down_out", (share, width + 256),
            (own, shared, shared_sib, got1, got_sib, early, early_got, early_sib), [rim_out],
        )
        small = mine + swap(send, "seq", 1)
        small = small + swap(small, "seq", 2)
        small = small + swap(small, "seq", 4)
        tied = (parts1[0], parts2[0])


    gproj, smalls_short, *late = single(
        partial(short_back_kernel, ndocs, packed), "short_back", 3.0,
        [sds((block, 3 * width), BF16), sds((24, width), F32)]
        + ([sds((3 * width // 2, block), BF16)] * 2 if packed else []),
        meta, [ggate, for_in, for_values, rim_back, proj, short_weight], tied,
    )
    late_shape = (16, 3 * width // 2) if packed else (24, width)
    grad_tokens, smalls_late = single(
        tail_kernel, "tail", 2.5, [sds((block, width), F32), sds(late_shape, F32)],
        meta, [gproj, in_weight, tok, norm1_gain, gresid, smalls_short],
    )

    if packed:
        def placed(kernel, name, shapes, pieces):
            return single(kernel, name, 1.5, [sds(v, F32) for v in shapes], meta, pieces)

        keep1, send1 = parts1
        keep2, send2 = parts2
        pieces = spread_out(
            meta, [keep1, swap(send1, "rows", 2), keep2, swap(send2, "rows", 1)], (), (small,)
        )
        late, late_send = late
        late_got = swap(late_send, "rows", 1)
        late_sib = swap(
            collected(
                meta, [(late, (0, late.shape[0])), (late_got, (0, late.shape[0]))], [small]
            ), "seq", 1
        )
        keep3, send3 = partials(
            in_kernel, "in_grad", (share // 2, 3 * width // 2),
            (late, late_got, late_sib, early, early_got, early_sib),
        )
        pieces3 = spread_out(
            meta, [keep3, swap(send3, "rows", 2)], (smalls_late, swap(smalls_late, "seq", 1))
        )
        grad_down, grad_out, grad_up = placed(
            place_early_kernel, "place_early",
            ((hidden // blocks, width), (share, width), (share, hidden)), pieces,
        )
        (grad_in,) = placed(place_in_kernel, "place_in", ((share, 3 * width),), pieces3)

        (small,) = single(
            partial(small_kernel, share), "small", 0.5, [sds((half_rows, small_cols), F32)], meta, pieces
        )
        other = swap(small, "seq", 1)
        shapes = [
            (width,), (width,), (3 * width,), (taps_n, 3 * width), (3 * width,), (feats, fwidth),
            (fwidth,), (fwidth, fwidth), (fwidth,), (fwidth, fwidth), (fwidth,), (fwidth, width),
            (fwidth,), (width,), (width,), (width,), (width,), (hidden,), (width,),
        ]
        smalls = single(
            partial(unpack_kernel, taps_n, fwidth, feats, share // 2), "unpack", 1.5,
            [sds(v, F32) for v in shapes], meta, [small, other, *pieces3],
            scratch=[pltpu.VMEM((2 * half_rows, small_cols), F32), pltpu.VMEM(late_shape, F32)],
        )
    else:
        def summed(left, right):
            part = lax.psum_scatter(dot(left, right), "seq", scatter_dimension=0, tiled=True)
            return lax.psum(part, "rows")

        actt, gpre, n2t, gatedt, gmix = acts
        grad_in = summed(early, gproj)
        grad_out = summed(gatedt, gmix)
        grad_up = summed(n2t, gpre)
        grad_down = summed(actt, cot)
        small, late_sum, *fg = lax.psum((smalls_mlp, smalls_late, *filter_grads), ("rows", "seq"))
        wide = lambda first: late_sum[first : first + 3].reshape(-1)
        smalls = [
            late_sum[22], late_sum[23], wide(0), late_sum[3 : 3 + 3 * taps_n].reshape(taps_n, -1),
            wide(3 + 3 * taps_n), *fg, small[4, :width], small[3, :width], small[1, :width],
            small[2, :width], small[5:8].reshape(-1), small[0, :width],
        ]
    (grad_gain1, grad_shift1, grad_in_bias, grad_short_weight, grad_short_bias, f1, f1b, f2, f2b, f3,
     f3b, flast, freq, grad_filter_bias, grad_out_bias, grad_gain2, grad_shift2, grad_up_bias,
     grad_down_bias) = smalls
    return (
        output[None], grad_tokens[None], grad_gain1, grad_shift1, grad_in, grad_in_bias,
        grad_short_weight, grad_short_bias, f1, f1b, f2, f2b, f3, f3b, flast, freq,
        grad_filter_bias, grad_out, grad_out_bias, grad_gain2, grad_shift2, grad_up, grad_up_bias,
        grad_down, grad_down_bias,
    )


def solution(mesh):
    sharded = P("rows", "seq", None)
    placed = (sharded, P("rows", None)) + (P(),) * 23 + (sharded,)
    outs = [P()] * 25
    outs[0] = outs[1] = sharded
    for i in (4, 17, 21, 23):
        outs[i] = P("seq", None)
    return jax.shard_map(local, mesh=mesh, in_specs=placed, out_specs=tuple(outs), check_vma=False)
```

```python
from functools import partial
import math

import jax
import jax.numpy as jnp
import numpy as np
from jax import lax
from jax.experimental import pallas as pl
from jax.experimental.pallas import tpu as pltpu
from jax.sharding import PartitionSpec as P

EPSILON = 1e-05
HIGHEST = lax.Precision.HIGHEST
MIN_DECAY = math.log(100.0) / 1.5
MAX_DECAY = math.log(100.0) / 0.3
F32 = jnp.float32
BF16 = jnp.bfloat16
RIM = 16
OTHER_ROWS = 496
SMALL_BLOCK = 80
LATE_ROWS = tuple(range(15)) + (22, 23)
VMEM_LIMIT = 26 * 1024 * 1024
GELU_C = math.sqrt(2.0 / math.pi)
GELU_A = 0.044715


def params(limit=VMEM_LIMIT):
    return pltpu.CompilerParams(vmem_limit_bytes=limit)


def cost(micros):
    return pl.CostEstimate(flops=int(micros * 1.1e9), bytes_accessed=0, transcendentals=0)


def single(kernel, name, micros, outs, scalars, arrays, after=(), scratch=(), fetch=(), limit=VMEM_LIMIT):
    count, skip, nouts = len(arrays), len(after), len(outs)

    def body(meta, *refs):
        ins, made = list(refs[:count]), refs[count + skip : count + skip + nouts]
        rest = list(refs[count + skip + nouts :])
        if fetch:
            sems, rest = rest[-1], rest[:-1]
            held, rest = rest[: len(fetch)], rest[len(fetch) :]
            copies = [
                pltpu.make_async_copy(ins[p], dest, sems.at[i])
                for i, (p, dest) in enumerate(zip(fetch, held))
            ]
            for copy in copies:
                copy.start()
            for copy in copies:
                copy.wait()
            for p, dest in zip(fetch, held):
                ins[p] = dest
        kernel(meta, *ins, *made, *rest)

    own = [pltpu.VMEM(arrays[p].shape, arrays[p].dtype) for p in fetch]
    sems = [pltpu.SemaphoreType.DMA((len(fetch),))] if fetch else []
    return pl.pallas_call(
        body,
        grid=(1,),
        out_shape=tuple(outs),
        in_specs=[smem()]
        + [
            pl.BlockSpec(memory_space=pltpu.HBM) if p in fetch else whole(v.shape)
            for p, v in enumerate(arrays)
        ]
        + [pl.BlockSpec(memory_space=pl.ANY)] * skip,
        out_specs=tuple(whole(v.shape) for v in outs),
        scratch_shapes=own + list(scratch) + sems,
        compiler_params=params(limit),
        cost_estimate=cost(micros),
        name=name,
    )(scalars, *arrays, *after)


def smem():
    return pl.BlockSpec(memory_space=pltpu.SMEM)


def whole(shape):
    return pl.BlockSpec(shape, lambda *_: (0,) * len(shape))


def dot(left, right):
    return jnp.dot(left, right, preferred_element_type=F32)


def dot_t(left, right):
    return lax.dot_general(left, right, (((1,), (1,)), ((), ())), preferred_element_type=F32)


def high_low(values):
    high = values.astype(BF16)
    return high, (values - high.astype(F32)).astype(BF16)


def doc_at(meta, ndocs, position):
    total = jnp.int32(-1)
    for d in range(ndocs):
        total = total + (position >= meta[4 + d]).astype(jnp.int32)
    return total


def doc_start(meta, ndocs, position):
    found = jnp.int32(0)
    for d in range(ndocs):
        found = jnp.where(position >= meta[4 + d], meta[4 + d], found)
    return found


def doc_end(meta, ndocs, position, length):
    found = jnp.int32(length)
    for d in reversed(range(ndocs)):
        found = jnp.where(position < meta[4 + d], meta[4 + d], found)
    return found


def doc_column(meta, ndocs, first, rows):
    position = first + lax.broadcasted_iota(jnp.int32, (rows, 1), 0)
    total = jnp.full((rows, 1), -1, jnp.int32)
    for d in range(ndocs):
        total = total + (position >= meta[4 + d]).astype(jnp.int32)
    return position, total


def block_tables(block):
    period = 2 * block
    packed = np.arange(period)
    freq = np.where(packed <= block, packed, packed - block)
    places = np.arange(period)
    angle = 2.0 * np.pi / period * (freq[:, None] * places[None, :] % period)
    real = (packed <= block)[:, None]
    forward = np.where(real, np.cos(angle), -np.sin(angle))
    scaling = np.where((packed == 0) | (packed == block), 1.0, 2.0) / period
    inverse = (forward * scaling[:, None]).T[block:]
    left = forward[:, :block]

    def split(table):
        table = table.astype(np.float32)
        high = table.astype(BF16)
        return high, (table - high.astype(np.float32)).astype(BF16)

    lh, ll = split(left)
    ih, il = split(inverse)
    return dict(
        left2=np.concatenate([lh, ll], 1),
        left3=np.concatenate([lh, lh, ll], 1),
        inv3=np.concatenate([ih, ih, il], 1),
        invt2=np.concatenate([ih.T, il.T], 1),
        leftt3=np.concatenate([lh.T, lh.T, ll.T], 1),
    )


def spectrum2(table, signal):
    return dot(table, jnp.concatenate([signal, signal], axis=0))


def spectrum3(table, values):
    high, low = high_low(values)
    return dot(table, jnp.concatenate([high, low, high], axis=0))


def masked(signal, mask):
    return jnp.where(mask, signal.astype(F32), 0.0).astype(BF16)


def first_row(shape):
    return lax.broadcasted_iota(jnp.int32, shape, 0) == 0


def times(left, right):
    half = left.shape[0] // 2
    lre, lim = left[:half], left[half:]
    rre, rim = right[:half], right[half:]
    row = first_row(lre.shape)
    edge = jnp.where(row, 0.0, lim)
    return lre * rre - edge * rim, edge * rre + jnp.where(row, lim, lre) * rim


def times_back(left, grad):
    half = left.shape[0] // 2
    lre, lim = left[:half], left[half:]
    gre, gim = grad[:half], grad[half:]
    row = first_row(lre.shape)
    edge = jnp.where(row, 0.0, lim)
    return lre * gre + edge * gim, jnp.where(row, lim, lre) * gim - edge * gre


def add_spec(acc, pair):
    half = acc.shape[0] // 2
    acc[:half, :] += pair[0]
    acc[half:, :] += pair[1]


def set_spec(acc, pair):
    half = acc.shape[0] // 2
    acc[:half, :] = pair[0]
    acc[half:, :] = pair[1]


def normalise(values):
    average = jnp.mean(values, axis=-1, keepdims=True)
    centred = values - average
    spread = jnp.mean(centred * centred, axis=-1, keepdims=True)
    rstd = lax.rsqrt(spread + EPSILON)
    return centred * rstd, rstd


def row_of(ref):
    return ref[...].astype(F32).reshape(1, -1)


def part_of(ref, first, size):
    return ref[pl.ds(first, size)].astype(F32).reshape(1, -1)


def write_side(out, first, source, count, rows, parity):
    for z in range(count):
        out[pl.ds(first + z * rows, rows), :] = source[
            pl.ds(pl.multiple_of((2 * z + parity) * rows, 16), rows), :
        ]


def write_strips(out, first, source, count, rows, core):
    for p in range(2):
        for z in range(count):
            out[pl.ds(first + (p * count + z) * rows, rows), :] = source[
                pl.ds(pl.multiple_of((2 * z + (core ^ p)) * rows, 16), rows), :
            ]


def write_tiles(out, first, source, start, count):
    tokens = source.shape[0]
    for t in range(count):
        out[pl.ds(first + t * tokens, tokens), :] = source[
            :, pl.ds(pl.multiple_of(start + t * 128, 128), 128)
        ]


def front_kernel(ndocs, packed, meta, tokens, rim, cot, gain, bias, weight, wbias, taps, tbias,
                 proj_ref, normt_ref, mixed_ref, carried_ref, turned):
    block, width = tokens.shape
    taps_n = taps.shape[0]
    ext = jnp.concatenate([rim[...], tokens[...]], axis=0).astype(F32)
    hat, _ = normalise(ext)
    normed = hat * row_of(gain) + row_of(bias)
    turned[...] = normed[RIM:].T.astype(BF16)
    if packed:
        chips = packed
        write_strips(normt_ref, 0, turned, chips, width // (2 * chips), meta[1])
        write_tiles(normt_ref, width, cot, 0, width // 128)
    else:
        normt_ref[...] = turned[...]
    low = normed.astype(BF16)
    base = meta[0] * block
    position, ids = doc_column(meta, ndocs, base, block)
    masks = []
    for k in range(taps_n):
        _, back = doc_column(meta, ndocs, base - k, block)
        masks.append(((back == ids) & (position >= k)).astype(F32))
    for third in range(3):
        cols = slice(third * width, (third + 1) * width)
        proj_ref[:, cols] = dot(low, weight[:, cols]) + part_of(wbias, third * width, width)
        total = part_of(tbias, third * width, width)
        for k in range(taps_n):
            moved = proj_ref[pl.ds(RIM - k, block), cols]
            total = total + taps[k : k + 1, cols].astype(F32) * moved * masks[k]
        mixed_ref[:, cols] = total
    carried_ref[...] = (mixed_ref[:, 2 * width :] * mixed_ref[:, width : 2 * width]).astype(BF16)


def lag_kernel(taps, left3, out):
    blocks = taps.shape[0]
    sign = 1.0 - 2.0 * (lax.broadcasted_iota(jnp.int32, (out.shape[1], 1), 0) % 2).astype(F32)

    def step(j, carry):
        spec = spectrum3(left3[...], taps[j])
        out[j] = out[j] + sign * spec

        @pl.when(j + 1 < blocks)
        def _():
            out[j + 1] = spec

        return carry

    out[0] = jnp.zeros(out.shape[1:], F32)
    lax.fori_loop(0, blocks, step, 0)


def fill(meta, parts, first, held):
    near, sibling = parts[:-1], parts[-1]
    block, width = held.shape[1:]
    for k, ref in enumerate(near):
        z = meta[2] ^ k
        held[2 * z + meta[1]] = ref[...]
        for t in range(width // 128):
            rows = pl.ds(first + (k * (width // 128) + t) * block, block)
            held[2 * z + 1 - meta[1], :, t * 128 : (t + 1) * 128] = sibling[rows, :]


def conv_kernel(ndocs, nparts, first, meta, *refs):
    parts, (lags, left2, inv3, out, acc), rest = refs[:nparts], refs[nparts : nparts + 5], refs[nparts + 5 :]
    signal = parts[0]
    if nparts > 1:
        (signal,) = rest
        fill(meta, parts, first, signal)
    block = signal.shape[1]
    me = meta[0]
    base = me * block
    start = doc_start(meta, ndocs, base)
    low_block = start // block
    _, ids = doc_column(meta, ndocs, base, block)
    first_doc = doc_at(meta, ndocs, base)
    last_doc = doc_at(meta, ndocs, base + block - 1)
    own = signal[me]
    spec = spectrum2(left2[...], masked(own, ids == first_doc))
    set_spec(acc, times(lags[0], spec))

    def cross(s, carry):
        position = s * block + lax.broadcasted_iota(jnp.int32, (block, 1), 0)
        spec = spectrum2(left2[...], masked(signal[s], position >= start))
        add_spec(acc, times(lags[me - s], spec))
        return carry

    lax.fori_loop(low_block, me, cross, 0)
    out[...] = jnp.where(ids == first_doc, spectrum3(inv3[...], acc[...]), 0.0)

    def inner(d, carry):
        spec = spectrum2(left2[...], masked(own, ids == d))
        set_spec(acc, times(lags[0], spec))
        out[...] += jnp.where(ids == d, spectrum3(inv3[...], acc[...]), 0.0)
        return carry

    lax.fori_loop(first_doc + 1, last_doc + 1, inner, 0)


def mlp_kernel(packed, meta, tokens, cot, conv, carried, gate_out, fbias, w_out, b_out, gain, shift,
               up, up_bias, down, down_bias, *refs):
    (output, gresid, glong, glong16, ggate, smalls), refs = refs[:6], refs[6:]
    (own, shared, e1_send, e2_send) = refs[:4]
    if packed:
        refs = refs[4:]
    else:
        actt, gpre_out, n2t_out, gatedt_out, gmix_out = refs[:5]
        refs = refs[5:]
    resid, n2, hat2, rstd2, oacc, gacc, ubias, ubias_grad, turned, rows_held = refs
    j = pl.program_id(0)
    block, width = tokens.shape
    ff = up.shape[1]
    core, x, y = meta[1], meta[3] % 2, meta[3] // 2
    chips = packed
    if packed:
        share, big = width // (2 * chips), ff // 2
        half = big // 2
        slot = chips * (half + share)

    @pl.when(j == 0)
    def _():
        ubias[...] = row_of(up_bias)
        long_out = conv[...] + row_of(fbias) * carried[...].astype(F32)
        gated = long_out * gate_out[...]
        gated_t = gated.T.astype(BF16)
        r = tokens[...].astype(F32) + dot(gated.astype(BF16), w_out[...]) + row_of(b_out)
        resid[...] = r
        hat, rstd = normalise(r)
        hat2[...] = hat
        rstd2[...] = rstd
        normed = hat * row_of(gain) + row_of(shift)
        n2[...] = normed.astype(BF16)
        oacc[...] = jnp.zeros_like(oacc)
        gacc[...] = jnp.zeros_like(gacc)
        if packed:
            turned[...] = gated_t
            later = chips * half
            for dest, p, first in ((own, 0, later), (shared, 1, later), (e1_send, 0, later),
                                   (e1_send, 1, slot + later)):
                write_side(dest, first, turned, chips, share, core ^ p)
            turned[...] = normed.T.astype(BF16)
            after1 = slot + width // 2
            for dest, p, first in ((own, 0, slot), (shared, 1, after1), (e2_send, 0, 0),
                                   (e2_send, 1, chips * share)):
                write_side(dest, first, turned, chips, share, core ^ p)
        else:
            gatedt_out[...] = gated_t
            n2t_out[...] = normed.T.astype(BF16)

    bias = ubias[:, pl.ds(pl.multiple_of(j * ff, 128), ff)]
    pre = dot(n2[...], up[...]) + bias
    sq = pre * pre
    th = jnp.tanh(GELU_C * (pre * (1.0 + GELU_A * sq)))
    act = 0.5 * pre * (1.0 + th)
    slope = 0.5 * (1.0 + th) + 0.5 * pre * (1.0 - th * th) * (
        GELU_C * (1.0 + 3.0 * GELU_A * sq)
    )
    if packed:
        turned[...] = act.T.astype(BF16)
        for dest, p, side, first in ((own, 0, x, 0), (shared, 1, x, 0), (e1_send, 0, 1 - x, 0),
                                     (e1_send, 1, 1 - x, slot)):
            dest[pl.ds(pl.multiple_of(first + j * half, 16), half), :] = turned[
                pl.ds(pl.multiple_of((core ^ p) * big + side * half, 16), half), :
            ]
    else:
        actt[...] = act.T.astype(BF16)
    oacc[...] += dot(act.astype(BF16), down[...])
    gpre = (dot_t(cot[...], down[...]) * slope).astype(BF16)
    if packed:
        rows_held[...] = gpre
        per = chips // 2
        for t in range(ff // 128):
            at = ((j % per) * (ff // 128) + t) * block
            tile = gpre[:, t * 128 : (t + 1) * 128]

            @pl.when(j // per == y)
            def _():
                first = slot + width // 2 + chips * share
                shared[pl.ds(pl.multiple_of(first + at, 16), block), :] = tile

            @pl.when(j // per != y)
            def _():
                e2_send[pl.ds(pl.multiple_of(width + at, 16), block), :] = tile
    else:
        gpre_out[...] = gpre
    ubias_grad[:, pl.ds(pl.multiple_of(j * ff, 128), ff)] = jnp.sum(
        gpre.astype(F32), axis=0, keepdims=True
    )
    gacc[...] += dot_t(gpre, up[...])

    @pl.when(j == pl.num_programs(0) - 1)
    def _():
        output[...] = (resid[...] + oacc[...] + row_of(down_bias)).astype(BF16)
        top = cot[...].astype(F32)
        gn = gacc[...]
        hat = hat2[...]
        q = gn * row_of(gain)
        mean_q = jnp.mean(q, axis=-1, keepdims=True)
        mean_qh = jnp.mean(q * hat, axis=-1, keepdims=True)
        gr = top + (q - mean_q - hat * mean_qh) * rstd2[...]
        gresid[...] = gr
        gm = gr.astype(BF16)
        if packed:
            rows_held[...] = gm
            write_tiles(shared, slot, rows_held, x * (width // 2), width // 256)
            write_tiles(e1_send, 2 * slot, rows_held, (1 - x) * (width // 2), width // 256)
        else:
            gmix_out[...] = gm
        gg = dot_t(gm, w_out[...])
        c = carried[...].astype(F32)
        long_out = conv[...] + row_of(fbias) * c
        gl = gg * gate_out[...]
        glong[...] = gl
        glong16[...] = gl.astype(BF16)
        ggate[...] = gg * long_out
        rows = [
            jnp.sum(top, axis=0, keepdims=True),
            jnp.sum(gn * hat, axis=0, keepdims=True),
            jnp.sum(gn, axis=0, keepdims=True),
            jnp.sum(gm.astype(F32), axis=0, keepdims=True),
            jnp.sum(gl * c, axis=0, keepdims=True),
        ]
        lanes = smalls.shape[1]
        for i, made in enumerate(rows):
            smalls[i : i + 1, :width] = made
            smalls[i : i + 1, width:] = jnp.zeros((1, lanes - width), F32)
        for i in range(ubias_grad.shape[1] // lanes):
            smalls[len(rows) + i : len(rows) + i + 1, :] = ubias_grad[:, i * lanes : (i + 1) * lanes]


def conv_back_kernel(ndocs, length, nparts, first, meta, *refs):
    parts, refs = refs[:nparts], refs[nparts:]
    (own_grad, lags, invt2, leftt3, fbias, gate_in, values, ggate, short_gate, short_in,
     short_values, for_in, for_values, rim, acc) = refs[:15]
    grads = parts[0]
    if nparts > 1:
        grads = refs[15]
        fill(meta, parts, first, grads)
    block = grads.shape[1]
    me = meta[0]
    base = me * block
    _, ids = doc_column(meta, ndocs, base, block)
    first_doc = doc_at(meta, ndocs, base)
    last_doc = doc_at(meta, ndocs, base + block - 1)
    last_block = (doc_end(meta, ndocs, base + block - 1, length) - 1) // block
    own = grads[me]
    spec = spectrum2(invt2[...], masked(own, ids == last_doc))
    set_spec(acc, times_back(lags[0], spec))

    def cross(t, carry):
        _, far = doc_column(meta, ndocs, t * block, block)
        spec = spectrum2(invt2[...], masked(grads[t], far == last_doc))
        add_spec(acc, times_back(lags[t - me], spec))
        return carry

    lax.fori_loop(me + 1, last_block + 1, cross, 0)
    for_in[...] = jnp.where(ids == last_doc, spectrum3(leftt3[...], acc[...]), 0.0)

    def inner(d, carry):
        spec = spectrum2(invt2[...], masked(own, ids == d))
        set_spec(acc, times_back(lags[0], spec))
        for_in[...] += jnp.where(ids == d, spectrum3(leftt3[...], acc[...]), 0.0)
        return carry

    lax.fori_loop(first_doc, last_doc, inner, 0)
    total = for_in[...] + row_of(fbias) * own_grad[...]
    for_in[...] = total * values[...]
    for_values[...] = total * gate_in[...]
    reach = short_gate.shape[0] - 1
    for third, (grad, taps) in enumerate(
        ((ggate, short_gate), (for_in, short_in), (for_values, short_values))
    ):
        rows = [jnp.zeros((8 - reach, grad.shape[1]), F32)]
        for p in range(reach):
            made = jnp.zeros((1, grad.shape[1]), F32)
            for k in range(1, reach + 1):
                t = p - reach + k
                if 0 <= t < reach:
                    same = doc_at(meta, ndocs, base - reach + p) == doc_at(meta, ndocs, base + t)
                    keep = (same & (base > 0)).astype(F32)
                    made = made + taps[k : k + 1, :].astype(F32) * grad[t : t + 1, :] * keep
            rows.append(made)
        rim[third] = jnp.concatenate(rows, axis=0)


def taps_grad_kernel(ndocs, nparts, first, meta, *refs):
    parts, refs = refs[:nparts], refs[nparts:]
    own_grad, left2, invt2, leftt3, out, win, gspec = refs[:7]
    signal = parts[0]
    if nparts > 1:
        signal = refs[7]
        fill(meta, parts, first, signal)
    blocks, block = signal.shape[0], signal.shape[1]
    me = meta[0]
    base = me * block
    start = doc_start(meta, ndocs, base)
    low_block = start // block
    _, ids = doc_column(meta, ndocs, base, block)
    first_doc = doc_at(meta, ndocs, base)
    last_doc = doc_at(meta, ndocs, base + block - 1)
    sign = 1.0 - 2.0 * (lax.broadcasted_iota(jnp.int32, (2 * block, 1), 0) % 2).astype(F32)
    own = signal[me]
    grad = own_grad[...]
    out[...] = jnp.zeros_like(out)
    win[me - low_block + 1] = jnp.zeros(win.shape[1:], F32)
    gspec[...] = spectrum2(invt2[...], masked(grad, ids == first_doc))
    spec = spectrum2(left2[...], masked(own, ids == first_doc))
    set_spec(win.at[0], times_back(spec, gspec[...]))

    def inner(d, carry):
        spec = spectrum2(left2[...], masked(own, ids == d))
        back = spectrum2(invt2[...], masked(grad, ids == d))
        add_spec(win.at[0], times_back(spec, back))
        return carry

    lax.fori_loop(first_doc + 1, last_doc + 1, inner, 0)

    def cross(s, carry):
        position = s * block + lax.broadcasted_iota(jnp.int32, (block, 1), 0)
        spec = spectrum2(left2[...], masked(signal[s], position >= start))
        set_spec(win.at[me - s], times_back(spec, gspec[...]))
        return carry

    lax.fori_loop(low_block, me, cross, 0)

    def emit(k, carry):
        out[k] = spectrum3(leftt3[...], win[k + 1] + sign * win[k])
        return carry

    lax.fori_loop(0, me - low_block + 1, emit, 0)


def short_back_kernel(ndocs, packed, meta, ggate, for_in, for_values, rim, proj, taps,
                      gproj_ref, smalls, *sends):
    block, width = ggate.shape
    taps_n = taps.shape[0]
    base = meta[0] * block
    position, ids = doc_column(meta, ndocs, base, block)
    masks = []
    for k in range(taps_n):
        _, back = doc_column(meta, ndocs, base - k, block)
        masks.append(((back == ids) & (position >= k)).astype(F32))
    row = lax.broadcasted_iota(jnp.int32, (block, 1), 0)
    ahead = []
    for k in range(1, taps_n):
        _, later = doc_column(meta, ndocs, base + k, block)
        ahead.append(((later == ids) & (row < block - k)).astype(F32))
    bias_rows, weight_rows, short_rows = [], [], []
    for third, grad_ref in enumerate((ggate, for_in, for_values)):
        cols = slice(third * width, (third + 1) * width)
        grad = grad_ref[...]
        total = taps[0:1, cols].astype(F32) * grad
        weights = [jnp.sum(grad * proj[pl.ds(RIM, block), cols], axis=0, keepdims=True)]
        for k in range(1, taps_n):
            moved = pltpu.roll(grad, block - k, 0) * ahead[k - 1]
            total = total + taps[k : k + 1, cols].astype(F32) * moved
            weights.append(
                jnp.sum(grad * masks[k] * proj[pl.ds(RIM - k, block), cols], axis=0, keepdims=True)
            )
        tail = jnp.concatenate([jnp.zeros((block - 8, width), F32), rim[third]], axis=0)
        low = (total + tail).astype(BF16)
        gproj_ref[:, cols] = low
        bias_rows.append(jnp.sum(low.astype(F32), axis=0, keepdims=True))
        short_rows.append(jnp.sum(grad, axis=0, keepdims=True))
        weight_rows.append(weights)
    rows = bias_rows + [weight_rows[t][k] for k in range(taps_n) for t in range(3)] + short_rows
    pad = smalls.shape[0] - len(rows)
    smalls[...] = jnp.concatenate(rows + [jnp.zeros((pad, width), F32)], axis=0)
    if packed:
        x = meta[3] % 2
        half = 3 * width // 2
        for dest, side in zip(sends, (x, 1 - x)):
            write_tiles(dest, 0, gproj_ref, side * half, half // 128)


def tail_kernel(meta, gproj, weight, tokens, gain, gresid, others, out, smalls):
    gn = dot_t(gproj[...], weight[...])
    hat, rstd = normalise(tokens[...].astype(F32))
    q = gn * row_of(gain)
    mean_q = jnp.mean(q, axis=-1, keepdims=True)
    mean_qh = jnp.mean(q * hat, axis=-1, keepdims=True)
    out[...] = gresid[...] + (q - mean_q - hat * mean_qh) * rstd
    rows = [others[i : i + 1, :] for i in range(others.shape[0] - 2)]
    rows += [jnp.sum(gn * hat, axis=0, keepdims=True), jnp.sum(gn, axis=0, keepdims=True)]
    if smalls.shape[1] == others.shape[1]:
        smalls[...] = jnp.concatenate(rows, axis=0)
        return
    smalls[...] = jnp.zeros_like(smalls)
    half = others.shape[1] // 2
    for k, (r, h) in enumerate((r, h) for r in LATE_ROWS for h in range(2)):
        smalls[k // 3 : k // 3 + 1, k % 3 * half : (k % 3 + 1) * half] = rows[r][:, h * half : (h + 1) * half]


def filter_taps(first, first_bias, second, second_bias, third, third_bias, last, sine_freq, length):
    lags = jnp.arange(length)
    bands = (first.shape[0] - 1) // 2
    moment = lags.astype(F32) / (length - 1)
    band_freq = jnp.linspace(0.0001, bands - 1, bands, dtype=F32)
    phase = 2.0 * math.pi / length * lags.astype(F32)
    angles = phase[:, None] * band_freq[None, :]
    features = jnp.concatenate([moment[:, None], jnp.cos(angles), -jnp.sin(angles)], axis=1)
    hidden = jnp.sin(sine_freq * (jnp.dot(features, first, precision=HIGHEST) + first_bias))
    hidden = jnp.sin(sine_freq * (jnp.dot(hidden, second, precision=HIGHEST) + second_bias))
    hidden = jnp.sin(sine_freq * (jnp.dot(hidden, third, precision=HIGHEST) + third_bias))
    rates = jnp.linspace(MIN_DECAY, MAX_DECAY, last.shape[1], dtype=F32)
    window = jnp.exp(-moment[:, None] * rates[None, :])
    return jnp.dot(hidden, last, precision=HIGHEST) * window


def sine_pair(values):
    turns = jnp.floor(values * (2.0 / math.pi) + 0.5)
    rest = values - turns * 1.5703125
    rest = rest - turns * 4.837512969970703125e-4
    rest = rest - turns * 7.549789948768648e-8
    sq = rest * rest
    s = ((-1.9515295891e-4 * sq + 8.3321608736e-3) * sq - 1.6666654611e-1) * sq * rest + rest
    c = ((2.443315711809948e-5 * sq - 1.388731625493765e-3) * sq + 4.166664568298827e-2) * sq * sq
    c = c - 0.5 * sq + 1.0
    quarter = turns.astype(jnp.int32)
    odd = (quarter & 1) == 1
    half = (quarter & 2) == 2
    first = jnp.where(odd, c, s)
    second = jnp.where(odd, s, c)
    return jnp.where(half, -first, first), jnp.where(half ^ odd, -second, second)


def exact_dot(weights, values):
    high = values.astype(BF16)
    rest = values - high.astype(F32)
    middle = rest.astype(BF16)
    low = (rest - middle.astype(F32)).astype(BF16)
    return dot(weights, high) + (dot(weights, middle) + dot(weights, low))


def feature_table(length, bands):
    lags = np.arange(length).astype(np.float32)
    moment = lags / np.float32(length - 1)
    freq = np.linspace(0.0001, bands - 1, bands).astype(np.float32)
    phase = np.float32(2.0 * math.pi / length) * lags
    angles = (phase[:, None] * freq[None, :]).astype(np.float64)
    table = np.concatenate(
        [moment[:, None].astype(np.float64), np.cos(angles), -np.sin(angles)], axis=1
    )
    return np.pad(table.astype(np.float32), ((0, 0), (0, -table.shape[1] % 8))).T


def decay_window(width, length):
    moment = lax.broadcasted_iota(jnp.int32, (length, 1), 0).astype(F32) / (length - 1)
    step = (MAX_DECAY - MIN_DECAY) / (width - 1)
    rates = MIN_DECAY + step * lax.broadcasted_iota(jnp.int32, (1, width), 1).astype(F32)
    return jnp.exp(-moment * rates)


def turned_column(ref):
    return jnp.broadcast_to(row_of(ref), (8, ref.shape[0])).T[:, :1]


def filter_kernel(meta, table, first, b1, second, b2, third, b3, last, freq, left3,
                  lags, window, act, slope, pre, a3):
    blocks, period, width = lags.shape
    block = period // 2
    length = blocks * block
    fwidth = freq.shape[0]
    scale = turned_column(freq)
    hidden = table[...]
    pad = table.shape[0] - first.shape[0]
    firsts = jnp.concatenate([first[...].astype(F32), jnp.zeros((pad, fwidth), F32)], axis=0)
    for i, (weight, bias) in enumerate(
        ((firsts, b1), (second[...].astype(F32), b2), (third[...].astype(F32), b3))
    ):
        u = exact_dot(weight.T.astype(BF16), hidden) + turned_column(bias)
        hidden, cosine = sine_pair(scale * u)
        rows = slice(i * fwidth, (i + 1) * fwidth)
        act[rows, :] = hidden
        slope[rows, :] = cosine
        pre[rows, :] = u
    a3[...] = hidden.T
    window[...] = decay_window(width, length)
    sign = 1.0 - 2.0 * (lax.broadcasted_iota(jnp.int32, (period, 1), 0) % 2).astype(F32)
    before = None
    for j in range(blocks):
        part = a3[j * block : (j + 1) * block, :]
        high = part.astype(BF16)
        rest = part - high.astype(F32)
        middle = rest.astype(BF16)
        low = (rest - middle.astype(F32)).astype(BF16)
        lhs = jnp.concatenate([high, middle, low], axis=1)
        rhs = jnp.concatenate([last[...]] * 3, axis=0)
        taps = dot(lhs, rhs) * window[j * block : (j + 1) * block, :]
        spec = spectrum3(left3[...], taps)
        lags[j] = sign * spec if before is None else before + sign * spec
        before = spec


def filter_back_kernel(meta, grads, window, act, slope, pre, table, first, second, third, last,
                       freq, others, mine, send, packed):
    blocks, block, width = grads.shape
    length = blocks * block
    fwidth = freq.shape[0]
    scale = turned_column(freq)
    core = meta[1]
    weighted = grads[...].reshape(length, width) * window[...]
    wh, wl = high_low(weighted)
    ah, al = high_low(act[2 * fwidth :, :])
    packed[...] = jnp.zeros_like(packed)
    made = dot(ah, wh) + (dot(ah, wl) + dot(al, wh))
    place = 0
    for t in range(width // 128):
        packed[place : place + fwidth, :] = made[:, t * 128 : (t + 1) * 128]
        place += fwidth
    for i in range(others.shape[0]):
        count = others.shape[1] // 128 if i >= 5 else width // 128
        for t in range(count):
            row = OTHER_ROWS + (i * 6 + t if i < 5 else 30 + (i - 5) * count + t)
            packed[row : row + 1, :] = others[i : i + 1, t * 128 : (t + 1) * 128]
    back = dot_t(last[...], wh) + dot_t(last[...], wl)
    ones = jnp.ones((8, length), BF16)

    def wide_t(left, right):
        lh, ll = high_low(left)
        rh, rl = high_low(right)
        return dot_t(lh, rh) + (dot_t(lh, rl) + dot_t(ll, rh))

    def sums(values):
        high, low = high_low(values)
        return (dot_t(ones, high) + dot_t(ones, low))[:1]

    freq_total = jnp.zeros((1, fwidth), F32)
    for i, weight in ((2, third), (1, second), (0, first)):
        rows = slice(i * fwidth, (i + 1) * fwidth)
        step = back * slope[rows, :]
        freq_total = freq_total + sums(step * pre[rows, :])
        step = step * scale
        below = act[(i - 1) * fwidth : i * fwidth, :] if i else table[...]
        made = wide_t(below, step)
        at, lanes = ((place + fwidth, 0), (place, fwidth), (place, 0))[i]
        packed[at : at + made.shape[0], lanes : lanes + fwidth] = made
        packed[place + fwidth + i : place + fwidth + i + 1, fwidth:] = sums(step)
        if i:
            high, low = high_low(step)
            back = dot(weight[...], high) + dot(weight[...], low)
    packed[place + fwidth + 3 : place + fwidth + 4, fwidth:] = freq_total
    size = SMALL_BLOCK
    for z in range(mine.shape[0] // size):
        out = slice(z * size, (z + 1) * size)
        mine[out, :] = packed[pl.ds(pl.multiple_of((2 * z + core) * size, 8), size), :]
        send[out, :] = packed[pl.ds(pl.multiple_of((2 * z + 1 - core) * size, 8), size), :]


def shift(block, axis, distance):
    devices = range(lax.axis_size(axis))
    return lax.ppermute(block, axis, [(i - distance, i) for i in devices if i - distance in devices])


def swap(block, axis, mask):
    return lax.ppermute(block, axis, [(i, i ^ mask) for i in range(lax.axis_size(axis))])


def collect_kernel(spans, meta, *refs):
    out, place = refs[-1], 0
    for ref, span in zip(refs[:-1], spans):
        if span is None:
            write_tiles(out, place, ref, 0, ref.shape[1] // 128)
            place += ref.shape[0] * (ref.shape[1] // 128)
        else:
            out[pl.ds(place, span[1] - span[0]), :] = ref[pl.ds(span[0], span[1] - span[0]), :]
            place += span[1] - span[0]


def collected(meta, pieces, after=()):
    rows = sum(v.shape[0] * v.shape[1] // 128 if span is None else span[1] - span[0] for v, span in pieces)
    (out,) = single(
        partial(collect_kernel, [span for _, span in pieces]), "collect", 0.6,
        [jax.ShapeDtypeStruct((rows, 128), BF16)], meta, [v for v, _ in pieces], after,
    )
    return out


def near_blocks(block, blocks):
    got = {k: swap(block, "seq", 2 * k) for k in (2, 3, 1)}
    return [block] + [got[k] for k in range(1, blocks // 2)]


def joined_left(sources, rows):
    return jnp.concatenate([ref[pl.ds(first, rows), :] for ref, first in sources], axis=1)


def joined_right(sources, block, start, count):
    return jnp.concatenate(
        [
            jnp.concatenate(
                [ref[pl.ds(first + t * block, block), :] for t in range(start, start + count)], axis=1
            )
            for ref, first in sources
        ],
        axis=0,
    )


def pick(flag, keep, send, store):
    @pl.when(flag)
    def _():
        store(keep)

    @pl.when(jnp.logical_not(flag))
    def _():
        store(send)


def early_sources(early, early_got, early_sib, width, columns):
    half = width // 2
    if columns:
        return ((early, width), (early_sib, half), (early_got, width), (early_sib, 2 * width))
    return ((early, 0), (early_sib, 0), (early_got, 0), (early_sib, half + width))


def down_out_kernel(chips, meta, own, shared, shared_sib, got, got_sib, early, early_got, early_sib,
                    keep, send):
    block = own.shape[1]
    share = keep.shape[1]
    width = early.shape[0] // 2
    half = 2 * share
    slot = chips * (half + share)
    y, chip = meta[3] // 2, meta[2]
    sources = (own, shared_sib, got, got_sib)
    made = dot(
        joined_left([(v, 0) for v in sources], chips * half),
        joined_right(early_sources(early, early_got, early_sib, width, True), block, 0, width // 128),
    ).astype(BF16)
    right = ((shared, slot), (shared_sib, slot), (got, 2 * slot), (got_sib, slot))
    out = dot(
        joined_left([(v, chips * half) for v in sources], chips * share),
        joined_right(right, block, 0, width // 256),
    ).astype(BF16)
    part = share // 2
    for side in range(2):

        def store(dest):
            for z in range(chips):
                at = z ^ chip
                first = z * half + side * share
                dest[at, :, :width] = made[first : first + share]
                rows = out[z * share + side * part : z * share + (side + 1) * part]
                dest[at, :part, width : width + 128] = rows[:, :128]
                dest[at, part:, width : width + 128] = rows[:, 128:256]
                dest[at, :part, width + 128 :] = rows[:, 256:]
                dest[at, part:, width + 128 :] = jnp.zeros((part, 128), BF16)

        pick(y == side, keep, send, store)


def up_kernel(chips, meta, own, shared, shared_sib, got, got_sib, keep, send):
    block = own.shape[1]
    share, width = keep.shape[1:]
    x, chip = meta[3] % 2, meta[2]
    rows = chips * share
    slot = 3 * rows
    first = slot + width // 2
    left = joined_left(((own, slot), (shared_sib, first), (got, 0), (got_sib, first)), rows)
    right = ((shared, first + rows), (shared_sib, first + rows), (got, 2 * rows), (got_sib, first + rows))
    for side in range(2):
        made = dot(left, joined_right(right, block, side * (width // 128), width // 128)).astype(BF16)

        def store(dest):
            for z in range(chips):
                dest[z ^ chip] = made[z * share : (z + 1) * share]

        pick(x == side, keep, send, store)


def in_kernel(chips, meta, mine, got, sib, early, early_got, early_sib, keep, send):
    block = mine.shape[1]
    part, cols = keep.shape[1:]
    width = early.shape[0] // 2
    y, chip = meta[3] // 2, meta[2]
    right = ((mine, 0), (sib, 0), (got, 0), (sib, mine.shape[0]))
    made = dot(
        joined_left(early_sources(early, early_got, early_sib, width, False), width // 2),
        joined_right(right, block, 0, cols // 128),
    ).astype(BF16)
    for side in range(2):

        def store(dest):
            for z in range(chips):
                first = (2 * z + side) * part
                dest[z ^ chip] = made[first : first + part]

        pick(y == side, keep, send, store)


def merge_kernel(pairs, kind, meta, *refs):
    ins, refs = refs[: 2 * pairs], refs[2 * pairs :]
    chips, rows = ins[0].shape[:2]
    extra, (own, *sends) = refs[:-chips], refs[-chips:]
    first = 0
    for p in range(pairs):
        keep, got = ins[2 * p : 2 * p + 2]
        cols = slice(first, first + keep.shape[2])
        first += keep.shape[2]
        own[:rows, cols] = keep[0].astype(F32) + got[0].astype(F32)
        for j, dest in enumerate(sends):
            dest[:rows, cols] = (keep[j + 1].astype(F32) + got[j + 1].astype(F32)).astype(BF16)
    if kind == "rows":
        value = (extra[0][...] + extra[1][...]).astype(BF16)
        own[rows:, :] = value.astype(F32)
        for dest in sends:
            dest[rows:, :] = value
    if kind == "tiles":
        size = SMALL_BLOCK
        for j, dest in enumerate((own, *sends)):
            take = pl.ds(pl.multiple_of((meta[2] ^ j) * size, 8), size)
            value = extra[0][take, :] + extra[1][take, :]
            dest[:size, first:] = value.astype(dest.dtype)
            dest[size:, first:] = jnp.zeros((rows - size, dest.shape[1] - first), dest.dtype)


def total_kernel(meta, own, one, two, three, out):
    out[...] = (
        (own[...] + one[...].astype(F32)) + (two[...].astype(F32) + three[...].astype(F32))
    ).astype(BF16)


def chip_sums(meta, pairs, kind, extra):
    chips, rows, _ = pairs[0].shape
    cols = sum(v.shape[2] for v in pairs[::2])
    rows += extra[0].shape[0] if kind == "rows" else 0
    cols += 128 if kind == "tiles" else 0
    sds = jax.ShapeDtypeStruct
    return single(
        partial(merge_kernel, len(pairs) // 2, kind), "merge", 1.0,
        [sds((rows, cols), F32)] + [sds((rows, cols), BF16)] * (chips - 1), meta, (*pairs, *extra),
    )


def spread_out(meta, sums, after=()):
    own, *sends = sums
    got = {j: swap(sends[j - 1], "seq", 2 * j) for j in (2, 3, 1)}
    (total,) = single(
        total_kernel, "total", 1.0, [jax.ShapeDtypeStruct(own.shape, BF16)], meta,
        [own, got[1], got[2], got[3]], after,
    )
    return [total] + [swap(total, "rows", j) for j in (1, 2, 3)]


def merge_halves_kernel(meta, keep, got, left, right, keep_out, send_out):
    rows = keep.shape[1]
    for dest, order in ((keep_out, (0, 2)), (send_out, (1, 3))):
        for i, j in enumerate(order):
            dest[i, :rows, :] = (keep[j].astype(F32) + got[j].astype(F32)).astype(dest.dtype)
            dest[i, rows:, :] = (left[...] + right[...]).astype(BF16).astype(dest.dtype)


def halve_kernel(exact, meta, keep, got, own, send):
    mine = keep[0] + got[0].astype(F32)
    own[:exact, :] = mine[:exact]
    own[exact:, :] = mine[exact:].astype(BF16).astype(F32)
    send[...] = (keep[1] + got[1].astype(F32)).astype(BF16)


def add_kernel(meta, own, got, out):
    out[...] = (own[...] + got[...].astype(F32)).astype(BF16)


def late_sums_of(meta, keep, got, left, right):
    _, rows, cols = keep.shape
    full = rows + left.shape[0]
    sds = jax.ShapeDtypeStruct
    kept, send = single(
        merge_halves_kernel, "merge_late", 1.0, [sds((2, full, cols), F32), sds((2, full, cols), BF16)],
        meta, [keep, got, left, right],
    )
    halves = single(
        partial(halve_kernel, rows), "halve", 1.0, [sds((full, cols), F32), sds((full, cols), BF16)],
        meta, [kept, swap(send, "seq", 2)],
    )
    return kept, halves


def spread_late(meta, halves):
    own, send = halves
    (total,) = single(
        add_kernel, "total_late", 1.0, [jax.ShapeDtypeStruct(own.shape, BF16)], meta,
        [own, swap(send, "seq", 4)],
    )
    return [total] + [swap(total, "rows", j) for j in (1, 2, 3)]


def small_kernel(meta, *refs):
    pieces, out = refs[:4], refs[4]
    lanes = pieces[0].shape[1] - 128
    a, b, c, d = (ref[:, lanes:].astype(F32) for ref in pieces)
    out[...] = ((a + b) + (c + d))[: out.shape[0]]


def copy_kernel(meta, *refs):
    half = len(refs) // 2
    for source, dest in zip(refs[:half], refs[half:]):
        dest[...] = source[...]


def stack_kernel(meta, *refs):
    for k, ref in enumerate(refs[:-1]):
        refs[-1][k] = ref[...]


def unpack_kernel(taps_n, fwidth, feats, first_late, meta, small, other, *refs):
    late_pieces, outs, packed, late = refs[:4], refs[4:-2], refs[-2], refs[-1]
    chips, size = small.shape[:2]
    core = meta[1]
    for k in range(chips):
        z = meta[2] ^ k
        packed[pl.ds(pl.multiple_of((2 * z + core) * size, 8), size), :] = small[k]
        packed[pl.ds(pl.multiple_of((2 * z + 1 - core) * size, 8), size), :] = other[k]
    (gain1, shift1, in_bias, short_weight, short_bias, f1, f1b, f2, f2b, f3, f3b, flast, freq,
     fbias, obias, gain2, shift2, ubias, dbias) = outs
    width = gain1.shape[0]
    take = pl.ds(first_late, late_pieces[0].shape[0] - first_late)
    a, b, c, d = (ref[take, :].astype(F32) for ref in late_pieces)
    late[...] = (a + b) + (c + d)
    place = 0
    for t in range(width // 128):
        flast[:, t * 128 : (t + 1) * 128] = packed[place : place + fwidth, :]
        place += fwidth
    f3[...] = packed[place : place + fwidth, :fwidth]
    f2[...] = packed[place : place + fwidth, fwidth:]
    place += fwidth
    f1[...] = packed[place : place + feats, :fwidth]
    for i, ref in enumerate((f1b, f2b, f3b, freq)):
        ref[...] = packed[place + i : place + i + 1, fwidth:].reshape(-1)

    def line(first, count):
        return jnp.concatenate(
            [packed[OTHER_ROWS + first + t : OTHER_ROWS + first + t + 1, :] for t in range(count)], axis=1
        ).reshape(-1)

    for i, ref in enumerate((dbias, gain2, shift2, obias, fbias)):
        ref[...] = line(6 * i, 6)
    ubias[...] = line(30, ubias.shape[0] // 128)
    side = late.shape[1] // 3

    def row(r):
        return [
            late[k // 3 : k // 3 + 1, k % 3 * side : (k % 3 + 1) * side] for k in (2 * r, 2 * r + 1)
        ]

    def wide(first):
        return jnp.concatenate(row(first) + row(first + 1) + row(first + 2), axis=1)

    in_bias[...] = wide(0).reshape(-1)
    for k in range(taps_n):
        short_weight[k : k + 1, :] = wide(3 + 3 * k)
    short_bias[...] = wide(3 + 3 * taps_n).reshape(-1)
    count = 6 + 3 * taps_n
    gain1[...] = jnp.concatenate(row(count), axis=1).reshape(-1)
    shift1[...] = jnp.concatenate(row(count + 1), axis=1).reshape(-1)


def place_early_kernel(meta, *refs):
    pieces, (down, out, up) = refs[:4], refs[4:]
    row = meta[3]
    share, width = out.shape
    part = share // 2
    for j, piece in enumerate(pieces):
        x, y = (row ^ j) % 2, (row ^ j) // 2
        down[pl.ds(pl.multiple_of((2 * x + y) * share, 8), share), :] = piece[:share, :width].astype(F32)
        tiles = (
            piece[:part, width : width + 128],
            piece[part:share, width : width + 128],
            piece[:part, width + 128 : width + 256],
        )
        for t, tile in enumerate(tiles):
            cols = pl.ds(pl.multiple_of(x * (width // 2) + t * 128, 128), 128)
            out[pl.ds(pl.multiple_of(y * part, 8), part), cols] = tile.astype(F32)
        cols = pl.ds(pl.multiple_of((2 * y + x) * width, 128), width)
        up[:, cols] = piece[:share, width + 256 : 2 * width + 256].astype(F32)


def place_in_kernel(meta, *refs):
    pieces, full = refs[:4], refs[4]
    part, cols = full.shape[0] // 2, pieces[0].shape[1]
    for j, piece in enumerate(pieces):
        x, y = (meta[3] ^ j) % 2, (meta[3] ^ j) // 2
        full[pl.ds(pl.multiple_of(y * part, 8), part), pl.ds(pl.multiple_of(x * cols, 128), cols)] = (
            piece[:part, :].astype(F32)
        )


def local(
    tokens, doc_starts, norm1_gain, norm1_bias, in_weight, in_bias, short_weight, short_bias,
    filter_first, filter_first_bias, filter_second, filter_second_bias, filter_third,
    filter_third_bias, filter_last, sine_freq, filter_bias, out_weight, out_bias, norm2_gain,
    norm2_bias, up_weight, up_bias, down_weight, down_bias, cotangent,
):
    block, width = tokens.shape[1:]
    blocks = lax.axis_size("seq")
    chips = blocks // 2
    nrows = lax.axis_size("rows")
    length = block * blocks
    hidden = up_weight.shape[1]
    index = lax.axis_index("seq")
    row = lax.axis_index("rows")
    starts = doc_starts[0]
    ndocs = starts.shape[0]
    taps_n = short_weight.shape[0]
    ff = width
    fsteps = hidden // ff
    share = width // blocks
    fits = blocks == 8 and nrows == 4 and fsteps == chips and share % 32 == 0 and block == 128
    packed = chips if fits and width == 768 else 0
    meta = jnp.concatenate(
        [jnp.stack([index, index % 2, index // 2, row]).astype(jnp.int32), starts]
    )
    tables = {k: jnp.asarray(v) for k, v in block_tables(block).items()}
    chunk = width if blocks <= 8 else 128
    steps = width // chunk
    tok, cot = tokens[0], cotangent[0]
    mat = whole((block, width))
    vec = whole((width,))
    sds = jax.ShapeDtypeStruct

    rim = shift(tok[block - RIM :], "seq", 1)
    proj, early, mixed, carried = single(
        partial(front_kernel, ndocs, packed), "front", 3.0,
        [sds((block + RIM, 3 * width), F32), sds((2 * width if packed else width, block), BF16),
         sds((block, 3 * width), F32), sds((block, width), BF16)],
        meta,
        [tok, rim, cot, norm1_gain, norm1_bias, in_weight, in_bias, short_weight, short_bias],
        scratch=[pltpu.VMEM((width, block), BF16)], limit=58 * 1024 * 1024,
    )

    early_got = swap(early, "rows", 1) if packed else None

    by_chunk = lambda lead: pl.BlockSpec(lead + (chunk,), lambda i: (0,) * len(lead) + (i,))
    fwidth, feats = sine_freq.shape[0], filter_first.shape[0]
    if packed:
        table = jnp.asarray(feature_table(length, (feats - 1) // 2))
        lags, window, *net = single(
            filter_kernel, "filter", 8.0,
            [sds((blocks, 2 * block, width), F32), sds((length, width), F32)]
            + [sds((3 * fwidth, length), F32)] * 3,
            meta,
            [table, filter_first, filter_first_bias, filter_second, filter_second_bias, filter_third,
             filter_third_bias, filter_last, sine_freq, tables["left3"]],
            after=[carried], scratch=[pltpu.VMEM((length, fwidth), F32)],
        )
    else:
        filter_params = tuple(
            v.astype(F32)
            for v in (filter_first, filter_first_bias, filter_second, filter_second_bias, filter_third,
                      filter_third_bias, filter_last, sine_freq)
        )
        taps, taps_pull = jax.vjp(partial(filter_taps, length=length), *filter_params)
        lags = pl.pallas_call(
            lag_kernel,
            grid=(steps,),
            out_shape=sds((blocks, 2 * block, width), F32),
            in_specs=[by_chunk((blocks, block)), whole(tables["left3"].shape)],
            out_specs=by_chunk((blocks, 2 * block)),
            compiler_params=params(),
            name="lags",
        )(taps.reshape(blocks, block, width), tables["left3"])

    if packed:
        near = near_blocks(carried, blocks)
        span = (width // 2, 2 * width)
        early_sib = swap(
            collected(
                meta, [(early, span), (early_got, span)] + [(v, None) for v in near], [lags]
            ), "seq", 1,
        )
        signal, signal_row = near + [early_sib], 3 * width
        nparts = len(signal)
        part_specs = [whole(v.shape) for v in signal]
        held = [pltpu.VMEM((blocks, block, chunk), BF16)]
    else:
        signal, signal_row = [lax.all_gather(carried, "seq", axis=0, tiled=False)], 0
        nparts, part_specs, held = 1, [by_chunk((blocks, block))], []
    spec_scratch = pltpu.VMEM((2 * block, chunk), F32)
    conv = pl.pallas_call(
        partial(conv_kernel, ndocs, nparts, signal_row),
        grid=(steps,),
        out_shape=sds((block, width), F32),
        in_specs=[smem()] + part_specs + [by_chunk((blocks, 2 * block)),
                  whole(tables["left2"].shape), whole(tables["inv3"].shape)],
        out_specs=by_chunk((block,)),
        scratch_shapes=[spec_scratch] + held,
        compiler_params=params(),
        cost_estimate=cost(3.0),
        name="conv",
    )(meta, *signal, lags, tables["left2"], tables["inv3"])

    if packed:
        left1, right1, left2, right2 = chips * 3 * share, width // 2, width // 2, hidden // 2
        row_counts = (
            left1 + left2, left1 + right1 + left2 + right2, 2 * left1 + right1, 2 * left2 + right2
        )
        extra = tuple(sds((n, block), BF16) for n in row_counts)
        extra_specs = tuple(whole((n, block)) for n in row_counts)
    else:
        extra = (sds((hidden, block), BF16), sds((block, hidden), BF16), sds((width, block), BF16),
                 sds((width, block), BF16), sds((block, width), BF16))
        extra_specs = (pl.BlockSpec((ff, block), lambda i: (i, 0)),
                       pl.BlockSpec((block, ff), lambda i: (0, i)),
                       whole((width, block)), whole((width, block)), mat)
    lanes = hidden // 3
    output, gresid, glong, glong16, ggate, smalls_mlp, *acts = pl.pallas_call(
        partial(mlp_kernel, packed),
        grid=(fsteps,),
        out_shape=(
            sds((block, width), BF16), sds((block, width), F32),
            sds((block, width), F32), sds((block, width), BF16), sds((block, width), F32),
            sds((8, lanes), F32),
        ) + extra,
        in_specs=[
            smem(), mat, mat, mat, mat, mat, vec, whole((width, width)), vec, vec, vec,
            pl.BlockSpec((width, ff), lambda i: (0, i)), whole((hidden,)),
            pl.BlockSpec((ff, width), lambda i: (i, 0)), vec,
        ],
        out_specs=(mat, mat, mat, mat, mat, whole((8, lanes))) + extra_specs,
        scratch_shapes=[
            pltpu.VMEM((block, width), F32), pltpu.VMEM((block, width), BF16),
            pltpu.VMEM((block, width), F32), pltpu.VMEM((block, 1), F32),
            pltpu.VMEM((block, width), F32), pltpu.VMEM((block, width), F32),
            pltpu.VMEM((1, hidden), F32), pltpu.VMEM((1, hidden), F32),
            pltpu.VMEM((width, block), BF16), pltpu.VMEM((block, width), BF16),
        ],
        compiler_params=params(),
        cost_estimate=cost(10.0),
        name="mlp",
    )(meta, tok, cot, conv, carried, mixed, filter_bias, out_weight, out_bias, norm2_gain,
      norm2_bias, up_weight, up_bias, down_weight, down_bias)

    taps_grad = pl.pallas_call(
        partial(taps_grad_kernel, ndocs, nparts, signal_row),
        grid=(steps,),
        out_shape=sds((blocks, block, width), F32),
        in_specs=[smem()] + part_specs + [
            by_chunk((block,)), whole(tables["left2"].shape), whole(tables["invt2"].shape),
            whole(tables["leftt3"].shape)],
        out_specs=by_chunk((blocks, block)),
        scratch_shapes=[pltpu.VMEM((blocks + 1, 2 * block, chunk), F32), spec_scratch] + held,
        compiler_params=params(),
        cost_estimate=cost(4.0),
        name="taps_grad",
    )(meta, *signal, glong, tables["left2"], tables["invt2"], tables["leftt3"])
    if packed:
        own, shared, e1_send, e2_send = acts
        got1, got2 = swap(e1_send, "rows", 1), swap(e2_send, "rows", 2)
        near = near_blocks(glong16, blocks)
        shared_sib = swap(shared, "seq", 1)
        near_all = collected(meta, [(v, None) for v in near])
        grads, grads_row = near + [swap(near_all, "seq", 1)], 0
        got_sib = swap(
            collected(
                meta, [(got1, (left1, 2 * left1 + right1)), (got2, (left2, 2 * left2 + right2))],
                [near_all],
            ), "seq", 1,
        )
        grad_specs = [whole(v.shape) for v in grads]
        half_rows, small_cols = chips * SMALL_BLOCK, 128
        mine, send = single(
            filter_back_kernel, "filter_back", 5.0, [sds((half_rows, small_cols), F32)] * 2, meta,
            [taps_grad, window, *net, table, filter_first, filter_second, filter_third, filter_last,
             sine_freq, smalls_mlp],
            after=[near_all], scratch=[pltpu.VMEM((2 * half_rows, small_cols), F32)],
        )
    else:
        grads, grads_row = [lax.all_gather(glong16, "seq", axis=0, tiled=False)], 0
        grad_specs = part_specs
        filter_grads = taps_pull(taps_grad.reshape(length, width))

    tied = ()
    third = lambda n: pl.BlockSpec((block, chunk), lambda i: (0, n * steps + i))
    tap_third = lambda n: pl.BlockSpec((taps_n, chunk), lambda i: (0, n * steps + i))
    for_in, for_values, rim_out = pl.pallas_call(
        lambda *refs: conv_back_kernel(
            ndocs, length, nparts, grads_row, *refs[: nparts + 12], *refs[nparts + 12 + len(tied) :]
        ),
        grid=(steps,),
        out_shape=(sds((block, width), F32), sds((block, width), F32), sds((3, 8, width), F32)),
        in_specs=[smem()] + grad_specs + [
            by_chunk((block,)), by_chunk((blocks, 2 * block)), whole(tables["invt2"].shape),
            whole(tables["leftt3"].shape), vec if steps == 1 else by_chunk((1,)), third(1), third(2),
            by_chunk((block,)), tap_third(0), tap_third(1), tap_third(2)]
        + [pl.BlockSpec(memory_space=pl.ANY)] * len(tied),
        out_specs=(by_chunk((block,)), by_chunk((block,)), by_chunk((3, 8))),
        scratch_shapes=[spec_scratch] + held,
        compiler_params=params(),
        cost_estimate=cost(4.0),
        name="conv_back",
    )(meta, *grads, glong, lags, tables["invt2"], tables["leftt3"],
      filter_bias if steps == 1 else filter_bias.reshape(1, -1),
      mixed, mixed, ggate, short_weight, short_weight, short_weight, *tied)
    rim_back = shift(rim_out, "seq", -1)
    if packed:
        def partials(kernel, name, piece, arrays, after=()):
            return single(
                partial(kernel, chips), name, 3.0, [sds((chips,) + piece, BF16)] * 2, meta, arrays, after
            )

        parts2 = partials(up_kernel, "up_grad", (share, width), (own, shared, shared_sib, got2, got_sib), [rim_out])
        parts1 = partials(
            down_out_kernel, "down_out", (share, width + 256),
            (own, shared, shared_sib, got1, got_sib, early, early_got, early_sib), [rim_out],
        )
        tied = (parts1[0], parts2[0])
        keep1, send1 = parts1
        keep2, send2 = parts2
        pairs = [keep1, swap(send1, "rows", 2), keep2, swap(send2, "rows", 1)]
        first_sums = chip_sums(meta, pairs, "tiles", (mine, swap(send, "seq", 1)))


    tied = tied if packed else ()
    gproj, smalls_short, *late = single(
        partial(short_back_kernel, ndocs, packed), "short_back", 3.0,
        [sds((block, 3 * width), BF16), sds((24, width), F32)]
        + ([sds((3 * width // 2, block), BF16)] * 2 if packed else []),
        meta, [ggate, for_in, for_values, rim_back, proj, short_weight], tied,
    )
    late_shape = (16, 3 * width // 2) if packed else (24, width)
    grad_tokens, smalls_late = single(
        tail_kernel, "tail", 2.5, [sds((block, width), F32), sds(late_shape, F32)],
        meta, [gproj, in_weight, tok, norm1_gain, gresid, smalls_short],
    )

    if packed:
        def placed(kernel, name, shapes, pieces):
            return single(kernel, name, 1.5, [sds(v, F32) for v in shapes], meta, pieces)

        late, late_send = late
        late_got = swap(late_send, "rows", 1)
        late_sib = swap(
            collected(
                meta, [(late, (0, late.shape[0])), (late_got, (0, late.shape[0]))]
            ), "seq", 1
        )
        keep3, send3 = partials(
            in_kernel, "in_grad", (share // 2, 3 * width // 2),
            (late, late_got, late_sib, early, early_got, early_sib), first_sums[:1],
        )
        kept3, halves3 = late_sums_of(
            meta, keep3, swap(send3, "rows", 2), smalls_late, swap(smalls_late, "seq", 1)
        )
        pieces = spread_out(meta, first_sums, [kept3])
        pieces3 = spread_late(meta, halves3)
        grad_down, grad_out, grad_up = placed(
            place_early_kernel, "place_early",
            ((hidden // blocks, width), (share, width), (share, hidden)), pieces,
        )
        (grad_in,) = placed(place_in_kernel, "place_in", ((share, 3 * width),), pieces3)

        (small,) = single(
            small_kernel, "small", 0.5, [sds((SMALL_BLOCK, 128), F32)], meta, pieces
        )
        near = [small] + [swap(small, "seq", 2 * k) for k in (1, 2, 3)]
        (small,) = single(
            stack_kernel, "stack", 0.5, [sds((chips, SMALL_BLOCK, 128), F32)], meta, near, [grad_up]
        )
        other = swap(small, "seq", 1)
        shapes = [
            (width,), (width,), (3 * width,), (taps_n, 3 * width), (3 * width,), (feats, fwidth),
            (fwidth,), (fwidth, fwidth), (fwidth,), (fwidth, fwidth), (fwidth,), (fwidth, width),
            (fwidth,), (width,), (width,), (width,), (width,), (hidden,), (width,),
        ]
        smalls = single(
            partial(unpack_kernel, taps_n, fwidth, feats, share // 2), "unpack", 1.5,
            [sds(v, F32) for v in shapes], meta, [small, other, *pieces3],
            scratch=[pltpu.VMEM((2 * half_rows, small_cols), F32), pltpu.VMEM(late_shape, F32)],
        )
    else:
        def summed(left, right):
            part = lax.psum_scatter(dot(left, right), "seq", scatter_dimension=0, tiled=True)
            return lax.psum(part, "rows")

        actt, gpre, n2t, gatedt, gmix = acts
        grad_in = summed(early, gproj)
        grad_out = summed(gatedt, gmix)
        grad_up = summed(n2t, gpre)
        grad_down = summed(actt, cot)
        small, late_sum, *fg = lax.psum((smalls_mlp, smalls_late, *filter_grads), ("rows", "seq"))
        wide = lambda first: late_sum[first : first + 3].reshape(-1)
        smalls = [
            late_sum[22], late_sum[23], wide(0), late_sum[3 : 3 + 3 * taps_n].reshape(taps_n, -1),
            wide(3 + 3 * taps_n), *fg, small[4, :width], small[3, :width], small[1, :width],
            small[2, :width], small[5:8].reshape(-1), small[0, :width],
        ]
    (grad_gain1, grad_shift1, grad_in_bias, grad_short_weight, grad_short_bias, f1, f1b, f2, f2b, f3,
     f3b, flast, freq, grad_filter_bias, grad_out_bias, grad_gain2, grad_shift2, grad_up_bias,
     grad_down_bias) = smalls
    return (
        output[None], grad_tokens[None], grad_gain1, grad_shift1, grad_in, grad_in_bias,
        grad_short_weight, grad_short_bias, f1, f1b, f2, f2b, f3, f3b, flast, freq,
        grad_filter_bias, grad_out, grad_out_bias, grad_gain2, grad_shift2, grad_up, grad_up_bias,
        grad_down, grad_down_bias,
    )


def solution(mesh):
    sharded = P("rows", "seq", None)
    placed = (sharded, P("rows", None)) + (P(),) * 23 + (sharded,)
    outs = [P()] * 25
    outs[0] = outs[1] = sharded
    for i in (4, 17, 21, 23):
        outs[i] = P("seq", None)
    return jax.shard_map(local, mesh=mesh, in_specs=placed, out_specs=tuple(outs), check_vma=False)
```

```python
from functools import partial
import math

import jax
import jax.numpy as jnp
import numpy as np
from jax import lax
from jax.experimental import pallas as pl
from jax.experimental.pallas import tpu as pltpu
from jax.sharding import PartitionSpec as P

EPSILON = 1e-05
HIGHEST = lax.Precision.HIGHEST
MIN_DECAY = math.log(100.0) / 1.5
MAX_DECAY = math.log(100.0) / 0.3
F32 = jnp.float32
BF16 = jnp.bfloat16
RIM = 16
OTHER_ROWS = 496
SMALL_BLOCK = 80
LATE_ROWS = tuple(range(15)) + (22, 23)
VMEM_LIMIT = 26 * 1024 * 1024
GELU_C = math.sqrt(2.0 / math.pi)
GELU_A = 0.044715


def params(limit=VMEM_LIMIT):
    return pltpu.CompilerParams(vmem_limit_bytes=limit)


def cost(micros):
    return pl.CostEstimate(flops=int(micros * 1.1e9), bytes_accessed=0, transcendentals=0)


def single(kernel, name, micros, outs, scalars, arrays, after=(), scratch=(), fetch=(), limit=VMEM_LIMIT):
    count, skip, nouts = len(arrays), len(after), len(outs)

    def body(meta, *refs):
        ins, made = list(refs[:count]), refs[count + skip : count + skip + nouts]
        rest = list(refs[count + skip + nouts :])
        if fetch:
            sems, rest = rest[-1], rest[:-1]
            held, rest = rest[: len(fetch)], rest[len(fetch) :]
            copies = [
                pltpu.make_async_copy(ins[p], dest, sems.at[i])
                for i, (p, dest) in enumerate(zip(fetch, held))
            ]
            for copy in copies:
                copy.start()
            for copy in copies:
                copy.wait()
            for p, dest in zip(fetch, held):
                ins[p] = dest
        kernel(meta, *ins, *made, *rest)

    own = [pltpu.VMEM(arrays[p].shape, arrays[p].dtype) for p in fetch]
    sems = [pltpu.SemaphoreType.DMA((len(fetch),))] if fetch else []
    return pl.pallas_call(
        body,
        grid=(1,),
        out_shape=tuple(outs),
        in_specs=[smem()]
        + [
            pl.BlockSpec(memory_space=pltpu.HBM) if p in fetch else whole(v.shape)
            for p, v in enumerate(arrays)
        ]
        + [pl.BlockSpec(memory_space=pl.ANY)] * skip,
        out_specs=tuple(whole(v.shape) for v in outs),
        scratch_shapes=own + list(scratch) + sems,
        compiler_params=params(limit),
        cost_estimate=cost(micros),
        name=name,
    )(scalars, *arrays, *after)


def smem():
    return pl.BlockSpec(memory_space=pltpu.SMEM)


def whole(shape):
    return pl.BlockSpec(shape, lambda *_: (0,) * len(shape))


def dot(left, right):
    return jnp.dot(left, right, preferred_element_type=F32)


def dot_t(left, right):
    return lax.dot_general(left, right, (((1,), (1,)), ((), ())), preferred_element_type=F32)


def high_low(values):
    high = values.astype(BF16)
    return high, (values - high.astype(F32)).astype(BF16)


def doc_at(meta, ndocs, position):
    total = jnp.int32(-1)
    for d in range(ndocs):
        total = total + (position >= meta[4 + d]).astype(jnp.int32)
    return total


def doc_start(meta, ndocs, position):
    found = jnp.int32(0)
    for d in range(ndocs):
        found = jnp.where(position >= meta[4 + d], meta[4 + d], found)
    return found


def doc_end(meta, ndocs, position, length):
    found = jnp.int32(length)
    for d in reversed(range(ndocs)):
        found = jnp.where(position < meta[4 + d], meta[4 + d], found)
    return found


def doc_column(meta, ndocs, first, rows):
    position = first + lax.broadcasted_iota(jnp.int32, (rows, 1), 0)
    total = jnp.full((rows, 1), -1, jnp.int32)
    for d in range(ndocs):
        total = total + (position >= meta[4 + d]).astype(jnp.int32)
    return position, total


def block_tables(block):
    period = 2 * block
    packed = np.arange(period)
    freq = np.where(packed <= block, packed, packed - block)
    places = np.arange(period)
    angle = 2.0 * np.pi / period * (freq[:, None] * places[None, :] % period)
    real = (packed <= block)[:, None]
    forward = np.where(real, np.cos(angle), -np.sin(angle))
    scaling = np.where((packed == 0) | (packed == block), 1.0, 2.0) / period
    inverse = (forward * scaling[:, None]).T[block:]
    left = forward[:, :block]

    def split(table):
        table = table.astype(np.float32)
        high = table.astype(BF16)
        return high, (table - high.astype(np.float32)).astype(BF16)

    lh, ll = split(left)
    ih, il = split(inverse)
    return dict(
        left2=np.concatenate([lh, ll], 1),
        left3=np.concatenate([lh, lh, ll], 1),
        inv3=np.concatenate([ih, ih, il], 1),
        invt2=np.concatenate([ih.T, il.T], 1),
        leftt3=np.concatenate([lh.T, lh.T, ll.T], 1),
    )


def spectrum2(table, signal):
    return dot(table, jnp.concatenate([signal, signal], axis=0))


def spectrum3(table, values):
    high, low = high_low(values)
    return dot(table, jnp.concatenate([high, low, high], axis=0))


def masked(signal, mask):
    return jnp.where(mask, signal.astype(F32), 0.0).astype(BF16)


def first_row(shape):
    return lax.broadcasted_iota(jnp.int32, shape, 0) == 0


def times(left, right):
    half = left.shape[0] // 2
    lre, lim = left[:half], left[half:]
    rre, rim = right[:half], right[half:]
    row = first_row(lre.shape)
    edge = jnp.where(row, 0.0, lim)
    return lre * rre - edge * rim, edge * rre + jnp.where(row, lim, lre) * rim


def times_back(left, grad):
    half = left.shape[0] // 2
    lre, lim = left[:half], left[half:]
    gre, gim = grad[:half], grad[half:]
    row = first_row(lre.shape)
    edge = jnp.where(row, 0.0, lim)
    return lre * gre + edge * gim, jnp.where(row, lim, lre) * gim - edge * gre


def add_spec(acc, pair):
    half = acc.shape[0] // 2
    acc[:half, :] += pair[0]
    acc[half:, :] += pair[1]


def set_spec(acc, pair):
    half = acc.shape[0] // 2
    acc[:half, :] = pair[0]
    acc[half:, :] = pair[1]


def normalise(values):
    average = jnp.mean(values, axis=-1, keepdims=True)
    centred = values - average
    spread = jnp.mean(centred * centred, axis=-1, keepdims=True)
    rstd = lax.rsqrt(spread + EPSILON)
    return centred * rstd, rstd


def row_of(ref):
    return ref[...].astype(F32).reshape(1, -1)


def part_of(ref, first, size):
    return ref[pl.ds(first, size)].astype(F32).reshape(1, -1)


def write_side(out, first, source, count, rows, parity):
    for z in range(count):
        out[pl.ds(first + z * rows, rows), :] = source[
            pl.ds(pl.multiple_of((2 * z + parity) * rows, 16), rows), :
        ]


def write_strips(out, first, source, count, rows, core):
    for p in range(2):
        for z in range(count):
            out[pl.ds(first + (p * count + z) * rows, rows), :] = source[
                pl.ds(pl.multiple_of((2 * z + (core ^ p)) * rows, 16), rows), :
            ]


def write_tiles(out, first, source, start, count):
    tokens = source.shape[0]
    for t in range(count):
        out[pl.ds(first + t * tokens, tokens), :] = source[
            :, pl.ds(pl.multiple_of(start + t * 128, 128), 128)
        ]


def front_kernel(ndocs, packed, meta, tokens, rim, cot, gain, bias, weight, wbias, taps, tbias,
                 proj_ref, normt_ref, mixed_ref, carried_ref, turned):
    block, width = tokens.shape
    taps_n = taps.shape[0]
    ext = jnp.concatenate([rim[...], tokens[...]], axis=0).astype(F32)
    hat, _ = normalise(ext)
    normed = hat * row_of(gain) + row_of(bias)
    turned[...] = normed[RIM:].T.astype(BF16)
    if packed:
        chips = packed
        write_strips(normt_ref, 0, turned, chips, width // (2 * chips), meta[1])
        write_tiles(normt_ref, width, cot, 0, width // 128)
    else:
        normt_ref[...] = turned[...]
    low = normed.astype(BF16)
    base = meta[0] * block
    position, ids = doc_column(meta, ndocs, base, block)
    masks = []
    for k in range(taps_n):
        _, back = doc_column(meta, ndocs, base - k, block)
        masks.append(((back == ids) & (position >= k)).astype(F32))
    for third in range(3):
        cols = slice(third * width, (third + 1) * width)
        proj_ref[:, cols] = dot(low, weight[:, cols]) + part_of(wbias, third * width, width)
        total = part_of(tbias, third * width, width)
        for k in range(taps_n):
            moved = proj_ref[pl.ds(RIM - k, block), cols]
            total = total + taps[k : k + 1, cols].astype(F32) * moved * masks[k]
        mixed_ref[:, cols] = total
    carried_ref[...] = (mixed_ref[:, 2 * width :] * mixed_ref[:, width : 2 * width]).astype(BF16)


def lag_kernel(taps, left3, out):
    blocks = taps.shape[0]
    sign = 1.0 - 2.0 * (lax.broadcasted_iota(jnp.int32, (out.shape[1], 1), 0) % 2).astype(F32)

    def step(j, carry):
        spec = spectrum3(left3[...], taps[j])
        out[j] = out[j] + sign * spec

        @pl.when(j + 1 < blocks)
        def _():
            out[j + 1] = spec

        return carry

    out[0] = jnp.zeros(out.shape[1:], F32)
    lax.fori_loop(0, blocks, step, 0)


def fill(meta, parts, first, held):
    near, sibling = parts[:-1], parts[-1]
    block, width = held.shape[1:]
    for k, ref in enumerate(near):
        z = meta[2] ^ k
        held[2 * z + meta[1]] = ref[...]
        for t in range(width // 128):
            rows = pl.ds(first + (k * (width // 128) + t) * block, block)
            held[2 * z + 1 - meta[1], :, t * 128 : (t + 1) * 128] = sibling[rows, :]


def conv_kernel(ndocs, nparts, first, meta, *refs):
    parts, (lags, left2, inv3, out, acc), rest = refs[:nparts], refs[nparts : nparts + 5], refs[nparts + 5 :]
    signal = parts[0]
    if nparts > 1:
        (signal,) = rest
        fill(meta, parts, first, signal)
    block = signal.shape[1]
    me = meta[0]
    base = me * block
    start = doc_start(meta, ndocs, base)
    low_block = start // block
    _, ids = doc_column(meta, ndocs, base, block)
    first_doc = doc_at(meta, ndocs, base)
    last_doc = doc_at(meta, ndocs, base + block - 1)
    own = signal[me]
    spec = spectrum2(left2[...], masked(own, ids == first_doc))
    set_spec(acc, times(lags[0], spec))

    def cross(pair, carry):
        total = None
        for s in (low_block + 2 * pair, low_block + 2 * pair + 1):
            position = s * block + lax.broadcasted_iota(jnp.int32, (block, 1), 0)
            spec = spectrum2(left2[...], masked(signal[s], (position >= start) & (position < base)))
            made = times(lags[me - s], spec)
            total = made if total is None else (total[0] + made[0], total[1] + made[1])
        add_spec(acc, total)
        return carry

    lax.fori_loop(0, (me - low_block + 1) // 2, cross, 0)
    out[...] = jnp.where(ids == first_doc, spectrum3(inv3[...], acc[...]), 0.0)

    def inner(d, carry):
        spec = spectrum2(left2[...], masked(own, ids == d))
        set_spec(acc, times(lags[0], spec))
        out[...] += jnp.where(ids == d, spectrum3(inv3[...], acc[...]), 0.0)
        return carry

    lax.fori_loop(first_doc + 1, last_doc + 1, inner, 0)


def mlp_kernel(packed, meta, tokens, cot, conv, carried, gate_out, fbias, w_out, b_out, gain, shift,
               up, up_bias, down, down_bias, *refs):
    (output, gresid, glong, glong16, ggate, smalls), refs = refs[:6], refs[6:]
    (own, shared, e1_send, e2_send) = refs[:4]
    if packed:
        refs = refs[4:]
    else:
        actt, gpre_out, n2t_out, gatedt_out, gmix_out = refs[:5]
        refs = refs[5:]
    resid, n2, hat2, rstd2, oacc, gacc, ubias, ubias_grad, turned, rows_held = refs
    j = pl.program_id(0)
    block, width = tokens.shape
    ff = up.shape[1]
    core, x, y = meta[1], meta[3] % 2, meta[3] // 2
    chips = packed
    if packed:
        share, big = width // (2 * chips), ff // 2
        half = big // 2
        slot = chips * (half + share)

    @pl.when(j == 0)
    def _():
        ubias[...] = row_of(up_bias)
        long_out = conv[...] + row_of(fbias) * carried[...].astype(F32)
        gated = long_out * gate_out[...]
        gated_t = gated.T.astype(BF16)
        r = tokens[...].astype(F32) + dot(gated.astype(BF16), w_out[...]) + row_of(b_out)
        resid[...] = r
        hat, rstd = normalise(r)
        hat2[...] = hat
        rstd2[...] = rstd
        normed = hat * row_of(gain) + row_of(shift)
        n2[...] = normed.astype(BF16)
        oacc[...] = jnp.zeros_like(oacc)
        gacc[...] = jnp.zeros_like(gacc)
        if packed:
            turned[...] = gated_t
            later = chips * half
            for dest, p, first in ((own, 0, later), (shared, 1, later), (e1_send, 0, later),
                                   (e1_send, 1, slot + later)):
                write_side(dest, first, turned, chips, share, core ^ p)
            turned[...] = normed.T.astype(BF16)
            after1 = slot + width // 2
            for dest, p, first in ((own, 0, slot), (shared, 1, after1), (e2_send, 0, 0),
                                   (e2_send, 1, chips * share)):
                write_side(dest, first, turned, chips, share, core ^ p)
        else:
            gatedt_out[...] = gated_t
            n2t_out[...] = normed.T.astype(BF16)

    bias = ubias[:, pl.ds(pl.multiple_of(j * ff, 128), ff)]
    pre = dot(n2[...], up[...]) + bias
    sq = pre * pre
    th = jnp.tanh(GELU_C * (pre * (1.0 + GELU_A * sq)))
    act = 0.5 * pre * (1.0 + th)
    slope = 0.5 * (1.0 + th) + 0.5 * pre * (1.0 - th * th) * (
        GELU_C * (1.0 + 3.0 * GELU_A * sq)
    )
    if packed:
        turned[...] = act.T.astype(BF16)
        for dest, p, side, first in ((own, 0, x, 0), (shared, 1, x, 0), (e1_send, 0, 1 - x, 0),
                                     (e1_send, 1, 1 - x, slot)):
            dest[pl.ds(pl.multiple_of(first + j * half, 16), half), :] = turned[
                pl.ds(pl.multiple_of((core ^ p) * big + side * half, 16), half), :
            ]
    else:
        actt[...] = act.T.astype(BF16)
    oacc[...] += dot(act.astype(BF16), down[...])
    gpre = (dot_t(cot[...], down[...]) * slope).astype(BF16)
    if packed:
        rows_held[...] = gpre
        per = chips // 2
        for t in range(ff // 128):
            at = ((j % per) * (ff // 128) + t) * block
            tile = gpre[:, t * 128 : (t + 1) * 128]

            @pl.when(j // per == y)
            def _():
                first = slot + width // 2 + chips * share
                shared[pl.ds(pl.multiple_of(first + at, 16), block), :] = tile

            @pl.when(j // per != y)
            def _():
                e2_send[pl.ds(pl.multiple_of(width + at, 16), block), :] = tile
    else:
        gpre_out[...] = gpre
    ubias_grad[:, pl.ds(pl.multiple_of(j * ff, 128), ff)] = jnp.sum(
        gpre.astype(F32), axis=0, keepdims=True
    )
    gacc[...] += dot_t(gpre, up[...])

    @pl.when(j == pl.num_programs(0) - 1)
    def _():
        output[...] = (resid[...] + oacc[...] + row_of(down_bias)).astype(BF16)
        top = cot[...].astype(F32)
        gn = gacc[...]
        hat = hat2[...]
        q = gn * row_of(gain)
        mean_q = jnp.mean(q, axis=-1, keepdims=True)
        mean_qh = jnp.mean(q * hat, axis=-1, keepdims=True)
        gr = top + (q - mean_q - hat * mean_qh) * rstd2[...]
        gresid[...] = gr
        gm = gr.astype(BF16)
        if packed:
            rows_held[...] = gm
            write_tiles(shared, slot, rows_held, x * (width // 2), width // 256)
            write_tiles(e1_send, 2 * slot, rows_held, (1 - x) * (width // 2), width // 256)
        else:
            gmix_out[...] = gm
        gg = dot_t(gm, w_out[...])
        c = carried[...].astype(F32)
        long_out = conv[...] + row_of(fbias) * c
        gl = gg * gate_out[...]
        glong[...] = gl
        glong16[...] = gl.astype(BF16)
        ggate[...] = gg * long_out
        rows = [
            jnp.sum(top, axis=0, keepdims=True),
            jnp.sum(gn * hat, axis=0, keepdims=True),
            jnp.sum(gn, axis=0, keepdims=True),
            jnp.sum(gm.astype(F32), axis=0, keepdims=True),
            jnp.sum(gl * c, axis=0, keepdims=True),
        ]
        lanes = smalls.shape[1]
        for i, made in enumerate(rows):
            smalls[i : i + 1, :width] = made
            smalls[i : i + 1, width:] = jnp.zeros((1, lanes - width), F32)
        for i in range(ubias_grad.shape[1] // lanes):
            smalls[len(rows) + i : len(rows) + i + 1, :] = ubias_grad[:, i * lanes : (i + 1) * lanes]


def conv_back_kernel(ndocs, length, nparts, first, meta, *refs):
    parts, refs = refs[:nparts], refs[nparts:]
    (own_grad, lags, invt2, leftt3, fbias, gate_in, values, ggate, short_gate, short_in,
     short_values, for_in, for_values, rim, acc) = refs[:15]
    grads = parts[0]
    if nparts > 1:
        grads = refs[15]
        fill(meta, parts, first, grads)
    block = grads.shape[1]
    me = meta[0]
    base = me * block
    _, ids = doc_column(meta, ndocs, base, block)
    first_doc = doc_at(meta, ndocs, base)
    last_doc = doc_at(meta, ndocs, base + block - 1)
    last_block = (doc_end(meta, ndocs, base + block - 1, length) - 1) // block
    own = grads[me]
    spec = spectrum2(invt2[...], masked(own, ids == last_doc))
    set_spec(acc, times_back(lags[0], spec))

    def cross(pair, carry):
        total = None
        for t in (me + 1 + 2 * pair, me + 2 + 2 * pair):
            place = jnp.minimum(t, grads.shape[0] - 1)
            _, far = doc_column(meta, ndocs, place * block, block)
            spec = spectrum2(
                invt2[...], masked(grads[place], (far == last_doc) & (t <= last_block))
            )
            made = times_back(lags[place - me], spec)
            total = made if total is None else (total[0] + made[0], total[1] + made[1])
        add_spec(acc, total)
        return carry

    lax.fori_loop(0, (last_block - me + 1) // 2, cross, 0)
    for_in[...] = jnp.where(ids == last_doc, spectrum3(leftt3[...], acc[...]), 0.0)

    def inner(d, carry):
        spec = spectrum2(invt2[...], masked(own, ids == d))
        set_spec(acc, times_back(lags[0], spec))
        for_in[...] += jnp.where(ids == d, spectrum3(leftt3[...], acc[...]), 0.0)
        return carry

    lax.fori_loop(first_doc, last_doc, inner, 0)
    total = for_in[...] + row_of(fbias) * own_grad[...]
    for_in[...] = total * values[...]
    for_values[...] = total * gate_in[...]
    reach = short_gate.shape[0] - 1
    for third, (grad, taps) in enumerate(
        ((ggate, short_gate), (for_in, short_in), (for_values, short_values))
    ):
        rows = [jnp.zeros((8 - reach, grad.shape[1]), F32)]
        for p in range(reach):
            made = jnp.zeros((1, grad.shape[1]), F32)
            for k in range(1, reach + 1):
                t = p - reach + k
                if 0 <= t < reach:
                    same = doc_at(meta, ndocs, base - reach + p) == doc_at(meta, ndocs, base + t)
                    keep = (same & (base > 0)).astype(F32)
                    made = made + taps[k : k + 1, :].astype(F32) * grad[t : t + 1, :] * keep
            rows.append(made)
        rim[third] = jnp.concatenate(rows, axis=0)


def taps_grad_kernel(ndocs, nparts, first, meta, *refs):
    parts, refs = refs[:nparts], refs[nparts:]
    own_grad, left2, invt2, leftt3, out, win, gspec = refs[:7]
    signal = parts[0]
    if nparts > 1:
        signal = refs[7]
        fill(meta, parts, first, signal)
    blocks, block = signal.shape[0], signal.shape[1]
    me = meta[0]
    base = me * block
    start = doc_start(meta, ndocs, base)
    low_block = start // block
    _, ids = doc_column(meta, ndocs, base, block)
    first_doc = doc_at(meta, ndocs, base)
    last_doc = doc_at(meta, ndocs, base + block - 1)
    sign = 1.0 - 2.0 * (lax.broadcasted_iota(jnp.int32, (2 * block, 1), 0) % 2).astype(F32)
    own = signal[me]
    grad = own_grad[...]
    out[...] = jnp.zeros_like(out)
    win[me - low_block + 1] = jnp.zeros(win.shape[1:], F32)
    gspec[...] = spectrum2(invt2[...], masked(grad, ids == first_doc))
    spec = spectrum2(left2[...], masked(own, ids == first_doc))
    set_spec(win.at[0], times_back(spec, gspec[...]))

    def inner(d, carry):
        spec = spectrum2(left2[...], masked(own, ids == d))
        back = spectrum2(invt2[...], masked(grad, ids == d))
        add_spec(win.at[0], times_back(spec, back))
        return carry

    lax.fori_loop(first_doc + 1, last_doc + 1, inner, 0)

    def cross(s, carry):
        position = s * block + lax.broadcasted_iota(jnp.int32, (block, 1), 0)
        spec = spectrum2(left2[...], masked(signal[s], position >= start))
        set_spec(win.at[me - s], times_back(spec, gspec[...]))
        return carry

    lax.fori_loop(low_block, me, cross, 0)

    def emit(k, carry):
        out[k] = spectrum3(leftt3[...], win[k + 1] + sign * win[k])
        return carry

    lax.fori_loop(0, me - low_block + 1, emit, 0)


def short_back_kernel(ndocs, packed, meta, ggate, for_in, for_values, rim, proj, taps,
                      gproj_ref, smalls, *sends):
    block, width = ggate.shape
    taps_n = taps.shape[0]
    base = meta[0] * block
    position, ids = doc_column(meta, ndocs, base, block)
    masks = []
    for k in range(taps_n):
        _, back = doc_column(meta, ndocs, base - k, block)
        masks.append(((back == ids) & (position >= k)).astype(F32))
    row = lax.broadcasted_iota(jnp.int32, (block, 1), 0)
    ahead = []
    for k in range(1, taps_n):
        _, later = doc_column(meta, ndocs, base + k, block)
        ahead.append(((later == ids) & (row < block - k)).astype(F32))
    bias_rows, weight_rows, short_rows = [], [], []
    for third, grad_ref in enumerate((ggate, for_in, for_values)):
        cols = slice(third * width, (third + 1) * width)
        grad = grad_ref[...]
        total = taps[0:1, cols].astype(F32) * grad
        weights = [jnp.sum(grad * proj[pl.ds(RIM, block), cols], axis=0, keepdims=True)]
        for k in range(1, taps_n):
            moved = pltpu.roll(grad, block - k, 0) * ahead[k - 1]
            total = total + taps[k : k + 1, cols].astype(F32) * moved
            weights.append(
                jnp.sum(grad * masks[k] * proj[pl.ds(RIM - k, block), cols], axis=0, keepdims=True)
            )
        tail = jnp.concatenate([jnp.zeros((block - 8, width), F32), rim[third]], axis=0)
        low = (total + tail).astype(BF16)
        gproj_ref[:, cols] = low
        bias_rows.append(jnp.sum(low.astype(F32), axis=0, keepdims=True))
        short_rows.append(jnp.sum(grad, axis=0, keepdims=True))
        weight_rows.append(weights)
    rows = bias_rows + [weight_rows[t][k] for k in range(taps_n) for t in range(3)] + short_rows
    pad = smalls.shape[0] - len(rows)
    smalls[...] = jnp.concatenate(rows + [jnp.zeros((pad, width), F32)], axis=0)
    if packed:
        x = meta[3] % 2
        half = 3 * width // 2
        for dest, side in zip(sends, (x, 1 - x)):
            write_tiles(dest, 0, gproj_ref, side * half, half // 128)


def tail_kernel(meta, gproj, weight, tokens, gain, gresid, others, out, smalls):
    gn = dot_t(gproj[...], weight[...])
    hat, rstd = normalise(tokens[...].astype(F32))
    q = gn * row_of(gain)
    mean_q = jnp.mean(q, axis=-1, keepdims=True)
    mean_qh = jnp.mean(q * hat, axis=-1, keepdims=True)
    out[...] = gresid[...] + (q - mean_q - hat * mean_qh) * rstd
    rows = [others[i : i + 1, :] for i in range(others.shape[0] - 2)]
    rows += [jnp.sum(gn * hat, axis=0, keepdims=True), jnp.sum(gn, axis=0, keepdims=True)]
    if smalls.shape[1] == others.shape[1]:
        smalls[...] = jnp.concatenate(rows, axis=0)
        return
    smalls[...] = jnp.zeros_like(smalls)
    half = others.shape[1] // 2
    for k, (r, h) in enumerate((r, h) for r in LATE_ROWS for h in range(2)):
        smalls[k // 3 : k // 3 + 1, k % 3 * half : (k % 3 + 1) * half] = rows[r][:, h * half : (h + 1) * half]


def filter_taps(first, first_bias, second, second_bias, third, third_bias, last, sine_freq, length):
    lags = jnp.arange(length)
    bands = (first.shape[0] - 1) // 2
    moment = lags.astype(F32) / (length - 1)
    band_freq = jnp.linspace(0.0001, bands - 1, bands, dtype=F32)
    phase = 2.0 * math.pi / length * lags.astype(F32)
    angles = phase[:, None] * band_freq[None, :]
    features = jnp.concatenate([moment[:, None], jnp.cos(angles), -jnp.sin(angles)], axis=1)
    hidden = jnp.sin(sine_freq * (jnp.dot(features, first, precision=HIGHEST) + first_bias))
    hidden = jnp.sin(sine_freq * (jnp.dot(hidden, second, precision=HIGHEST) + second_bias))
    hidden = jnp.sin(sine_freq * (jnp.dot(hidden, third, precision=HIGHEST) + third_bias))
    rates = jnp.linspace(MIN_DECAY, MAX_DECAY, last.shape[1], dtype=F32)
    window = jnp.exp(-moment[:, None] * rates[None, :])
    return jnp.dot(hidden, last, precision=HIGHEST) * window


def sine_pair(values):
    turns = jnp.floor(values * (2.0 / math.pi) + 0.5)
    rest = values - turns * 1.5703125
    rest = rest - turns * 4.837512969970703125e-4
    rest = rest - turns * 7.549789948768648e-8
    sq = rest * rest
    s = ((-1.9515295891e-4 * sq + 8.3321608736e-3) * sq - 1.6666654611e-1) * sq * rest + rest
    c = ((2.443315711809948e-5 * sq - 1.388731625493765e-3) * sq + 4.166664568298827e-2) * sq * sq
    c = c - 0.5 * sq + 1.0
    quarter = turns.astype(jnp.int32)
    odd = (quarter & 1) == 1
    half = (quarter & 2) == 2
    first = jnp.where(odd, c, s)
    second = jnp.where(odd, s, c)
    return jnp.where(half, -first, first), jnp.where(half ^ odd, -second, second)


def exact_dot(weights, values):
    high = values.astype(BF16)
    rest = values - high.astype(F32)
    middle = rest.astype(BF16)
    low = (rest - middle.astype(F32)).astype(BF16)
    return dot(weights, high) + (dot(weights, middle) + dot(weights, low))


def feature_table(length, bands):
    lags = np.arange(length).astype(np.float32)
    moment = lags / np.float32(length - 1)
    freq = np.linspace(0.0001, bands - 1, bands).astype(np.float32)
    phase = np.float32(2.0 * math.pi / length) * lags
    angles = (phase[:, None] * freq[None, :]).astype(np.float64)
    table = np.concatenate(
        [moment[:, None].astype(np.float64), np.cos(angles), -np.sin(angles)], axis=1
    )
    return np.pad(table.astype(np.float32), ((0, 0), (0, -table.shape[1] % 8))).T


def decay_window(width, length):
    moment = lax.broadcasted_iota(jnp.int32, (length, 1), 0).astype(F32) / (length - 1)
    step = (MAX_DECAY - MIN_DECAY) / (width - 1)
    rates = MIN_DECAY + step * lax.broadcasted_iota(jnp.int32, (1, width), 1).astype(F32)
    return jnp.exp(-moment * rates)


def turned_column(ref):
    return jnp.broadcast_to(row_of(ref), (8, ref.shape[0])).T[:, :1]


def filter_kernel(meta, table, first, b1, second, b2, third, b3, last, freq, left3,
                  lags, window, act, slope, pre, a3):
    blocks, period, width = lags.shape
    block = period // 2
    length = blocks * block
    fwidth = freq.shape[0]
    scale = turned_column(freq)
    hidden = table[...]
    pad = table.shape[0] - first.shape[0]
    firsts = jnp.concatenate([first[...].astype(F32), jnp.zeros((pad, fwidth), F32)], axis=0)
    for i, (weight, bias) in enumerate(
        ((firsts, b1), (second[...].astype(F32), b2), (third[...].astype(F32), b3))
    ):
        u = exact_dot(weight.T.astype(BF16), hidden) + turned_column(bias)
        hidden, cosine = sine_pair(scale * u)
        rows = slice(i * fwidth, (i + 1) * fwidth)
        act[rows, :] = hidden
        slope[rows, :] = cosine
        pre[rows, :] = u
    a3[...] = hidden.T
    window[...] = decay_window(width, length)
    sign = 1.0 - 2.0 * (lax.broadcasted_iota(jnp.int32, (period, 1), 0) % 2).astype(F32)
    before = None
    for j in range(blocks):
        part = a3[j * block : (j + 1) * block, :]
        high = part.astype(BF16)
        rest = part - high.astype(F32)
        middle = rest.astype(BF16)
        low = (rest - middle.astype(F32)).astype(BF16)
        lhs = jnp.concatenate([high, middle, low], axis=1)
        rhs = jnp.concatenate([last[...]] * 3, axis=0)
        taps = dot(lhs, rhs) * window[j * block : (j + 1) * block, :]
        spec = spectrum3(left3[...], taps)
        lags[j] = sign * spec if before is None else before + sign * spec
        before = spec


def filter_back_kernel(meta, grads, window, act, slope, pre, table, first, second, third, last,
                       freq, others, mine, send, packed):
    blocks, block, width = grads.shape
    length = blocks * block
    fwidth = freq.shape[0]
    scale = turned_column(freq)
    core = meta[1]
    weighted = grads[...].reshape(length, width) * window[...]
    wh, wl = high_low(weighted)
    ah, al = high_low(act[2 * fwidth :, :])
    packed[...] = jnp.zeros_like(packed)
    made = dot(ah, wh) + (dot(ah, wl) + dot(al, wh))
    place = 0
    for t in range(width // 128):
        packed[place : place + fwidth, :] = made[:, t * 128 : (t + 1) * 128]
        place += fwidth
    for i in range(others.shape[0]):
        count = others.shape[1] // 128 if i >= 5 else width // 128
        for t in range(count):
            row = OTHER_ROWS + (i * 6 + t if i < 5 else 30 + (i - 5) * count + t)
            packed[row : row + 1, :] = others[i : i + 1, t * 128 : (t + 1) * 128]
    back = dot_t(last[...], wh) + dot_t(last[...], wl)
    ones = jnp.ones((8, length), BF16)

    def wide_t(left, right):
        lh, ll = high_low(left)
        rh, rl = high_low(right)
        return dot_t(lh, rh) + (dot_t(lh, rl) + dot_t(ll, rh))

    def sums(values):
        high, low = high_low(values)
        return (dot_t(ones, high) + dot_t(ones, low))[:1]

    freq_total = jnp.zeros((1, fwidth), F32)
    for i, weight in ((2, third), (1, second), (0, first)):
        rows = slice(i * fwidth, (i + 1) * fwidth)
        step = back * slope[rows, :]
        freq_total = freq_total + sums(step * pre[rows, :])
        step = step * scale
        below = act[(i - 1) * fwidth : i * fwidth, :] if i else table[...]
        made = wide_t(below, step)
        at, lanes = ((place + fwidth, 0), (place, fwidth), (place, 0))[i]
        packed[at : at + made.shape[0], lanes : lanes + fwidth] = made
        packed[place + fwidth + i : place + fwidth + i + 1, fwidth:] = sums(step)
        if i:
            high, low = high_low(step)
            back = dot(weight[...], high) + dot(weight[...], low)
    packed[place + fwidth + 3 : place + fwidth + 4, fwidth:] = freq_total
    size = SMALL_BLOCK
    for z in range(mine.shape[0] // size):
        out = slice(z * size, (z + 1) * size)
        mine[out, :] = packed[pl.ds(pl.multiple_of((2 * z + core) * size, 8), size), :]
        send[out, :] = packed[pl.ds(pl.multiple_of((2 * z + 1 - core) * size, 8), size), :]


def shift(block, axis, distance):
    devices = range(lax.axis_size(axis))
    return lax.ppermute(block, axis, [(i - distance, i) for i in devices if i - distance in devices])


def swap(block, axis, mask):
    return lax.ppermute(block, axis, [(i, i ^ mask) for i in range(lax.axis_size(axis))])


def collect_kernel(spans, meta, *refs):
    out, place = refs[-1], 0
    for ref, span in zip(refs[:-1], spans):
        if span is None:
            write_tiles(out, place, ref, 0, ref.shape[1] // 128)
            place += ref.shape[0] * (ref.shape[1] // 128)
        else:
            out[pl.ds(place, span[1] - span[0]), :] = ref[pl.ds(span[0], span[1] - span[0]), :]
            place += span[1] - span[0]


def collected(meta, pieces, after=()):
    rows = sum(v.shape[0] * v.shape[1] // 128 if span is None else span[1] - span[0] for v, span in pieces)
    (out,) = single(
        partial(collect_kernel, [span for _, span in pieces]), "collect", 0.6,
        [jax.ShapeDtypeStruct((rows, 128), BF16)], meta, [v for v, _ in pieces], after,
    )
    return out


def near_blocks(block, blocks):
    got = {k: swap(block, "seq", 2 * k) for k in (2, 3, 1)}
    return [block] + [got[k] for k in range(1, blocks // 2)]


def joined_left(sources, rows):
    return jnp.concatenate([ref[pl.ds(first, rows), :] for ref, first in sources], axis=1)


def joined_right(sources, block, start, count):
    return jnp.concatenate(
        [
            jnp.concatenate(
                [ref[pl.ds(first + t * block, block), :] for t in range(start, start + count)], axis=1
            )
            for ref, first in sources
        ],
        axis=0,
    )


def pick(flag, keep, send, store):
    @pl.when(flag)
    def _():
        store(keep)

    @pl.when(jnp.logical_not(flag))
    def _():
        store(send)


def early_sources(early, early_got, early_sib, width, columns):
    half = width // 2
    if columns:
        return ((early, width), (early_sib, half), (early_got, width), (early_sib, 2 * width))
    return ((early, 0), (early_sib, 0), (early_got, 0), (early_sib, half + width))


def down_out_kernel(chips, meta, own, shared, shared_sib, got, got_sib, early, early_got, early_sib,
                    keep, send):
    block = own.shape[1]
    share = keep.shape[1]
    width = early.shape[0] // 2
    half = 2 * share
    slot = chips * (half + share)
    y, chip = meta[3] // 2, meta[2]
    sources = (own, shared_sib, got, got_sib)
    made = dot(
        joined_left([(v, 0) for v in sources], chips * half),
        joined_right(early_sources(early, early_got, early_sib, width, True), block, 0, width // 128),
    ).astype(BF16)
    right = ((shared, slot), (shared_sib, slot), (got, 2 * slot), (got_sib, slot))
    out = dot(
        joined_left([(v, chips * half) for v in sources], chips * share),
        joined_right(right, block, 0, width // 256),
    ).astype(BF16)
    part = share // 2
    for side in range(2):

        def store(dest):
            for z in range(chips):
                at = z ^ chip
                first = z * half + side * share
                dest[at, :, :width] = made[first : first + share]
                rows = out[z * share + side * part : z * share + (side + 1) * part]
                dest[at, :part, width : width + 128] = rows[:, :128]
                dest[at, part:, width : width + 128] = rows[:, 128:256]
                dest[at, :part, width + 128 :] = rows[:, 256:]
                dest[at, part:, width + 128 :] = jnp.zeros((part, 128), BF16)

        pick(y == side, keep, send, store)


def up_kernel(chips, meta, own, shared, shared_sib, got, got_sib, keep, send):
    block = own.shape[1]
    share, width = keep.shape[1:]
    x, chip = meta[3] % 2, meta[2]
    rows = chips * share
    slot = 3 * rows
    first = slot + width // 2
    left = joined_left(((own, slot), (shared_sib, first), (got, 0), (got_sib, first)), rows)
    right = ((shared, first + rows), (shared_sib, first + rows), (got, 2 * rows), (got_sib, first + rows))
    for side in range(2):
        made = dot(left, joined_right(right, block, side * (width // 128), width // 128)).astype(BF16)

        def store(dest):
            for z in range(chips):
                dest[z ^ chip] = made[z * share : (z + 1) * share]

        pick(x == side, keep, send, store)


def in_kernel(chips, meta, mine, got, sib, early, early_got, early_sib, keep, send):
    block = mine.shape[1]
    part, cols = keep.shape[1:]
    width = early.shape[0] // 2
    y, chip = meta[3] // 2, meta[2]
    right = ((mine, 0), (sib, 0), (got, 0), (sib, mine.shape[0]))
    made = dot(
        joined_left(early_sources(early, early_got, early_sib, width, False), width // 2),
        joined_right(right, block, 0, cols // 128),
    ).astype(BF16)
    for side in range(2):

        def store(dest):
            for z in range(chips):
                first = (2 * z + side) * part
                dest[z ^ chip] = made[first : first + part]

        pick(y == side, keep, send, store)


def merge_kernel(pairs, kind, meta, *refs):
    ins, refs = refs[: 2 * pairs], refs[2 * pairs :]
    chips, rows = ins[0].shape[:2]
    extra, (own, *sends) = refs[:-chips], refs[-chips:]
    first = 0
    for p in range(pairs):
        keep, got = ins[2 * p : 2 * p + 2]
        cols = slice(first, first + keep.shape[2])
        first += keep.shape[2]
        own[:rows, cols] = keep[0].astype(F32) + got[0].astype(F32)
        for j, dest in enumerate(sends):
            dest[:rows, cols] = (keep[j + 1].astype(F32) + got[j + 1].astype(F32)).astype(BF16)
    if kind == "rows":
        value = (extra[0][...] + extra[1][...]).astype(BF16)
        own[rows:, :] = value.astype(F32)
        for dest in sends:
            dest[rows:, :] = value
    if kind == "tiles":
        size = SMALL_BLOCK
        for j, dest in enumerate((own, *sends)):
            take = pl.ds(pl.multiple_of((meta[2] ^ j) * size, 8), size)
            value = extra[0][take, :] + extra[1][take, :]
            dest[:size, first:] = value.astype(dest.dtype)
            dest[size:, first:] = jnp.zeros((rows - size, dest.shape[1] - first), dest.dtype)


def total_kernel(meta, own, one, two, three, out):
    out[...] = (
        (own[...] + one[...].astype(F32)) + (two[...].astype(F32) + three[...].astype(F32))
    ).astype(BF16)


def chip_sums(meta, pairs, kind, extra):
    chips, rows, _ = pairs[0].shape
    cols = sum(v.shape[2] for v in pairs[::2])
    rows += extra[0].shape[0] if kind == "rows" else 0
    cols += 128 if kind == "tiles" else 0
    sds = jax.ShapeDtypeStruct
    return single(
        partial(merge_kernel, len(pairs) // 2, kind), "merge", 1.0,
        [sds((rows, cols), F32)] + [sds((rows, cols), BF16)] * (chips - 1), meta, (*pairs, *extra),
    )


def spread_out(meta, sums, after=()):
    own, *sends = sums
    got = {j: swap(sends[j - 1], "seq", 2 * j) for j in (2, 3, 1)}
    (total,) = single(
        total_kernel, "total", 1.0, [jax.ShapeDtypeStruct(own.shape, BF16)], meta,
        [own, got[1], got[2], got[3]], after,
    )
    return [total] + [swap(total, "rows", j) for j in (1, 2, 3)]


def merge_halves_kernel(meta, keep, got, left, right, keep_out, send_out):
    rows = keep.shape[1]
    for dest, order in ((keep_out, (0, 2)), (send_out, (1, 3))):
        for i, j in enumerate(order):
            dest[i, :rows, :] = (keep[j].astype(F32) + got[j].astype(F32)).astype(dest.dtype)
            dest[i, rows:, :] = (left[...] + right[...]).astype(BF16).astype(dest.dtype)


def halve_kernel(exact, meta, keep, got, own, send):
    mine = keep[0] + got[0].astype(F32)
    own[:exact, :] = mine[:exact]
    own[exact:, :] = mine[exact:].astype(BF16).astype(F32)
    send[...] = (keep[1] + got[1].astype(F32)).astype(BF16)


def add_kernel(meta, own, got, out):
    out[...] = (own[...] + got[...].astype(F32)).astype(BF16)


def late_sums_of(meta, keep, got, left, right):
    _, rows, cols = keep.shape
    full = rows + left.shape[0]
    sds = jax.ShapeDtypeStruct
    kept, send = single(
        merge_halves_kernel, "merge_late", 1.0, [sds((2, full, cols), F32), sds((2, full, cols), BF16)],
        meta, [keep, got, left, right],
    )
    halves = single(
        partial(halve_kernel, rows), "halve", 1.0, [sds((full, cols), F32), sds((full, cols), BF16)],
        meta, [kept, swap(send, "seq", 2)],
    )
    return kept, halves


def spread_late(meta, halves):
    own, send = halves
    (total,) = single(
        add_kernel, "total_late", 1.0, [jax.ShapeDtypeStruct(own.shape, BF16)], meta,
        [own, swap(send, "seq", 4)],
    )
    return [total] + [swap(total, "rows", j) for j in (1, 2, 3)]


def small_kernel(meta, *refs):
    pieces, out = refs[:4], refs[4]
    lanes = pieces[0].shape[1] - 128
    a, b, c, d = (ref[:, lanes:].astype(F32) for ref in pieces)
    out[...] = ((a + b) + (c + d))[: out.shape[0]]


def copy_kernel(meta, *refs):
    half = len(refs) // 2
    for source, dest in zip(refs[:half], refs[half:]):
        dest[...] = source[...]


def stack_kernel(meta, *refs):
    for k, ref in enumerate(refs[:-1]):
        refs[-1][k] = ref[...]


def unpack_kernel(taps_n, fwidth, feats, first_late, meta, small, other, *refs):
    late_pieces, outs, packed, late = refs[:4], refs[4:-2], refs[-2], refs[-1]
    chips, size = small.shape[:2]
    core = meta[1]
    for k in range(chips):
        z = meta[2] ^ k
        packed[pl.ds(pl.multiple_of((2 * z + core) * size, 8), size), :] = small[k]
        packed[pl.ds(pl.multiple_of((2 * z + 1 - core) * size, 8), size), :] = other[k]
    (gain1, shift1, in_bias, short_weight, short_bias, f1, f1b, f2, f2b, f3, f3b, flast, freq,
     fbias, obias, gain2, shift2, ubias, dbias) = outs
    width = gain1.shape[0]
    take = pl.ds(first_late, late_pieces[0].shape[0] - first_late)
    a, b, c, d = (ref[take, :].astype(F32) for ref in late_pieces)
    late[...] = (a + b) + (c + d)
    place = 0
    for t in range(width // 128):
        flast[:, t * 128 : (t + 1) * 128] = packed[place : place + fwidth, :]
        place += fwidth
    f3[...] = packed[place : place + fwidth, :fwidth]
    f2[...] = packed[place : place + fwidth, fwidth:]
    place += fwidth
    f1[...] = packed[place : place + feats, :fwidth]
    for i, ref in enumerate((f1b, f2b, f3b, freq)):
        ref[...] = packed[place + i : place + i + 1, fwidth:].reshape(-1)

    def line(first, count):
        return jnp.concatenate(
            [packed[OTHER_ROWS + first + t : OTHER_ROWS + first + t + 1, :] for t in range(count)], axis=1
        ).reshape(-1)

    for i, ref in enumerate((dbias, gain2, shift2, obias, fbias)):
        ref[...] = line(6 * i, 6)
    ubias[...] = line(30, ubias.shape[0] // 128)
    side = late.shape[1] // 3

    def row(r):
        return [
            late[k // 3 : k // 3 + 1, k % 3 * side : (k % 3 + 1) * side] for k in (2 * r, 2 * r + 1)
        ]

    def wide(first):
        return jnp.concatenate(row(first) + row(first + 1) + row(first + 2), axis=1)

    in_bias[...] = wide(0).reshape(-1)
    for k in range(taps_n):
        short_weight[k : k + 1, :] = wide(3 + 3 * k)
    short_bias[...] = wide(3 + 3 * taps_n).reshape(-1)
    count = 6 + 3 * taps_n
    gain1[...] = jnp.concatenate(row(count), axis=1).reshape(-1)
    shift1[...] = jnp.concatenate(row(count + 1), axis=1).reshape(-1)


def place_early_kernel(meta, *refs):
    pieces, (down, out, up) = refs[:4], refs[4:]
    row = meta[3]
    share, width = out.shape
    part = share // 2
    for j, piece in enumerate(pieces):
        x, y = (row ^ j) % 2, (row ^ j) // 2
        down[pl.ds(pl.multiple_of((2 * x + y) * share, 8), share), :] = piece[:share, :width].astype(F32)
        tiles = (
            piece[:part, width : width + 128],
            piece[part:share, width : width + 128],
            piece[:part, width + 128 : width + 256],
        )
        for t, tile in enumerate(tiles):
            cols = pl.ds(pl.multiple_of(x * (width // 2) + t * 128, 128), 128)
            out[pl.ds(pl.multiple_of(y * part, 8), part), cols] = tile.astype(F32)
        cols = pl.ds(pl.multiple_of((2 * y + x) * width, 128), width)
        up[:, cols] = piece[:share, width + 256 : 2 * width + 256].astype(F32)


def place_in_kernel(meta, *refs):
    pieces, full = refs[:4], refs[4]
    part, cols = full.shape[0] // 2, pieces[0].shape[1]
    for j, piece in enumerate(pieces):
        x, y = (meta[3] ^ j) % 2, (meta[3] ^ j) // 2
        full[pl.ds(pl.multiple_of(y * part, 8), part), pl.ds(pl.multiple_of(x * cols, 128), cols)] = (
            piece[:part, :].astype(F32)
        )


def local(
    tokens, doc_starts, norm1_gain, norm1_bias, in_weight, in_bias, short_weight, short_bias,
    filter_first, filter_first_bias, filter_second, filter_second_bias, filter_third,
    filter_third_bias, filter_last, sine_freq, filter_bias, out_weight, out_bias, norm2_gain,
    norm2_bias, up_weight, up_bias, down_weight, down_bias, cotangent,
):
    block, width = tokens.shape[1:]
    blocks = lax.axis_size("seq")
    chips = blocks // 2
    nrows = lax.axis_size("rows")
    length = block * blocks
    hidden = up_weight.shape[1]
    index = lax.axis_index("seq")
    row = lax.axis_index("rows")
    starts = doc_starts[0]
    ndocs = starts.shape[0]
    taps_n = short_weight.shape[0]
    ff = width
    fsteps = hidden // ff
    share = width // blocks
    fits = blocks == 8 and nrows == 4 and fsteps == chips and share % 32 == 0 and block == 128
    packed = chips if fits and width == 768 else 0
    meta = jnp.concatenate(
        [jnp.stack([index, index % 2, index // 2, row]).astype(jnp.int32), starts]
    )
    tables = {k: jnp.asarray(v) for k, v in block_tables(block).items()}
    chunk = width if blocks <= 8 else 128
    steps = width // chunk
    tok, cot = tokens[0], cotangent[0]
    mat = whole((block, width))
    vec = whole((width,))
    sds = jax.ShapeDtypeStruct

    rim = shift(tok[block - RIM :], "seq", 1)
    proj, early, mixed, carried = single(
        partial(front_kernel, ndocs, packed), "front", 3.0,
        [sds((block + RIM, 3 * width), F32), sds((2 * width if packed else width, block), BF16),
         sds((block, 3 * width), F32), sds((block, width), BF16)],
        meta,
        [tok, rim, cot, norm1_gain, norm1_bias, in_weight, in_bias, short_weight, short_bias],
        scratch=[pltpu.VMEM((width, block), BF16)], limit=58 * 1024 * 1024,
    )

    early_got = swap(early, "rows", 1) if packed else None

    by_chunk = lambda lead: pl.BlockSpec(lead + (chunk,), lambda i: (0,) * len(lead) + (i,))
    fwidth, feats = sine_freq.shape[0], filter_first.shape[0]
    if packed:
        table = jnp.asarray(feature_table(length, (feats - 1) // 2))
        lags, window, *net = single(
            filter_kernel, "filter", 8.0,
            [sds((blocks, 2 * block, width), F32), sds((length, width), F32)]
            + [sds((3 * fwidth, length), F32)] * 3,
            meta,
            [table, filter_first, filter_first_bias, filter_second, filter_second_bias, filter_third,
             filter_third_bias, filter_last, sine_freq, tables["left3"]],
            after=[carried], scratch=[pltpu.VMEM((length, fwidth), F32)],
        )
    else:
        filter_params = tuple(
            v.astype(F32)
            for v in (filter_first, filter_first_bias, filter_second, filter_second_bias, filter_third,
                      filter_third_bias, filter_last, sine_freq)
        )
        taps, taps_pull = jax.vjp(partial(filter_taps, length=length), *filter_params)
        lags = pl.pallas_call(
            lag_kernel,
            grid=(steps,),
            out_shape=sds((blocks, 2 * block, width), F32),
            in_specs=[by_chunk((blocks, block)), whole(tables["left3"].shape)],
            out_specs=by_chunk((blocks, 2 * block)),
            compiler_params=params(),
            name="lags",
        )(taps.reshape(blocks, block, width), tables["left3"])

    if packed:
        near = near_blocks(carried, blocks)
        span = (width // 2, 2 * width)
        early_sib = swap(
            collected(
                meta, [(early, span), (early_got, span)] + [(v, None) for v in near], [lags]
            ), "seq", 1,
        )
        signal, signal_row = near + [early_sib], 3 * width
        nparts = len(signal)
        part_specs = [whole(v.shape) for v in signal]
        held = [pltpu.VMEM((blocks, block, chunk), BF16)]
    else:
        signal, signal_row = [lax.all_gather(carried, "seq", axis=0, tiled=False)], 0
        nparts, part_specs, held = 1, [by_chunk((blocks, block))], []
    spec_scratch = pltpu.VMEM((2 * block, chunk), F32)
    conv = pl.pallas_call(
        partial(conv_kernel, ndocs, nparts, signal_row),
        grid=(steps,),
        out_shape=sds((block, width), F32),
        in_specs=[smem()] + part_specs + [by_chunk((blocks, 2 * block)),
                  whole(tables["left2"].shape), whole(tables["inv3"].shape)],
        out_specs=by_chunk((block,)),
        scratch_shapes=[spec_scratch] + held,
        compiler_params=params(),
        cost_estimate=cost(3.0),
        name="conv",
    )(meta, *signal, lags, tables["left2"], tables["inv3"])

    if packed:
        left1, right1, left2, right2 = chips * 3 * share, width // 2, width // 2, hidden // 2
        row_counts = (
            left1 + left2, left1 + right1 + left2 + right2, 2 * left1 + right1, 2 * left2 + right2
        )
        extra = tuple(sds((n, block), BF16) for n in row_counts)
        extra_specs = tuple(whole((n, block)) for n in row_counts)
    else:
        extra = (sds((hidden, block), BF16), sds((block, hidden), BF16), sds((width, block), BF16),
                 sds((width, block), BF16), sds((block, width), BF16))
        extra_specs = (pl.BlockSpec((ff, block), lambda i: (i, 0)),
                       pl.BlockSpec((block, ff), lambda i: (0, i)),
                       whole((width, block)), whole((width, block)), mat)
    lanes = hidden // 3
    output, gresid, glong, glong16, ggate, smalls_mlp, *acts = pl.pallas_call(
        partial(mlp_kernel, packed),
        grid=(fsteps,),
        out_shape=(
            sds((block, width), BF16), sds((block, width), F32),
            sds((block, width), F32), sds((block, width), BF16), sds((block, width), F32),
            sds((8, lanes), F32),
        ) + extra,
        in_specs=[
            smem(), mat, mat, mat, mat, mat, vec, whole((width, width)), vec, vec, vec,
            pl.BlockSpec((width, ff), lambda i: (0, i)), whole((hidden,)),
            pl.BlockSpec((ff, width), lambda i: (i, 0)), vec,
        ],
        out_specs=(mat, mat, mat, mat, mat, whole((8, lanes))) + extra_specs,
        scratch_shapes=[
            pltpu.VMEM((block, width), F32), pltpu.VMEM((block, width), BF16),
            pltpu.VMEM((block, width), F32), pltpu.VMEM((block, 1), F32),
            pltpu.VMEM((block, width), F32), pltpu.VMEM((block, width), F32),
            pltpu.VMEM((1, hidden), F32), pltpu.VMEM((1, hidden), F32),
            pltpu.VMEM((width, block), BF16), pltpu.VMEM((block, width), BF16),
        ],
        compiler_params=params(),
        cost_estimate=cost(10.0),
        name="mlp",
    )(meta, tok, cot, conv, carried, mixed, filter_bias, out_weight, out_bias, norm2_gain,
      norm2_bias, up_weight, up_bias, down_weight, down_bias)

    if packed:
        own, shared, e1_send, e2_send = acts
        got1, got2 = swap(e1_send, "rows", 1), swap(e2_send, "rows", 2)
        near = near_blocks(glong16, blocks)
        shared_sib = swap(shared, "seq", 1)
        near_all = collected(meta, [(v, None) for v in near])
        grads, grads_row = near + [swap(near_all, "seq", 1)], 0
        got_sib = swap(
            collected(
                meta, [(got1, (left1, 2 * left1 + right1)), (got2, (left2, 2 * left2 + right2))],
                [near_all],
            ), "seq", 1,
        )
        grad_specs = [whole(v.shape) for v in grads]
    else:
        grads, grads_row = [lax.all_gather(glong16, "seq", axis=0, tiled=False)], 0
        grad_specs = part_specs

    tied = ()
    third = lambda n: pl.BlockSpec((block, chunk), lambda i: (0, n * steps + i))
    tap_third = lambda n: pl.BlockSpec((taps_n, chunk), lambda i: (0, n * steps + i))
    for_in, for_values, rim_out = pl.pallas_call(
        lambda *refs: conv_back_kernel(
            ndocs, length, nparts, grads_row, *refs[: nparts + 12], *refs[nparts + 12 + len(tied) :]
        ),
        grid=(steps,),
        out_shape=(sds((block, width), F32), sds((block, width), F32), sds((3, 8, width), F32)),
        in_specs=[smem()] + grad_specs + [
            by_chunk((block,)), by_chunk((blocks, 2 * block)), whole(tables["invt2"].shape),
            whole(tables["leftt3"].shape), vec if steps == 1 else by_chunk((1,)), third(1), third(2),
            by_chunk((block,)), tap_third(0), tap_third(1), tap_third(2)]
        + [pl.BlockSpec(memory_space=pl.ANY)] * len(tied),
        out_specs=(by_chunk((block,)), by_chunk((block,)), by_chunk((3, 8))),
        scratch_shapes=[spec_scratch] + held,
        compiler_params=params(),
        cost_estimate=cost(4.0),
        name="conv_back",
    )(meta, *grads, glong, lags, tables["invt2"], tables["leftt3"],
      filter_bias if steps == 1 else filter_bias.reshape(1, -1),
      mixed, mixed, ggate, short_weight, short_weight, short_weight, *tied)
    rim_back = shift(rim_out, "seq", -1)
    if packed:
        def partials(kernel, name, piece, arrays, after=()):
            return single(
                partial(kernel, chips), name, 3.0, [sds((chips,) + piece, BF16)] * 2, meta, arrays, after
            )

        parts2 = partials(up_kernel, "up_grad", (share, width), (own, shared, shared_sib, got2, got_sib), [rim_out])
        parts1 = partials(
            down_out_kernel, "down_out", (share, width + 256),
            (own, shared, shared_sib, got1, got_sib, early, early_got, early_sib), [rim_out],
        )
        tied = (parts1[0], parts2[0])
        keep1, send1 = parts1
        keep2, send2 = parts2
    tied = tied if packed else ()
    gproj, smalls_short, *late = single(
        partial(short_back_kernel, ndocs, packed), "short_back", 3.0,
        [sds((block, 3 * width), BF16), sds((24, width), F32)]
        + ([sds((3 * width // 2, block), BF16)] * 2 if packed else []),
        meta, [ggate, for_in, for_values, rim_back, proj, short_weight], tied,
    )
    if packed:
        late, late_send = late
        late_got = swap(late_send, "rows", 1)
        tied = (late_got,)
    else:
        tied = ()
    taps_grad = pl.pallas_call(
        lambda *refs: taps_grad_kernel(
            ndocs, nparts, signal_row, *refs[: nparts + 5], *refs[nparts + 5 + len(tied) :]
        ),
        grid=(steps,),
        out_shape=sds((blocks, block, width), F32),
        in_specs=[smem()] + part_specs + [
            by_chunk((block,)), whole(tables["left2"].shape), whole(tables["invt2"].shape),
            whole(tables["leftt3"].shape)]
        + [pl.BlockSpec(memory_space=pl.ANY)] * len(tied),
        out_specs=by_chunk((blocks, block)),
        scratch_shapes=[pltpu.VMEM((blocks + 1, 2 * block, chunk), F32), spec_scratch] + held,
        compiler_params=params(),
        cost_estimate=cost(4.0),
        name="taps_grad",
    )(meta, *signal, glong, tables["left2"], tables["invt2"], tables["leftt3"], *tied)
    if packed:
        half_rows, small_cols = chips * SMALL_BLOCK, 128
        mine, send = single(
            filter_back_kernel, "filter_back", 5.0, [sds((half_rows, small_cols), F32)] * 2, meta,
            [taps_grad, window, *net, table, filter_first, filter_second, filter_third, filter_last,
             sine_freq, smalls_mlp],
            after=[near_all], scratch=[pltpu.VMEM((2 * half_rows, small_cols), F32)],
        )
        pairs = [keep1, swap(send1, "rows", 2), keep2, swap(send2, "rows", 1)]
        first_sums = chip_sums(meta, pairs, "tiles", (mine, swap(send, "seq", 1)))
    else:
        filter_grads = taps_pull(taps_grad.reshape(length, width))

    late_shape = (16, 3 * width // 2) if packed else (24, width)
    grad_tokens, smalls_late = single(
        tail_kernel, "tail", 2.5, [sds((block, width), F32), sds(late_shape, F32)],
        meta, [gproj, in_weight, tok, norm1_gain, gresid, smalls_short],
    )

    if packed:
        def placed(kernel, name, shapes, pieces):
            return single(kernel, name, 1.5, [sds(v, F32) for v in shapes], meta, pieces)

        late_sib = swap(
            collected(
                meta, [(late, (0, late.shape[0])), (late_got, (0, late.shape[0]))]
            ), "seq", 1
        )
        keep3, send3 = partials(
            in_kernel, "in_grad", (share // 2, 3 * width // 2),
            (late, late_got, late_sib, early, early_got, early_sib), first_sums[:1],
        )
        kept3, halves3 = late_sums_of(
            meta, keep3, swap(send3, "rows", 2), smalls_late, swap(smalls_late, "seq", 1)
        )
        pieces = spread_out(meta, first_sums, [kept3])
        pieces3 = spread_late(meta, halves3)
        grad_down, grad_out, grad_up = placed(
            place_early_kernel, "place_early",
            ((hidden // blocks, width), (share, width), (share, hidden)), pieces,
        )
        (grad_in,) = placed(place_in_kernel, "place_in", ((share, 3 * width),), pieces3)

        (small,) = single(
            small_kernel, "small", 0.5, [sds((SMALL_BLOCK, 128), F32)], meta, pieces
        )
        near = [small] + [swap(small, "seq", 2 * k) for k in (1, 2, 3)]
        (small,) = single(
            stack_kernel, "stack", 0.5, [sds((chips, SMALL_BLOCK, 128), F32)], meta, near, [grad_up]
        )
        other = swap(small, "seq", 1)
        shapes = [
            (width,), (width,), (3 * width,), (taps_n, 3 * width), (3 * width,), (feats, fwidth),
            (fwidth,), (fwidth, fwidth), (fwidth,), (fwidth, fwidth), (fwidth,), (fwidth, width),
            (fwidth,), (width,), (width,), (width,), (width,), (hidden,), (width,),
        ]
        smalls = single(
            partial(unpack_kernel, taps_n, fwidth, feats, share // 2), "unpack", 1.5,
            [sds(v, F32) for v in shapes], meta, [small, other, *pieces3],
            scratch=[pltpu.VMEM((2 * half_rows, small_cols), F32), pltpu.VMEM(late_shape, F32)],
        )
    else:
        def summed(left, right):
            part = lax.psum_scatter(dot(left, right), "seq", scatter_dimension=0, tiled=True)
            return lax.psum(part, "rows")

        actt, gpre, n2t, gatedt, gmix = acts
        grad_in = summed(early, gproj)
        grad_out = summed(gatedt, gmix)
        grad_up = summed(n2t, gpre)
        grad_down = summed(actt, cot)
        small, late_sum, *fg = lax.psum((smalls_mlp, smalls_late, *filter_grads), ("rows", "seq"))
        wide = lambda first: late_sum[first : first + 3].reshape(-1)
        smalls = [
            late_sum[22], late_sum[23], wide(0), late_sum[3 : 3 + 3 * taps_n].reshape(taps_n, -1),
            wide(3 + 3 * taps_n), *fg, small[4, :width], small[3, :width], small[1, :width],
            small[2, :width], small[5:8].reshape(-1), small[0, :width],
        ]
    (grad_gain1, grad_shift1, grad_in_bias, grad_short_weight, grad_short_bias, f1, f1b, f2, f2b, f3,
     f3b, flast, freq, grad_filter_bias, grad_out_bias, grad_gain2, grad_shift2, grad_up_bias,
     grad_down_bias) = smalls
    return (
        output[None], grad_tokens[None], grad_gain1, grad_shift1, grad_in, grad_in_bias,
        grad_short_weight, grad_short_bias, f1, f1b, f2, f2b, f3, f3b, flast, freq,
        grad_filter_bias, grad_out, grad_out_bias, grad_gain2, grad_shift2, grad_up, grad_up_bias,
        grad_down, grad_down_bias,
    )


def solution(mesh):
    sharded = P("rows", "seq", None)
    placed = (sharded, P("rows", None)) + (P(),) * 23 + (sharded,)
    outs = [P()] * 25
    outs[0] = outs[1] = sharded
    for i in (4, 17, 21, 23):
        outs[i] = P("seq", None)
    return jax.shard_map(local, mesh=mesh, in_specs=placed, out_specs=tuple(outs), check_vma=False)
```
